32 devices in a mesh: dp: 8 (over y, x, core), tensor: 4 (over z).
Axes of the slice: x: 2, y: 2, z: 4, core: 2. Of those that a mesh axis runs over, the one named last changes fastest.
Arguments:
- tokens: bfloat16 [16384, 768], P(('dp', 'tensor')), may hold values from -6 to 6
- segments: int32 [16384], P('dp'), may hold values from 0 to 127, never falling along the last dimension, each value on 1 to 2048 neighbouring positions
- cotangent: bfloat16 [16384, 768], P(('dp', 'tensor')), may hold values from -6 to 6
- norm_gain: bfloat16 [768], replicated, may hold values from 0.099609375 to 1.8984375
- w_gate: bfloat16 [768, 1536], P('dp', 'tensor'), may hold values from -0.21875 to 0.21875
- w_inner: bfloat16 [768, 1536], P('dp', 'tensor'), may hold values from -0.21875 to 0.21875
- w_step: bfloat16 [768, 24], P('dp', 'tensor'), may hold values from -0.21875 to 0.21875
- w_state: bfloat16 [768, 256], P('dp'), may hold values from -0.21875 to 0.21875
- conv_inner: bfloat16 [5, 1536], P(None, 'tensor'), may hold values from -0.5 to 0.5
- conv_state: bfloat16 [5, 256], replicated, may hold values from -0.5 to 0.5
- step_bias: bfloat16 [24], P('tensor'), may hold values from -7 to -2.5
- decay_log: bfloat16 [24], P('tensor'), may hold values from -2.296875 to 2.6875
- skip_gain: bfloat16 [24], P('tensor'), may hold values from 0 to 2
- out_gain: bfloat16 [1536], P('tensor'), may hold values from 0.099609375 to 1.8984375
- w_out: bfloat16 [768, 1536], P('dp', 'tensor'), may hold values from -0.15625 to 0.15625
Outputs:
- mixed: bfloat16 [16384, 768], P(('dp', 'tensor'))
- grad_tokens: float32 [16384, 768], P(('dp', 'tensor'))
- grad_norm_gain: float32 [768], replicated
- grad_w_gate: float32 [768, 1536], P('dp', 'tensor')
- grad_w_inner: float32 [768, 1536], P('dp', 'tensor')
- grad_w_step: float32 [768, 24], P('dp', 'tensor')
- grad_w_state: float32 [768, 256], P('dp')
- grad_conv_inner: float32 [5, 1536], P(None, 'tensor')
- grad_conv_state: float32 [5, 256], replicated
- grad_step_bias: float32 [24], P('tensor')
- grad_decay_log: float32 [24], P('tensor')
- grad_skip_gain: float32 [24], P('tensor')
- grad_out_gain: float32 [1536], P('tensor')
- grad_w_out: float32 [768, 1536], P('dp', 'tensor')
The draws below stay inside these ranges and needn't reach their ends.
Inputs may be any that keep to these rules, and one draw needn't show every extreme that they name: `segments`: segment numbers never fall along the tokens; each document holds 1 to 2048 tokens and one holds exactly 2048; a document may run past the end of a sequence, where it is cut.
All inputs are finite; a program needn't handle non-finite values.
Results may differ from the reference program's by a relative error of at most 0.02.
Values may be sent and summed in bfloat16 or wider, within the bound.
No kernel may reach another device: no remote copies, remote signals or barrier semaphores. Data moves between devices by JAX's collectives and lax.ppermute only.
A program may use at most 128 MiB of HBM per device.

```python
import math
import jax
import jax.numpy as jnp
import numpy as np
from jax import lax

D = 768
HEADS = 24
HEAD_DIM = 64
STATE = 128
INNER = 1536
KW = 4
BLOCK = 256
LENGTH = 2048
TOKENS = 16384


def levels(key, shape, shards, low, high):
    level, own = 1.0, jax.random.fold_in(key, 6)
    for dim, parts in shards:
        heights = jnp.exp(jax.random.uniform(jax.random.fold_in(own, dim), (parts,), jnp.float32, low / len(shards), high / len(shards)))
        level = level * jnp.repeat(heights, shape[dim] // parts).reshape([-1 if axis == dim else 1 for axis in range(len(shape))])
    return level


def profile(number_of, total, bound, slope):
    portions = [(1 << 20) // math.isqrt(grade ** slope) + 1 for grade in range(2, number_of + 1)]
    surplus, given = total - bound - (number_of - 1), [1] * (number_of - 1)
    while surplus > 0:
        free = [i for i in range(number_of - 1) if given[i] < bound]
        pool, left = sum([portions[i] for i in free]), surplus
        for i in free:
            more = min(bound - given[i], max(1, left * portions[i] // pool), surplus)
            given[i] = given[i] + more
            surplus = surplus - more
    return np.array([bound] + given)


def uneven(rng, count, total, limit, lean):
    if count == 2:
        one = jax.random.randint(rng, (), max(1, total - limit), min(limit, total - 1) + 1)
        return jnp.stack([one, total - one])
    sizes = jnp.asarray(profile(count, total, limit, lean), jnp.int32)
    twos = (count - 1) // 2
    giver, sink = sizes[1:1 + 2 * twos:2], sizes[2:2 + 2 * twos:2]
    room = jnp.minimum(giver - 1, limit - sink)
    moved = jax.random.randint(jax.random.fold_in(rng, 1), (twos,), 0, 1 << 20) % (room + 1)
    sizes = sizes.at[1:1 + 2 * twos:2].set(giver - moved).at[2:2 + 2 * twos:2].set(sink + moved)
    return sizes[jax.random.permutation(jax.random.fold_in(rng, 2), count)]


def bell_draw(rng, extent, spread, bound, cuts=(), kind=jnp.bfloat16):
    values = spread * jax.random.normal(rng, extent, jnp.float32)
    if cuts:
        values = values * levels(rng, extent, cuts, -0.22, 0.18)
    return jnp.clip(values, -bound, bound).astype(kind)


def setup_inputs(seed: int = 0) -> dict:
    key_list = jax.random.split(jax.random.key(seed), 16)
    return {
        "tokens": bell_draw(key_list[0], (TOKENS, D), 1.0, 6.0, ((0, 32),)),
        "segments": jnp.searchsorted(jnp.cumsum(uneven(key_list[1], TOKENS // min(LENGTH // 2, 128), TOKENS, LENGTH, 2)), jnp.arange(TOKENS), side="right").astype(jnp.int32),
        "cotangent": bell_draw(key_list[2], (TOKENS, D), 1.0, 6.0, ((0, 32),)),
        "norm_gain": jnp.clip(1.0 + 0.18 * jax.random.normal(key_list[3], (D,), jnp.float32), 0.099609375, 1.8984375).astype(jnp.bfloat16),
        "w_gate": bell_draw(key_list[4], (D, INNER), D ** -0.5, 0.21875, ((0, 8), (1, 4))),
        "w_inner": bell_draw(key_list[5], (D, INNER), D ** -0.5, 0.21875, ((0, 8), (1, 4))),
        "w_step": bell_draw(key_list[6], (D, HEADS), D ** -0.5, 0.21875, ((0, 8), (1, 4))),
        "w_state": bell_draw(key_list[7], (D, 2 * STATE), D ** -0.5, 0.21875, ((0, 8),)),
        "conv_inner": jnp.clip(jax.random.uniform(key_list[8], (KW + 1, INNER), jnp.float32, -0.5, 0.5) * levels(key_list[8], (KW + 1, INNER), ((1, 4),), -0.4, 0.0), -0.5, 0.5).astype(jnp.bfloat16),
        "conv_state": jnp.clip(jax.random.uniform(key_list[9], (KW + 1, 2 * STATE), jnp.float32, -0.5, 0.5), -0.5, 0.5).astype(jnp.bfloat16),
        "step_bias": jnp.clip(-7.0 + 4.5 * jax.random.uniform(key_list[10], (HEADS,), jnp.float32) ** levels(key_list[10], (HEADS,), ((0, 4),), -0.2, 0.2), -7.0, -2.5).astype(jnp.bfloat16),
        "decay_log": jnp.clip(-2.296875 + 4.984375 * jax.random.uniform(key_list[11], (HEADS,), jnp.float32) ** levels(key_list[11], (HEADS,), ((0, 4),), -0.2, 0.2), -2.296875, 2.6875).astype(jnp.bfloat16),
        "skip_gain": jnp.clip(2.0 * jax.random.uniform(key_list[12], (HEADS,), jnp.float32) ** levels(key_list[12], (HEADS,), ((0, 4),), -0.2, 0.2), 0.0, 2.0).astype(jnp.bfloat16),
        "out_gain": jnp.clip(1.0 + 0.18 * jax.random.normal(key_list[13], (INNER,), jnp.float32), 0.099609375, 1.8984375).astype(jnp.bfloat16),
        "w_out": bell_draw(key_list[14], (D, INNER), INNER ** -0.5, 0.15625, ((0, 8), (1, 4))),
    }


@jax.custom_vjp
def low(v):
    return lax.optimization_barrier(v.astype(jnp.bfloat16)).astype(jnp.float32)

@jax.custom_vjp
def low_back(v):
    return v

def low_keep(v):
    return (low(v), None)

def low_pass(kept, grad):
    return (grad,)

def back_keep(v):
    return (v, None)

def back_low(kept, grad):
    return (low(grad),)
low.defvjp(low_keep, low_pass)
low_back.defvjp(back_keep, back_low)
eps = 1e-05
highest = lax.Precision.HIGHEST

def silu_act(values):
    return values * jax.nn.sigmoid(values)

def doc_numbers(seg_row):
    starts = jnp.concatenate([jnp.ones((1,), jnp.int32), (seg_row[1:] != seg_row[:-1]).astype(jnp.int32)])
    return jnp.cumsum(starts).astype(jnp.int32)

def conv_masks(doc_ids):
    mask_list = [jnp.ones(doc_ids.shape, jnp.float32)]
    for offset in range(1, KW):
        earlier = jnp.concatenate([jnp.full((offset,), -1, jnp.int32), doc_ids[:-offset]])
        mask_list.append((earlier == doc_ids).astype(jnp.float32))
    return mask_list

def shifted(values, offset):
    return jnp.concatenate([jnp.zeros((offset,) + values.shape[1:], values.dtype), values[:-offset]], 0)

def conv_apply(values, kernel, mask_list):
    result = kernel[KW] + kernel[0] * values
    for offset in range(1, KW):
        result = result + kernel[offset] * shifted(values, offset) * mask_list[offset][:, None]
    return result

def block_terms(step_block, decay_block, doc_block, prev_doc):
    length = doc_block.shape[0]
    cumulative = jnp.cumsum(decay_block, axis=0)
    places = jnp.arange(length)
    causal = ((places[:, None] >= places[None, :]) & (doc_block[:, None] == doc_block[None, :])).astype(jnp.float32)
    differ = cumulative[:, None, :] - cumulative[None, :, :]
    weight_in = jnp.exp(jnp.where(causal[:, :, None] > 0, differ, 0.0)) * causal[:, :, None] * step_block[None, :, :]
    from_prev = (doc_block == prev_doc).astype(jnp.float32)
    row_scale = jnp.exp(cumulative) * from_prev[:, None]
    at_last = (doc_block == doc_block[length - 1]).astype(jnp.float32)
    weight_out = jnp.exp(cumulative[length - 1][None, :] - cumulative) * at_last[:, None] * step_block
    keep_rate = jnp.exp(cumulative[length - 1]) * (doc_block[length - 1] == prev_doc).astype(jnp.float32)
    return (weight_in, row_scale, weight_out, keep_rate)

def state_space(inner_low, entry_low, readout_low, step_size, log_decay, doc_ids):
    block_count = inner_low.shape[0] // BLOCK
    head_count = step_size.shape[1]
    inner_blocks = inner_low.reshape(block_count, BLOCK, head_count, HEAD_DIM)
    entry_blocks = entry_low.reshape(block_count, BLOCK, STATE)
    read_blocks = readout_low.reshape(block_count, BLOCK, STATE)
    step_blocks = step_size.reshape(block_count, BLOCK, head_count)
    decay_blocks = log_decay.reshape(block_count, BLOCK, head_count)
    doc_blocks = doc_ids.reshape(block_count, BLOCK)
    prev_docs = jnp.concatenate([jnp.full((1,), -1, jnp.int32), doc_blocks[:-1, BLOCK - 1]])

    def one_block(carried, blocks):
        inner_block, entry_block, read_block, step_block, decay_block, doc_block, prev_doc = blocks
        weight_in, row_scale, weight_out, keep_rate = block_terms(step_block, decay_block, doc_block, prev_doc)
        score_mat = low_back(jnp.dot(read_block, entry_block.T, precision=highest))
        mix_low = low(score_mat[:, :, None] * weight_in)
        inner_part = jnp.einsum('ijh,jhp->ihp', mix_low, inner_block, precision=highest)
        raw_state = low_back(jnp.einsum('in,hpn->ihp', read_block, low(carried), precision=highest))
        state_part = raw_state * row_scale[:, :, None]
        scaled = low(inner_block * weight_out[:, :, None])
        contribution = low_back(jnp.einsum('jhp,jn->hpn', scaled, entry_block, precision=highest))
        return (carried * keep_rate[:, None, None] + contribution, low_back(inner_part + state_part))
    zero_state = jnp.zeros((head_count, HEAD_DIM, STATE), jnp.float32)
    _, outputs = lax.scan(one_block, zero_state, (inner_blocks, entry_blocks, read_blocks, step_blocks, decay_blocks, doc_blocks, prev_docs))
    return outputs.reshape(block_count * BLOCK, head_count, HEAD_DIM)

def gate_out(scan_out, inner_act, gate_pre, skip_gain):
    row_count = scan_out.shape[0]
    head_count = scan_out.shape[1]
    heads_sum = scan_out + inner_act.reshape(row_count, head_count, HEAD_DIM) * skip_gain[None, :, None]
    return heads_sum.reshape(row_count, head_count * HEAD_DIM) * silu_act(gate_pre)

def sequence_pass(tokens, seg_row, weights):
    norm_gain, w_gate, w_inner, w_step, w_state, conv_inner, conv_state, step_bias, decay_log, skip_gain, out_gain, w_out = weights
    doc_ids = doc_numbers(seg_row)
    mask_list = conv_masks(doc_ids)
    normed = low(tokens * lax.rsqrt(lax.optimization_barrier(jnp.mean(tokens * tokens, axis=1, keepdims=True)) + eps) * norm_gain)
    gate_pre = low_back(jnp.dot(normed, w_gate, precision=highest))
    inner_pre = low_back(jnp.dot(normed, w_inner, precision=highest))
    step_pre = low_back(jnp.dot(normed, w_step, precision=highest))
    state_pre = low_back(jnp.dot(normed, w_state, precision=highest))
    inner_act = silu_act(conv_apply(inner_pre, conv_inner, mask_list))
    state_act = silu_act(conv_apply(state_pre, conv_state, mask_list))
    step_size = jax.nn.softplus(step_pre + step_bias)
    log_decay = step_size * -jnp.exp(decay_log)
    state_low = low(state_act)
    scan_out = state_space(low(inner_act), state_low[:, :STATE], state_low[:, STATE:], step_size, log_decay, doc_ids)
    gated_out = gate_out(scan_out, inner_act, gate_pre, skip_gain)
    out_low = low(gated_out * lax.rsqrt(lax.optimization_barrier(jnp.mean(gated_out * gated_out, axis=1, keepdims=True)) + eps) * out_gain)
    return tokens + jnp.dot(out_low, w_out.T, precision=highest)

def reference(tokens, segments, cotangent, norm_gain, w_gate, w_inner, w_step, w_state, conv_inner, conv_state, step_bias, decay_log, skip_gain, out_gain, w_out):
    params = tuple((weight.astype(jnp.float32) for weight in (norm_gain, w_gate, w_inner, w_step, w_state, conv_inner, conv_state, step_bias, decay_log, skip_gain, out_gain, w_out)))
    seg_rows = segments.reshape(-1, LENGTH)
    token_rows = tokens.astype(jnp.float32)

    def forward(flat_tokens, *weights):

        def one_sequence(token_pair):
            return sequence_pass(token_pair[0], token_pair[1], weights)
        outputs = lax.map(jax.checkpoint(one_sequence), (flat_tokens.reshape(-1, LENGTH, D), seg_rows))
        return outputs.reshape(-1, D)
    result, pull_back = jax.vjp(forward, token_rows, *params)
    grads = pull_back(cotangent.astype(jnp.float32))
    return (result.astype(jnp.bfloat16), grads[0], grads[1], grads[2], grads[3], grads[4], grads[5], grads[6], grads[7], grads[8], grads[9], grads[10], grads[11], grads[12])
```

```python
import jax
import jax.numpy as jnp
from jax import lax
from jax.experimental import pallas as pl
from jax.experimental.pallas import tpu as pltpu
from jax.sharding import PartitionSpec as P

HEAD_DIM = 64
STATE = 128
KW = 4
BLOCK = 256
HALO = 16
LANES = 128
TILE = 256
ROWS = 128
EPS = 1e-05
F32 = jnp.float32
BF = jnp.bfloat16
HIGH = lax.Precision.HIGHEST
LIMIT = 56 * 2**20
ORDER = (0, 2, 4, 6, 1, 3, 5, 7)


def dot(a, b):
    return lax.dot_general(a, b, (((1,), (0,)), ((), ())), preferred_element_type=F32)


def dot_nt(a, b):
    return lax.dot_general(a, b, (((1,), (1,)), ((), ())), preferred_element_type=F32)


def dot_tn(a, b):
    return lax.dot_general(a, b, (((0,), (0,)), ((), ())), preferred_element_type=F32)


def dot_high(a, b):
    return lax.dot_general(
        a, b, (((1,), (0,)), ((), ())), precision=HIGH, preferred_element_type=F32
    )


def sigmoid(x):
    return 1.0 / (1.0 + jnp.exp(-x))


def expand(x, first, count):
    lane = lax.broadcasted_iota(jnp.int32, (x.shape[0], LANES), 1)
    return jnp.concatenate(
        [
            jnp.where(lane < HEAD_DIM, x[:, h : h + 1], x[:, h + 1 : h + 2])
            for h in range(first, first + count, 2)
        ],
        axis=1,
    )


def head_matrix(first, channels):
    channel = lax.broadcasted_iota(jnp.int32, (channels, LANES), 0)
    head = lax.broadcasted_iota(jnp.int32, (channels, LANES), 1)
    return (channel // HEAD_DIM + first == head).astype(BF)


def head_sum(x, matrix):
    hi = x.astype(BF)
    lo = (x - hi.astype(F32)).astype(BF)
    return dot(hi, matrix) + dot(lo, matrix)


def lower_matrix():
    i = lax.broadcasted_iota(jnp.int32, (BLOCK, BLOCK), 0)
    j = lax.broadcasted_iota(jnp.int32, (BLOCK, BLOCK), 1)
    return i, j


def conv_forward(values, taps, cols):
    result = taps[KW : KW + 1] + taps[0:1] * values[HALO:]
    for k in range(1, KW):
        result = result + taps[k : k + 1] * pltpu.roll(values, k, 0)[HALO:] * cols[:, k - 1 : k]
    return result


def conv_backward(grad, values, taps, cols):
    width = grad.shape[1]
    whole = HALO + grad.shape[0]
    zero = jnp.zeros((HALO, width), F32)
    base = jnp.concatenate([zero, grad], axis=0)
    result = taps[0:1] * base
    sums = [jnp.sum(grad * values[HALO:], axis=0, keepdims=True)]
    for k in range(1, KW):
        masked = jnp.concatenate([zero, grad * cols[:, k - 1 : k]], axis=0)
        back = pltpu.roll(masked, whole - k, 0)
        result = result + taps[k : k + 1] * back
        sums.append(jnp.sum(back * values, axis=0, keepdims=True))
    sums.append(jnp.sum(grad, axis=0, keepdims=True))
    return result, sums


def put_rows(rows, width):
    index = lax.broadcasted_iota(jnp.int32, (8, width), 0)
    result = jnp.zeros((8, width), F32)
    for i, row in enumerate(rows):
        result = jnp.where(index == i, row, result)
    return result


def call(kernel, outs, args, scratch=(), name=None, flops=0, far=(), far_outs=()):
    size = sum(a.size * a.dtype.itemsize for a in args)
    size += sum(o.size * o.dtype.itemsize for o in outs)

    def spec(space):
        return pl.BlockSpec(memory_space=space)

    ins = [
        spec(pltpu.SMEM if i == 0 else pl.ANY if i in far else pltpu.VMEM) for i in range(len(args))
    ]
    return pl.pallas_call(
        kernel,
        out_shape=outs,
        in_specs=ins,
        out_specs=[spec(pl.ANY if i in far_outs else pltpu.VMEM) for i in range(len(outs))],
        scratch_shapes=list(scratch),
        compiler_params=pltpu.CompilerParams(vmem_limit_bytes=LIMIT),
        cost_estimate=pl.CostEstimate(flops=flops, bytes_accessed=size, transcendentals=0),
        name=name,
    )(*args)


def sds(shape, dtype):
    return jax.ShapeDtypeStruct(shape, dtype)


def aligned(value, size):
    return pl.multiple_of(value * size, size)


def load_weights(place, refs, targets, sems):
    if len(refs[0].shape) == 2:
        copies = [pltpu.make_async_copy(r, t, sems.at[n]) for n, (r, t) in enumerate(zip(refs, targets))]
        for copy in copies:
            copy.start()
        return
    split = refs[0].shape[0] == 5
    depth, span = refs[0].shape[-2:]
    for n, k in enumerate(ORDER):
        row = pl.ds(aligned(place[0] ^ k, depth), depth)
        for m in range(4):
            column = pl.ds(aligned((place[1] + m) % 4, span), span)
            for g in range(1 if split else 2):
                source = refs[n].at[m] if split else refs[n].at[m, g]
                pltpu.make_async_copy(source, targets[g].at[row, column], sems.at[g]).start()
        if split:
            wide = targets[1].shape[1]
            pltpu.make_async_copy(refs[n].at[4, :, :wide], targets[1].at[row, :], sems.at[1]).start()
            pltpu.make_async_copy(refs[n].at[4, :, wide:], targets[2].at[row, :], sems.at[2]).start()


def wait_weights(targets, sems):
    for n, target in enumerate(targets):
        pltpu.make_async_copy(target, target, sems.at[n]).wait()


def store_grads(place, sources, outs, sems):
    if len(outs[0].shape) == 2:
        copies = [pltpu.make_async_copy(s, o, sems.at[n]) for n, (s, o) in enumerate(zip(sources, outs))]
        for copy in copies:
            copy.start()
    else:
        split = outs[0].shape[1] == 5
        depth, span = outs[0].shape[-2:]
        for n, k in enumerate(ORDER):
            out = outs[n // 4].at[n % 4]
            sem = sems.at[n // 4]
            row = pl.ds(aligned(place[0] ^ k, depth), depth)
            for m in range(4):
                column = pl.ds(aligned((place[1] + m) % 4, span), span)
                for g in range(1 if split else 2):
                    target = out.at[m] if split else out.at[m, g]
                    pltpu.make_async_copy(sources[g].at[row, column], target, sem).start()
            if split:
                wide = sources[1].shape[1]
                pltpu.make_async_copy(sources[1].at[row, :], out.at[4, :, :wide], sem).start()
                pltpu.make_async_copy(sources[2].at[row, :], out.at[4, :, wide:], sem).start()
    for n, out in enumerate(outs):
        pltpu.make_async_copy(out, out, sems.at[n]).wait()


def project_kernel(
    place, *refs
):
    (normed, taps, taps_state, par, cols), refs = refs[:5], refs[5:]
    weights, refs = refs[:-13], refs[-13:]
    pre, conv, spre, sconv, rw, st, keep, c_ref, pay, win, wst, wsp, sems = refs
    load_weights(place, weights, (win, wst, wsp), sems)
    wait_weights((win, wst, wsp), sems)
    project(normed, win, wst, wsp, taps, taps_state, par, cols, pre, conv, spre, sconv, rw, st, keep, c_ref, pay)


def project(
    normed, win, wst, wsp, taps, taps_state, par, cols, pre, conv, spre, sconv, rw, st, keep, c_ref, pay
):
    tokens = conv.shape[0]
    inner = conv.shape[1]
    blocks = tokens // BLOCK
    x = normed[...]
    low = x[HALO:]
    col = cols[...]
    sp = dot(low, wsp[...]) + par[0:1]
    step = jnp.maximum(sp, 0.0) + jnp.log1p(jnp.exp(-jnp.abs(sp)))
    decay = step * par[1:2]
    i, j = lower_matrix()
    lower = (i >= j).astype(F32)
    st[0] = sp
    st[1] = step
    keeps = []
    outs = []
    for b in range(blocks):
        rows = slice(b * BLOCK, (b + 1) * BLOCK)
        cum = dot_high(lower, decay[rows])
        last = cum[BLOCK - 1 : BLOCK]
        from_prev = col[rows, 3:4]
        out = jnp.exp(last - cum) * col[rows, 4:5]
        st[2, rows] = cum
        st[3, rows] = out
        st[4, rows] = jnp.exp(cum) * from_prev
        keeps.append(jnp.exp(last) * from_prev[BLOCK - 1 : BLOCK])
        outs.append(out * step[rows])
    keep[...] = put_rows(keeps, LANES)
    whole = keeps[0]
    for b in range(1, blocks):
        whole = whole * keeps[b]
    state = dot(x, wst[...])
    spre[...] = state
    sc = conv_forward(state, taps_state, col)
    sconv[...] = sc
    rw[...] = (sc * sigmoid(sc)).astype(BF)
    entry = rw[:, :STATE]
    index = lax.broadcasted_iota(jnp.int32, (HALO, TILE), 0)
    for tile in range(inner // TILE):
        lanes = slice(tile * TILE, (tile + 1) * TILE)
        heads = TILE // HEAD_DIM
        first = tile * heads
        value = dot(x, win[:, lanes])
        pre[:, lanes] = value.astype(BF)
        c = conv_forward(value, taps[:, lanes], col).astype(BF)
        conv[:, lanes] = c
        c = c.astype(F32)
        act = (c * sigmoid(c)).astype(BF).astype(F32)
        total = None
        for b in range(blocks):
            rows = slice(b * BLOCK, (b + 1) * BLOCK)
            scaled = (act[rows] * expand(outs[b], first, heads)).astype(BF)
            part = dot_tn(entry[rows], scaled)
            if b < blocks - 1:
                c_ref[b, :, lanes] = part
            total = part if b == 0 else total * expand(keeps[b], first, heads) + part
        pay[:STATE, lanes] = total.astype(BF)
        wide = expand(whole, first, heads)
        hi = wide.astype(BF).astype(F32)
        pay[STATE:, lanes] = jnp.where(index == 0, hi, jnp.where(index == 1, wide - hi, 0.0)).astype(BF)


def middle_kernel(place, normed, cot, conv, st, rw, seg_col, seg_row, *refs):
    weights, (gate, gout, y, smask, cum_t, wg, wo, sems) = refs[:-8], refs[-8:]
    load_weights(place, weights, (wg, wo), sems)
    tokens, inner = conv.shape
    blocks = tokens // BLOCK
    half = BLOCK // 2
    i, j = lower_matrix()
    lane = lax.broadcasted_iota(jnp.int32, (BLOCK, LANES), 1)
    for b in range(blocks):
        rows = slice(b * BLOCK, (b + 1) * BLOCK)
        scores = dot_nt(rw[rows, STATE:], rw[rows, :STATE])
        same = (i >= j) & (seg_col[rows, 0:1] == seg_row[0:1, rows])
        smask[...] = jnp.where(same, scores, 0.0)
        cum_t[...] = st[2, rows].T

        def pair(p, carry):
            cum = pltpu.roll(st[2, rows], LANES - 2 * p, 1)
            step = pltpu.roll(st[1, rows], LANES - 2 * p, 1)
            lanes = pl.ds(pl.multiple_of(p * LANES, LANES), LANES)
            c = conv[rows, lanes].astype(F32)
            act = (c * sigmoid(c)).astype(BF).astype(F32)
            xs = (act * jnp.where(lane < HEAD_DIM, step[:, 0:1], step[:, 1:2])).astype(BF)
            top = jnp.zeros((half, LANES), F32)
            bottom = jnp.zeros((half, LANES), F32)
            for a in range(2):
                mine = jnp.where((lane < HEAD_DIM) == (a == 0), xs, jnp.zeros_like(xs))
                row = cum_t[pl.ds(2 * p + a, 1), :]
                e = jnp.exp(jnp.minimum(cum[:half, a : a + 1] - row[:, :half], 0.0))
                top = top + dot((smask[:half, :half] * e).astype(BF), mine[:half])
                e = jnp.exp(jnp.minimum(cum[half:, a : a + 1] - row, 0.0))
                bottom = bottom + dot((smask[half:, :] * e).astype(BF), mine)
            y[b * BLOCK : b * BLOCK + half, lanes] = top
            y[b * BLOCK + half : (b + 1) * BLOCK, lanes] = bottom
            return carry

        lax.fori_loop(0, inner // LANES, pair, 0)
    wait_weights((wg, wo), sems)
    for tile in range(inner // TILE):
        lanes = slice(tile * TILE, (tile + 1) * TILE)
        gate[:, lanes] = dot(normed[HALO:, :], wg[:, lanes]).astype(BF)
        gout[:, lanes] = dot(cot[...], wo[:, lanes]).astype(BF)


def output_kernel(
    place, enter, c_ref, keep, gate, gout, y, conv, rw, st, wide, out_low, ggate, gscan, rowside, gread, states,
    d_ref, pay, sums, so_ref, d_all
):
    tokens, inner = conv.shape
    blocks = tokens // BLOCK
    tiles = inner // TILE
    heads = TILE // HEAD_DIM
    now = None
    for b in range(blocks):
        now = enter[...] if b == 0 else now * expand(keep[b - 1 : b], 0, inner // HEAD_DIM) + c_ref[b - 1]
        states[b] = now.astype(BF)
    sums[...] = jnp.zeros_like(sums)
    d_all[...] = jnp.zeros_like(d_all)

    def chunk(r, carry):
        rows = pl.ds(pl.multiple_of(r * ROWS, ROWS), ROWS)
        b = r // (BLOCK // ROWS)
        read = rw[rows, STATE:]
        scale = st[4, rows, :]
        total = jnp.zeros((ROWS, 1), F32)
        cross = jnp.zeros((ROWS, 1), F32)
        for tile in range(tiles):
            lanes = slice(tile * TILE, (tile + 1) * TILE)
            raw = dot(read, states[b, :, lanes])
            so = y[rows, lanes] + raw * expand(scale, tile * heads, heads)
            so_ref[:, lanes] = so
            c = conv[rows, lanes].astype(F32)
            u = so + wide[1:2, lanes] * (c * sigmoid(c))
            g = gate[rows, lanes].astype(F32)
            gated = u * (g * sigmoid(g))
            total = total + jnp.sum(gated * gated, axis=1, keepdims=True)
            go = gout[rows, lanes].astype(F32) * wide[0:1, lanes]
            cross = cross + jnp.sum(go * gated, axis=1, keepdims=True)
        rms = lax.rsqrt(total / inner + EPS)
        cube = rms * rms * rms * (cross / inner)
        side = jnp.zeros((ROWS, LANES), F32)
        read_grad = jnp.zeros((ROWS, STATE), F32)
        for tile in range(tiles):
            lanes = slice(tile * TILE, (tile + 1) * TILE)
            so = so_ref[:, lanes]
            c = conv[rows, lanes].astype(F32)
            act = c * sigmoid(c)
            u = so + wide[1:2, lanes] * act
            g = gate[rows, lanes].astype(F32)
            sg = sigmoid(g)
            silu = g * sg
            gated = u * silu
            gain = wide[0:1, lanes]
            out = gated * rms
            out_low[rows, lanes] = (out * gain).astype(BF)
            go = gout[rows, lanes].astype(F32)
            gg = go * gain * rms - gated * cube
            q = gg * silu
            ggate[rows, lanes] = (gg * u * (sg * (1.0 + g * (1.0 - sg)))).astype(BF)
            low = q.astype(BF)
            gscan[rows, lanes] = low
            low = low.astype(F32)
            sums[0:1, lanes] += jnp.sum(go * out, axis=0, keepdims=True)
            sums[1:2, lanes] += jnp.sum(q * act, axis=0, keepdims=True)
            side = side + head_sum(low * so, head_matrix(tile * heads, TILE))
            scaled = (low * expand(scale, tile * heads, heads)).astype(BF)
            d_all[b, :, lanes] += dot_tn(read, scaled)
            read_grad = read_grad + dot_nt(scaled, states[b, :, lanes])
        rowside[rows, :] = side
        gread[rows, :] = read_grad
        return carry

    lax.fori_loop(0, tokens // ROWS, chunk, 0)
    for b in range(1, blocks):
        d_ref[b - 1] = d_all[b]
    total = d_all[blocks - 1]
    whole = keep[blocks - 1 : blocks]
    for b in range(blocks - 2, -1, -1):
        total = d_all[b] + expand(keep[b : b + 1], 0, inner // HEAD_DIM) * total
        whole = whole * keep[b : b + 1]
    pay[:STATE] = total.astype(BF)
    index = lax.broadcasted_iota(jnp.int32, (HALO, inner), 0)
    wide_keep = expand(whole, 0, inner // HEAD_DIM)
    hi = wide_keep.astype(BF).astype(F32)
    pay[STATE:] = jnp.where(index == 0, hi, jnp.where(index == 1, wide_keep - hi, 0.0)).astype(BF)


def gate_grad_kernel(place, normed, cot, out_low, ggate, tok, *refs):
    (mixed, gn), refs = refs[-9:-7], refs[:-9] + refs[-7:]
    weights, (out_a, out_b, gwg, gwo, wg, wo, sems) = refs[:-7], refs[-7:]
    load_weights(place, weights, (wg, wo), sems)
    inner = out_low.shape[1]
    low = normed[HALO:, :]
    for tile in range(inner // TILE):
        lanes = slice(tile * TILE, (tile + 1) * TILE)
        gwo[:, lanes] = dot_tn(cot[...], out_low[:, lanes]).astype(BF)
        gwg[:, lanes] = dot_tn(low, ggate[:, lanes]).astype(BF)
    wait_weights((wg, wo), sems)
    gn[...] = dot_nt(ggate[...], wg[...])
    mixed[...] = (tok[HALO:, :].astype(F32) + dot_nt(out_low[...], wo[...])).astype(BF)
    store_grads(place, (gwg, gwo), (out_a, out_b), sems)


def scan_grad_kernel(place, gscan, conv, st, rw, seg_col, seg_row, z, colside, gentry, gread, smask, acc, cum_t):
    tokens, inner = conv.shape
    blocks = tokens // BLOCK
    half = BLOCK // 2
    j, i = lower_matrix()
    lane = lax.broadcasted_iota(jnp.int32, (BLOCK, LANES), 1)
    for b in range(blocks):
        rows = slice(b * BLOCK, (b + 1) * BLOCK)
        same = (i >= j) & (seg_col[rows, 0:1] == seg_row[0:1, rows])
        scores = dot_nt(rw[rows, :STATE], rw[rows, STATE:])
        smask[...] = jnp.where(same, scores, 0.0)
        cum_t[...] = st[2, rows].T
        acc[...] = jnp.zeros_like(acc)
        colside[rows, :] = jnp.zeros((BLOCK, LANES), F32)

        def pair(p, carry):
            cum = pltpu.roll(st[2, rows], LANES - 2 * p, 1)
            step = pltpu.roll(st[1, rows], LANES - 2 * p, 1)
            lanes = pl.ds(pl.multiple_of(p * LANES, LANES), LANES)
            c = conv[rows, lanes].astype(F32)
            act = (c * sigmoid(c)).astype(BF).astype(F32)
            xs = (act * jnp.where(lane < HEAD_DIM, step[:, 0:1], step[:, 1:2])).astype(BF)
            gs = gscan[rows, lanes]
            gs_t = gs.T
            top = jnp.zeros((half, LANES), F32)
            bottom = jnp.zeros((half, LANES), F32)
            for a in range(2):
                keep = (lane < HEAD_DIM) == (a == 0)
                mine = jnp.where(keep, xs, jnp.zeros_like(xs))
                grad = jnp.where(keep, gs, jnp.zeros_like(gs))
                row = cum_t[pl.ds(2 * p + a, 1), :]
                e = jnp.exp(jnp.minimum(row - cum[:half, a : a + 1], 0.0))
                top = top + dot((smask[:half, :] * e).astype(BF), grad)
                acc[:half, :] += dot(mine[:half], gs_t) * e
                e = jnp.exp(jnp.minimum(row[:, half:] - cum[half:, a : a + 1], 0.0))
                bottom = bottom + dot((smask[half:, half:] * e).astype(BF), grad[half:])
                acc[half:, half:] += dot(mine[half:], gs_t[:, half:]) * e
            both = jnp.concatenate([top, bottom], axis=0)
            z[rows, lanes] = both.astype(BF)
            channel = lax.broadcasted_iota(jnp.int32, (LANES, LANES), 0)
            head = lax.broadcasted_iota(jnp.int32, (LANES, LANES), 1)
            matrix = (channel // HEAD_DIM + 2 * p == head).astype(BF)
            colside[rows, :] += head_sum(both * xs.astype(F32), matrix)
            return carry

        lax.fori_loop(0, inner // LANES, pair, 0)
        low = jnp.where(same, acc[...], 0.0).astype(BF)
        gentry[rows, :] = dot(low, rw[rows, STATE:])
        gread[rows, :] = dot_tn(low, rw[rows, :STATE])


def input_grad_kernel(
    place, leave, d_ref, keep, states, conv, pre, gscan, z, st, rw, sconv, spre, rowside, colside, gentry,
    gread_a, gread_b, normed, taps, taps_state, par, wide, cols, low_inner, low_state, low_step, sums,
    sums_state, sums_head, *refs
):
    grad_outs, (gstates, gwi, gws, gwp, sems) = refs[:-5], refs[-5:]
    tokens, inner = conv.shape
    blocks = tokens // BLOCK
    tiles = inner // TILE
    heads = TILE // HEAD_DIM
    col = cols[...]
    x = normed[...]
    keep_sums = [[] for _ in range(blocks)]
    now = leave[...]
    keep_grads = [None] * blocks
    whole_matrix = head_matrix(0, inner)
    for b in range(blocks - 1, -1, -1):
        gstates[b] = now.astype(BF)
        sum_row = jnp.sum(now * states[b].astype(F32), axis=0, keepdims=True)
        keep_grads[b] = head_sum(jnp.broadcast_to(sum_row, (8, inner)), whole_matrix)[0:1]
        if b > 0:
            now = d_ref[b - 1] + expand(keep[b : b + 1], 0, inner // HEAD_DIM) * now
    step_grad = jnp.zeros((tokens, LANES), F32)
    out_side = jnp.zeros((tokens, LANES), F32)
    entry_grad = gentry[...]
    for tile in range(tiles):
        lanes = slice(tile * TILE, (tile + 1) * TILE)
        first = tile * heads
        matrix = head_matrix(first, TILE)
        c = conv[:, lanes].astype(F32)
        sg = sigmoid(c)
        act = (c * sg).astype(BF).astype(F32)
        step = expand(st[1], first, heads)
        out = expand(st[3], first, heads)
        scaled = (act * (step * out)).astype(BF)
        grads = []
        entries = []
        for b in range(blocks):
            rows = slice(b * BLOCK, (b + 1) * BLOCK)
            grads.append(dot(rw[rows, :STATE], gstates[b, :, lanes]))
            entries.append(dot_nt(scaled[rows], gstates[b, :, lanes]))
        grad_scaled = jnp.concatenate(grads, axis=0)
        entry_grad = entry_grad + jnp.concatenate(entries, axis=0)
        w = z[:, lanes].astype(F32) + out * grad_scaled
        step_grad = step_grad + head_sum(act * w, matrix)
        out_side = out_side + head_sum(scaled.astype(F32) * grad_scaled, matrix)
        grad = wide[1:2, lanes] * gscan[:, lanes].astype(F32) + step * w
        grad = grad * (sg * (1.0 + c * (1.0 - sg)))
        back, rows_sum = conv_backward(grad, pre[:, lanes].astype(F32), taps[:, lanes], col)
        low = back.astype(BF)
        low_inner[:, lanes] = low
        sums[:, lanes] = put_rows(rows_sum, TILE)
        gwi[:, lanes] = dot_tn(x, low).astype(BF)
    sc = sconv[...]
    sg = sigmoid(sc)
    grad = jnp.concatenate([entry_grad, gread_a[...] + gread_b[...]], axis=1)
    grad = grad * (sg * (1.0 + sc * (1.0 - sg)))
    back, rows_sum = conv_backward(grad, spre[...], taps_state, col)
    low = back.astype(BF)
    low_state[...] = low
    sums_state[...] = put_rows(rows_sum, 2 * STATE)
    gws[...] = dot_tn(x, low).astype(BF)
    i, j = lower_matrix()
    upper = (i <= j).astype(F32)
    at_end = lax.broadcasted_iota(jnp.int32, (BLOCK, LANES), 0) == BLOCK - 1
    decays = []
    for b in range(blocks):
        rows = slice(b * BLOCK, (b + 1) * BLOCK)
        side = out_side[rows]
        last = jnp.sum(side, axis=0, keepdims=True) + keep_grads[b] * keep[b : b + 1]
        cum_grad = rowside[rows, :] - colside[rows, :] - side + jnp.where(at_end, last, 0.0)
        decays.append(dot_high(upper, cum_grad))
    decay_grad = jnp.concatenate(decays, axis=0)
    rate = par[1:2]
    step_grad = (step_grad + decay_grad * rate) * sigmoid(st[0])
    rows_head = [
        jnp.sum(step_grad, axis=0, keepdims=True),
        jnp.sum(decay_grad * st[1] * rate, axis=0, keepdims=True),
    ]
    sums_head[...] = put_rows(rows_head, LANES)
    low = jnp.concatenate([jnp.zeros((HALO, LANES), F32), step_grad], axis=0).astype(BF)
    low_step[...] = low
    gwp[...] = dot_tn(x, low).astype(BF)
    store_grads(place, (gwi, gws, gwp), grad_outs, sems)


def token_grad_kernel(place, low_inner, low_state, low_step, gn_gate, tok, cot, gain, *refs):
    weights, (grad, back, sums, win, wst, wsp, sems) = refs[:-7], refs[-7:]
    load_weights(place, weights, (win, wst, wsp), sems)
    wait_weights((win, wst, wsp), sems)
    width = tok.shape[1]
    gn = dot_nt(low_inner[...], win[...]) + dot_nt(low_state[...], wst[...])
    gn = gn + dot_nt(low_step[...], wsp[...])
    gn = gn + jnp.concatenate([jnp.zeros((HALO, width), F32), gn_gate[...]], axis=0)
    t = tok[...].astype(F32)
    r = lax.rsqrt(jnp.mean(t * t, axis=1, keepdims=True) + EPS)
    scaled = t * r
    sums[...] = put_rows([jnp.sum(gn * scaled, axis=0, keepdims=True)], width)
    gg = gn * gain[0:1]
    result = gg * r - t * (r * r * r * jnp.mean(gg * t, axis=1, keepdims=True))
    back[...] = result[:HALO]
    grad[...] = result[HALO:] + cot[...].astype(F32)


def line(shift, size):
    return [(i, i + shift) for i in range(size) if 0 <= i + shift < size]


def pass_states(payload, size, sign):
    own = payload[:STATE].astype(F32)
    factor = payload[STATE].astype(F32) + payload[STATE + 1].astype(F32)
    came = lax.ppermute(payload, "tensor", line(sign, size))
    total = came[:STATE].astype(F32)
    total_factor = came[STATE].astype(F32) + came[STATE + 1].astype(F32)
    reach = 2
    while reach < size:
        send = own + factor[None] * total
        if 2 * reach < size:
            both = factor * total_factor
            hi = both.astype(BF)
            lo = (both - hi.astype(F32)).astype(BF)
            send = jnp.concatenate([send.astype(BF), hi[None], lo[None]], axis=0)
            came = lax.ppermute(send, "tensor", line(sign * reach, size))
            total = total + total_factor[None] * came[:STATE].astype(F32)
            total_factor = total_factor * (came[STATE].astype(F32) + came[STATE + 1].astype(F32))
        else:
            came = lax.ppermute(send.astype(BF), "tensor", line(sign * reach, size))
            total = total + total_factor[None] * came.astype(F32)
        reach = 2 * reach
    return total


def swap(values, mask):
    return lax.ppermute(values, "dp", [(i, i ^ mask) for i in range(8)])


def turn(values, shift):
    return lax.ppermute(values, "tensor", [(i, (i + shift) % 4) for i in range(4)])


def ring(values):
    return [values] + [turn(values, -m) for m in range(1, 4)]


def gather_pieces(column):
    same = [column] + [swap(column, k) for k in ORDER[1:4]]
    return same + [swap(v, 1) for v in same]


def reduce_swap(mine, other):
    came = swap(other, 1)
    parts = [mine[n] + came[n] for n in range(4)]
    total = parts[0].astype(F32)
    for n in range(1, 4):
        total = total + swap(parts[n], ORDER[n]).astype(F32)
    return total


def reduce_turn(parts):
    total = parts[0].astype(F32)
    for m in range(1, 4):
        total = total + turn(parts[m].astype(BF), m).astype(F32)
    return total


def reduce_all(values):
    values = values + swap(values, 1)
    values = values + swap(values, 2) + swap(values, 4) + swap(values, 6)
    return values + turn(values, 1) + turn(values, 2) + turn(values, 3)


def gather(shard):
    return lax.all_gather(
        lax.all_gather(shard, "tensor", axis=1, tiled=True), "dp", axis=0, tiled=True
    )


def scatter(grad):
    part = lax.psum_scatter(grad, "dp", scatter_dimension=0, tiled=True)
    return lax.psum_scatter(part, "tensor", scatter_dimension=1, tiled=True).astype(F32)


def make_shards(mesh):
    size = mesh.shape["tensor"]
    blocked = size == 4 and mesh.shape["dp"] == 8

    def shards(
        tokens, segments, cotangent, norm_gain, w_gate, w_inner, w_step, w_state, conv_inner, conv_state,
        step_bias, decay_log, skip_gain, out_gain, w_out,
    ):
        count, width = tokens.shape
        place = lax.axis_index("tensor")
        blocks = count // BLOCK
        inner = w_inner.shape[1] * size
        heads = w_step.shape[1] * size

        halo = lax.ppermute(tokens[count - HALO :], "tensor", line(1, size))
        tok = jnp.concatenate([halo, tokens], axis=0)
        wide_tok = tok.astype(F32)
        gain = norm_gain.astype(F32)
        rms = lax.rsqrt(jnp.mean(wide_tok * wide_tok, axis=1, keepdims=True) + EPS)
        normed = (wide_tok * rms * gain).astype(BF)

        padded = jnp.concatenate([jnp.full((HALO,), -1, jnp.int32), segments])
        near = lax.dynamic_slice(padded, (place * count,), (HALO + count,))
        seg = near[HALO:]
        masks = [near[HALO - k : HALO - k + count] == seg for k in range(1, KW)]
        grid = seg.reshape(blocks, BLOCK)
        prev = near[HALO - 1 : HALO - 1 + count].reshape(blocks, BLOCK)[:, :1]
        from_prev = (grid == prev).reshape(-1)
        at_last = (grid == grid[:, BLOCK - 1 :]).reshape(-1)
        cols = jnp.stack([*masks, from_prev, at_last], axis=1).astype(F32)
        seg_col = seg.astype(F32)[:, None]
        seg_row = seg.astype(F32)[None]

        def pad_heads(row):
            return jnp.pad(row, ((0, 0), (0, LANES - heads)))

        depth, span = w_inner.shape
        per = heads // size
        if blocked:
            small = jnp.zeros((HALO, span), BF)
            small = small.at[: KW + 1].set(conv_inner).at[KW + 1].set(out_gain)
            small = small.at[KW + 2, : 3 * per].set(jnp.concatenate([step_bias, decay_log, skip_gain]))
            side = jnp.pad(w_step, ((0, HALO), (0, LANES - per)))
            came = ring(jnp.concatenate([jnp.concatenate([w_inner, small], axis=0), side], axis=1))
            came_out = ring(jnp.stack([w_gate, w_out]))

            def in_order(parts):
                whole = jnp.concatenate(parts, axis=-1)
                return jnp.roll(whole, place * parts[0].shape[-1], axis=-1)

            steps = in_order([v[:depth, span : span + per] for v in came])
            last = jnp.concatenate([w_state, pad_heads(steps)], axis=1)
            pieces = gather_pieces(jnp.stack([v[:depth, :span] for v in came] + [last]))
            pieces_out = gather_pieces(jnp.stack(came_out))
            small = in_order([v[depth:, :span] for v in came]).astype(F32)
            conv_whole, gain_whole = small[: KW + 1], small[KW + 1]
            head_whole = [
                in_order([v[depth + KW + 2, n * per : (n + 1) * per] for v in came]).astype(F32)
                for n in range(3)
            ]
        else:
            conv_whole, head_whole, gain_whole = [
                lax.all_gather(v, "tensor", axis=v.ndim - 1, tiled=True).astype(F32)
                for v in (conv_inner, jnp.stack([step_bias, decay_log, skip_gain]), out_gain)
            ]
            pieces = [gather(w_inner), lax.all_gather(w_state, "dp", axis=0, tiled=True), pad_heads(gather(w_step))]
            pieces_out = [gather(w_gate), gather(w_out)]
        taps = jnp.pad(conv_whole, ((0, 8 - KW - 1), (0, 0)))
        taps_state = jnp.pad(conv_state.astype(F32), ((0, 8 - KW - 1), (0, 0)))
        bias, rate, skip = head_whole[0], -jnp.exp(head_whole[1]), head_whole[2]
        par = pad_heads(jnp.pad(jnp.stack([bias, rate]), ((0, 6), (0, 0))))
        wide = jnp.pad(jnp.stack([gain_whole, jnp.repeat(skip, HEAD_DIM)]), ((0, 6), (0, 0)))
        where = jnp.stack([lax.axis_index("dp"), place]).astype(jnp.int32)
        in_scratch = [
            pltpu.VMEM((width, inner), BF),
            pltpu.VMEM((width, 2 * STATE), BF),
            pltpu.VMEM((width, LANES), BF),
            pltpu.SemaphoreType.DMA((3,)),
        ]
        out_scratch = [
            pltpu.VMEM((width, inner), BF),
            pltpu.VMEM((width, inner), BF),
            pltpu.SemaphoreType.DMA((2,)),
        ]

        def last_args(fixed, arrays):
            return {"args": (where, *fixed, *arrays), "far": range(1 + len(fixed), 1 + len(fixed) + len(arrays))}

        pre, conv, spre, sconv, rw, st, keep, c_ref, pay = call(
            project_kernel,
            [
                sds((HALO + count, inner), BF),
                sds((count, inner), BF),
                sds((HALO + count, 2 * STATE), F32),
                sds((count, 2 * STATE), F32),
                sds((count, 2 * STATE), BF),
                sds((5, count, LANES), F32),
                sds((8, LANES), F32),
                sds((max(1, blocks - 1), STATE, inner), F32),
                sds((STATE + HALO, inner), BF),
            ],
            scratch=in_scratch,
            **last_args((normed, taps, taps_state, par, cols), pieces),
            name="project",
            flops=2 * count * width * (inner + 384),
        )
        enter = pass_states(pay, size, 1)
        gate, gout, y = call(
            middle_kernel,
            [sds((count, inner), BF), sds((count, inner), BF), sds((count, inner), F32)],
            scratch=[pltpu.VMEM((BLOCK, BLOCK), F32), pltpu.VMEM((LANES, BLOCK), F32), *out_scratch],
            **last_args((normed, cotangent, conv, st, rw, seg_col, seg_row), pieces_out),
            name="middle",
            flops=4 * count * width * inner,
        )
        out_low, ggate, gscan, rowside, gread_a, states, d_ref, pay, sums = call(
            output_kernel,
            [
                sds((count, inner), BF),
                sds((count, inner), BF),
                sds((count, inner), BF),
                sds((count, LANES), F32),
                sds((count, STATE), F32),
                sds((blocks, STATE, inner), BF),
                sds((max(1, blocks - 1), STATE, inner), F32),
                sds((STATE + HALO, inner), BF),
                sds((8, inner), F32),
            ],
            (where, enter, c_ref, keep, gate, gout, y, conv, rw, st, wide),
            [pltpu.VMEM((ROWS, inner), F32), pltpu.VMEM((blocks, STATE, inner), F32)],
            name="output",
            flops=6 * count * STATE * inner,
        )
        leave = pass_states(pay, size, -1)
        if blocked:
            shapes_out = [sds((4, 4, 2, depth, span), BF)] * 2
            shapes_in = [sds((4, 5, depth, span), BF)] * 2
        else:
            shapes_out = [sds((width, inner), BF)] * 2
            shapes_in = [sds((width, inner), BF), sds((width, 2 * STATE), BF), sds((width, LANES), BF)]
        mixed, gn_gate, *grads_out = call(
            gate_grad_kernel,
            [sds((count, width), BF), sds((count, width), F32), *shapes_out],
            far_outs=(2, 3),
            scratch=[
                pltpu.VMEM((width, inner), BF),
                pltpu.VMEM((width, inner), BF),
                *out_scratch,
            ],
            **last_args((normed, cotangent, out_low, ggate, tok), pieces_out),
            name="gate_grad",
            flops=8 * count * width * inner,
        )
        z, colside, gentry, gread_b = call(
            scan_grad_kernel,
            [
                sds((count, inner), BF),
                sds((count, LANES), F32),
                sds((count, STATE), F32),
                sds((count, STATE), F32),
            ],
            (where, gscan, conv, st, rw, seg_col, seg_row),
            [
                pltpu.VMEM((BLOCK, BLOCK), F32),
                pltpu.VMEM((BLOCK, BLOCK), F32),
                pltpu.VMEM((LANES, BLOCK), F32),
            ],
            name="scan_grad",
            flops=4 * count * BLOCK * inner,
        )
        low_inner, low_state, low_step, sums_in, sums_state, sums_head, *grads_in = call(
            input_grad_kernel,
            [
                sds((HALO + count, inner), BF),
                sds((HALO + count, 2 * STATE), BF),
                sds((HALO + count, LANES), BF),
                sds((8, inner), F32),
                sds((8, 2 * STATE), F32),
                sds((8, LANES), F32),
                *shapes_in,
            ],
            (
                where, leave, d_ref, keep, states, conv, pre, gscan, z, st, rw, sconv, spre, rowside, colside, gentry,
                gread_a, gread_b, normed, taps, taps_state, par, wide, cols,
            ),
            [pltpu.VMEM((blocks, STATE, inner), BF), *in_scratch],
            far_outs=range(6, 6 + len(shapes_in)),
            name="input_grad",
            flops=2 * count * width * inner,
        )
        grad, back, sums_norm = call(
            token_grad_kernel,
            [sds((count, width), F32), sds((HALO, width), F32), sds((8, width), F32)],
            scratch=in_scratch,
            **last_args((low_inner, low_state, low_step, gn_gate, tok, cotangent, gain[None]), pieces),
            name="token_grad",
            flops=2 * count * width * inner,
        )
        back = lax.ppermute(back, "tensor", line(-1, size))
        grad = grad.at[count - HALO :].add(back)

        skip_sums = sums[1].reshape(heads, HEAD_DIM).sum(1)
        if blocked:
            flat = jnp.concatenate(
                [
                    sums_in[: KW + 1].reshape(-1),
                    sums[0],
                    sums_state[: KW + 1].reshape(-1),
                    sums_norm[0],
                    sums_head[:2].reshape(-1),
                    skip_sums,
                ]
            )
            flat = jnp.pad(flat, (0, -flat.shape[0] % 1024)).reshape(-1, LANES)
            flat = reduce_all(flat).reshape(-1)
            small = []
            at = 0
            for shape in ((KW + 1, inner), (inner,), (KW + 1, 2 * STATE), (width,), (2, LANES), (heads,)):
                length = 1
                for extent in shape:
                    length = length * extent
                small.append(flat[at : at + length].reshape(shape))
                at = at + length
            out_sums = reduce_swap(*grads_out)
            out_sums = reduce_turn([out_sums[m] for m in range(4)])
            in_sums = reduce_swap(*grads_in)
            in_sums = reduce_turn([jnp.stack([in_sums[m], in_sums[4]]) for m in range(4)])
            grad_gate, grad_out = out_sums[0], out_sums[1]
            grad_inner = in_sums[0]
            grad_state = in_sums[1, :, : 2 * STATE]
            grad_step = lax.dynamic_slice(in_sums[1], (0, 2 * STATE + place * per), (depth, per))
        else:
            small = lax.psum(
                (sums_in, sums[0], sums_state, sums_norm[0], sums_head, skip_sums), ("dp", "tensor")
            )
            grad_gate, grad_out, grad_inner, grad_step = [
                scatter(v) for v in (*grads_out, grads_in[0], grads_in[2][:, :heads])
            ]
            grad_state = lax.psum_scatter(grads_in[1], "dp", scatter_dimension=0, tiled=True)
            grad_state = lax.psum(grad_state, "tensor").astype(F32)

        def mine(row, length):
            return lax.dynamic_slice(row, (place * length,), (length,))

        return (
            mixed,
            grad,
            small[3],
            grad_gate,
            grad_inner,
            grad_step,
            grad_state,
            lax.dynamic_slice(small[0], (0, place * span), (KW + 1, span)),
            small[2][: KW + 1],
            mine(small[4][0], per),
            mine(small[4][1], per),
            mine(small[5], per),
            mine(small[1], span),
            grad_out,
        )

    return shards


def solution(mesh):
    in_specs = (
        P(("dp", "tensor"), None),
        P("dp"),
        P(("dp", "tensor"), None),
        P(),
        P("dp", "tensor"),
        P("dp", "tensor"),
        P("dp", "tensor"),
        P("dp", None),
        P(None, "tensor"),
        P(),
        P("tensor"),
        P("tensor"),
        P("tensor"),
        P("tensor"),
        P("dp", "tensor"),
    )
    out_specs = (
        P(("dp", "tensor"), None),
        P(("dp", "tensor"), None),
        P(),
        P("dp", "tensor"),
        P("dp", "tensor"),
        P("dp", "tensor"),
        P("dp", None),
        P(None, "tensor"),
        P(),
        P("tensor"),
        P("tensor"),
        P("tensor"),
        P("tensor"),
        P("dp", "tensor"),
    )
    return jax.shard_map(
        make_shards(mesh), mesh=mesh, in_specs=in_specs, out_specs=out_specs, check_vma=False
    )
```

```python
import functools
import math

import jax
import jax.numpy as jnp
from jax import lax
from jax.experimental import pallas as pl
from jax.experimental.pallas import tpu as pltpu
from jax.sharding import PartitionSpec as P

HEAD_DIM = 64
STATE = 128
KW = 4
BLOCK = 256
HALO = 16
LANES = 128
TILE = 256
ROWS = 128
EPS = 1e-05
F32 = jnp.float32
BF = jnp.bfloat16
HIGH = lax.Precision.HIGHEST
SPARE = 3 * 2**20
ORDER = (0, 2, 4, 6, 1, 3, 5, 7)


def dot(a, b):
    return lax.dot_general(a, b, (((1,), (0,)), ((), ())), preferred_element_type=F32)


def dot_nt(a, b):
    return lax.dot_general(a, b, (((1,), (1,)), ((), ())), preferred_element_type=F32)


def dot_tn(a, b):
    return lax.dot_general(a, b, (((0,), (0,)), ((), ())), preferred_element_type=F32)


def dot_high(a, b):
    return lax.dot_general(
        a, b, (((1,), (0,)), ((), ())), precision=HIGH, preferred_element_type=F32
    )


def sigmoid(x):
    return 1.0 / (1.0 + jnp.exp(-x))


def expand(x, first, count):
    lane = lax.broadcasted_iota(jnp.int32, (x.shape[0], LANES), 1)
    return jnp.concatenate(
        [
            jnp.where(lane < HEAD_DIM, x[:, h : h + 1], x[:, h + 1 : h + 2])
            for h in range(first, first + count, 2)
        ],
        axis=1,
    )


def head_matrix(first, channels):
    channel = lax.broadcasted_iota(jnp.int32, (channels, LANES), 0)
    head = lax.broadcasted_iota(jnp.int32, (channels, LANES), 1)
    return (channel // HEAD_DIM + first == head).astype(BF)


def head_sum(x, matrix):
    hi = x.astype(BF)
    lo = (x - hi.astype(F32)).astype(BF)
    return dot(hi, matrix) + dot(lo, matrix)


def lower_matrix():
    i = lax.broadcasted_iota(jnp.int32, (BLOCK, BLOCK), 0)
    j = lax.broadcasted_iota(jnp.int32, (BLOCK, BLOCK), 1)
    return i, j


def conv_forward(values, taps, cols):
    result = taps[KW : KW + 1] + taps[0:1] * values[HALO:]
    for k in range(1, KW):
        result = result + taps[k : k + 1] * pltpu.roll(values, k, 0)[HALO:] * cols[:, k - 1 : k]
    return result


def conv_backward(grad, values, taps, cols):
    width = grad.shape[1]
    whole = HALO + grad.shape[0]
    zero = jnp.zeros((HALO, width), F32)
    base = jnp.concatenate([zero, grad], axis=0)
    result = taps[0:1] * base
    sums = [jnp.sum(grad * values[HALO:], axis=0, keepdims=True)]
    for k in range(1, KW):
        masked = jnp.concatenate([zero, grad * cols[:, k - 1 : k]], axis=0)
        back = pltpu.roll(masked, whole - k, 0)
        result = result + taps[k : k + 1] * back
        sums.append(jnp.sum(back * values, axis=0, keepdims=True))
    sums.append(jnp.sum(grad, axis=0, keepdims=True))
    return result, sums


def put_rows(rows, width):
    index = lax.broadcasted_iota(jnp.int32, (8, width), 0)
    result = jnp.zeros((8, width), F32)
    for i, row in enumerate(rows):
        result = jnp.where(index == i, row, result)
    return result


def call(kernel, outs, args, scratch=(), name=None, micros=1.0, far=(), far_outs=()):
    size = 1 << 20

    held = [a for i, a in enumerate(args) if i > 0 and i not in far]
    held += [o for i, o in enumerate(outs) if i not in far_outs]
    limit = SPARE + sum(a.size * a.dtype.itemsize for a in held)
    for item in scratch:
        limit += math.prod(item.shape) * 4

    def spec(space):
        return pl.BlockSpec(memory_space=space)

    ins = [
        spec(pltpu.SMEM if i == 0 else pltpu.HBM if i in far else pltpu.VMEM) for i in range(len(args))
    ]
    return pl.pallas_call(
        kernel,
        out_shape=outs,
        in_specs=ins,
        out_specs=[spec(pl.ANY if i in far_outs else pltpu.VMEM) for i in range(len(outs))],
        scratch_shapes=list(scratch),
        compiler_params=pltpu.CompilerParams(vmem_limit_bytes=limit),
        cost_estimate=pl.CostEstimate(flops=int(micros * 1.15e9), bytes_accessed=size, transcendentals=0),
        name=name,
    )(*args)


def sds(shape, dtype):
    return jax.ShapeDtypeStruct(shape, dtype)


def aligned(value, size):
    return pl.multiple_of(value * size, size)


def load_weights(place, refs, targets, sems):
    if len(refs[0].shape) == 2:
        copies = [pltpu.make_async_copy(r, t, sems.at[n]) for n, (r, t) in enumerate(zip(refs, targets))]
        for copy in copies:
            copy.start()
        return
    split = refs[0].shape[0] == 5
    depth, span = refs[0].shape[-2:]
    for n, k in enumerate(ORDER):
        row = pl.ds(aligned(place[0] ^ k, depth), depth)
        for m in range(4):
            column = pl.ds(aligned((place[1] + m) % 4, span), span)
            for g in range(1 if split else 2):
                source = refs[n].at[m] if split else refs[n].at[m, g]
                pltpu.make_async_copy(source, targets[g].at[row, column], sems.at[g]).start()
        if split:
            wide = targets[1].shape[1]
            pltpu.make_async_copy(refs[n].at[4, :, :wide], targets[1].at[row, :], sems.at[1]).start()
            pltpu.make_async_copy(refs[n].at[4, :, wide:], targets[2].at[row, :], sems.at[2]).start()


def wait_weights(targets, sems):
    for n, target in enumerate(targets):
        pltpu.make_async_copy(target, target, sems.at[n]).wait()


def store_grads(place, sources, outs, sems):
    if len(outs[0].shape) == 2:
        copies = [pltpu.make_async_copy(s, o, sems.at[n]) for n, (s, o) in enumerate(zip(sources, outs))]
        for copy in copies:
            copy.start()
    else:
        split = outs[0].shape[1] == 5
        depth, span = outs[0].shape[-2:]
        for n, k in enumerate(ORDER):
            out = outs[n // 4].at[n % 4]
            sem = sems.at[n // 4]
            row = pl.ds(aligned(place[0] ^ k, depth), depth)
            for m in range(4):
                column = pl.ds(aligned((place[1] + m) % 4, span), span)
                for g in range(1 if split else 2):
                    target = out.at[m] if split else out.at[m, g]
                    pltpu.make_async_copy(sources[g].at[row, column], target, sem).start()
            if split:
                wide = sources[1].shape[1]
                pltpu.make_async_copy(sources[1].at[row, :], out.at[4, :, :wide], sem).start()
                pltpu.make_async_copy(sources[2].at[row, :], out.at[4, :, wide:], sem).start()
    for n, out in enumerate(outs):
        pltpu.make_async_copy(out, out, sems.at[n]).wait()


def unpack_kernel(place, *refs):
    parts, (state, column, taps, par, wide) = refs[:4], refs[4:]
    depth, span = column.shape[1:]
    per = span // HEAD_DIM
    heads = wide.shape[1] // HEAD_DIM
    lane = lax.broadcasted_iota(jnp.int32, (8, LANES), 1)
    step = jnp.zeros((depth, LANES), F32)
    rows = [jnp.zeros((8, LANES), F32)] * 3
    for m, part in enumerate(parts):
        who = (place[1] + m) % 4
        lanes = pl.ds(aligned(who, span), span)
        column[m] = part[:depth, :span]
        step = step + pltpu.roll(part[:depth, span:].astype(F32), who * per, 1)
        low = part[depth:, :span].astype(F32)
        taps[:, lanes] = low[:8]
        wide[0:1, lanes] = low[KW + 1 : KW + 2]
        row = jnp.broadcast_to(low[KW + 2 : KW + 3, :LANES], (8, LANES))
        for n in range(3):
            own = pltpu.roll(row, LANES - n * per, 1) if n else row
            rows[n] = rows[n] + pltpu.roll(jnp.where(lane < per, own, 0.0), who * per, 1)
    column[4] = jnp.concatenate([state[...], step.astype(BF)], axis=1)
    par[...] = put_rows([rows[0][0:1], jnp.where(lane < heads, -jnp.exp(rows[1]), 0.0)[0:1]], LANES)
    wide[1:2, :] = expand(rows[2], 0, heads)[0:1]


def project_kernel(
    place, *refs
):
    (normed, taps, taps_state, par, cols), refs = refs[:5], refs[5:]
    weights, refs = refs[:-13], refs[-13:]
    pre, conv, spre, sconv, rw, st, keep, c_ref, pay, win, wst, wsp, sems = refs
    load_weights(place, weights, (win, wst, wsp), sems)
    wait_weights((win, wst, wsp), sems)
    project(normed, win, wst, wsp, taps, taps_state, par, cols, pre, conv, spre, sconv, rw, st, keep, c_ref, pay)


def project(
    normed, win, wst, wsp, taps, taps_state, par, cols, pre, conv, spre, sconv, rw, st, keep, c_ref, pay
):
    tokens = conv.shape[0]
    inner = conv.shape[1]
    blocks = tokens // BLOCK
    x = normed[...]
    low = x[HALO:]
    col = cols[...]
    sp = dot(low, wsp[...]) + par[0:1]
    step = jnp.maximum(sp, 0.0) + jnp.log1p(jnp.exp(-jnp.abs(sp)))
    decay = step * par[1:2]
    i, j = lower_matrix()
    lower = (i >= j).astype(F32)
    st[0] = sp
    st[1] = step
    keeps = []
    outs = []
    for b in range(blocks):
        rows = slice(b * BLOCK, (b + 1) * BLOCK)
        cum = dot_high(lower, decay[rows])
        last = cum[BLOCK - 1 : BLOCK]
        from_prev = col[rows, 3:4]
        out = jnp.exp(last - cum) * col[rows, 4:5]
        st[2, rows] = cum
        st[3, rows] = out
        st[4, rows] = jnp.exp(cum) * from_prev
        keeps.append(jnp.exp(last) * from_prev[BLOCK - 1 : BLOCK])
        outs.append(out * step[rows])
    keep[...] = put_rows(keeps, LANES)
    whole = keeps[0]
    for b in range(1, blocks):
        whole = whole * keeps[b]
    state = dot(x, wst[...])
    spre[...] = state
    sc = conv_forward(state, taps_state, col)
    sconv[...] = sc
    rw[...] = (sc * sigmoid(sc)).astype(BF)
    entry = rw[:, :STATE]
    index = lax.broadcasted_iota(jnp.int32, (HALO, TILE), 0)
    for tile in range(inner // TILE):
        lanes = slice(tile * TILE, (tile + 1) * TILE)
        heads = TILE // HEAD_DIM
        first = tile * heads
        value = dot(x, win[:, lanes])
        pre[:, lanes] = value.astype(BF)
        c = conv_forward(value, taps[:, lanes], col)
        conv[:, lanes] = c
        c = c.astype(F32)
        act = (c * sigmoid(c)).astype(BF).astype(F32)
        total = None
        for b in range(blocks):
            rows = slice(b * BLOCK, (b + 1) * BLOCK)
            scaled = (act[rows] * expand(outs[b], first, heads)).astype(BF)
            part = dot_tn(entry[rows], scaled)
            if b < blocks - 1:
                c_ref[b, :, lanes] = part
            total = part if b == 0 else total * expand(keeps[b], first, heads) + part
        pay[:STATE, lanes] = total.astype(BF)
        wide = expand(whole, first, heads)
        hi = wide.astype(BF).astype(F32)
        pay[STATE:, lanes] = jnp.where(index == 0, hi, jnp.where(index == 1, wide - hi, 0.0)).astype(BF)


def gate_kernel(place, normed, cot, *refs):
    weights, (gate, gout, wg, wo, sems) = refs[:-5], refs[-5:]
    load_weights(place, weights, (wg, wo), sems)
    wait_weights((wg, wo), sems)
    for tile in range(gate.shape[1] // TILE):
        lanes = slice(tile * TILE, (tile + 1) * TILE)
        gate[:, lanes] = dot(normed[HALO:, :], wg[:, lanes])
        gout[:, lanes] = dot(cot[...], wo[:, lanes])


def scan_kernel(place, conv, st, rw, seg_col, seg_row, y, smask, cum_t):
    tokens, inner = conv.shape
    blocks = tokens // BLOCK
    half = BLOCK // 2
    i, j = lower_matrix()
    lane = lax.broadcasted_iota(jnp.int32, (BLOCK, LANES), 1)
    for b in range(blocks):
        rows = slice(b * BLOCK, (b + 1) * BLOCK)
        scores = dot_nt(rw[rows, STATE:], rw[rows, :STATE])
        same = (i >= j) & (seg_col[rows, 0:1] == seg_row[0:1, rows])
        smask[...] = jnp.where(same, scores, 0.0)
        cum_t[...] = st[2, rows].T

        def pair(p, carry):
            cum = pltpu.roll(st[2, rows], LANES - 2 * p, 1)
            step = pltpu.roll(st[1, rows], LANES - 2 * p, 1)
            lanes = pl.ds(pl.multiple_of(p * LANES, LANES), LANES)
            c = conv[rows, lanes].astype(F32)
            act = (c * sigmoid(c)).astype(BF).astype(F32)
            xs = (act * jnp.where(lane < HEAD_DIM, step[:, 0:1], step[:, 1:2])).astype(BF)
            top = jnp.zeros((half, LANES), F32)
            bottom = jnp.zeros((half, LANES), F32)
            for a in range(2):
                mine = jnp.where((lane < HEAD_DIM) == (a == 0), xs, jnp.zeros_like(xs))
                row = cum_t[pl.ds(2 * p + a, 1), :]
                e = jnp.exp(jnp.minimum(cum[:half, a : a + 1] - row[:, :half], 0.0))
                top = top + dot((smask[:half, :half] * e).astype(BF), mine[:half])
                e = jnp.exp(jnp.minimum(cum[half:, a : a + 1] - row, 0.0))
                bottom = bottom + dot((smask[half:, :] * e).astype(BF), mine)
            y[b * BLOCK : b * BLOCK + half, lanes] = top
            y[b * BLOCK + half : (b + 1) * BLOCK, lanes] = bottom
            return carry

        lax.fori_loop(0, inner // LANES, pair, 0)


def output_kernel(
    place, near, far, c_ref, keep, gate, gout, y, conv, rw, st, wide, out_low, ggate, gscan, rowside, gread, states,
    d_ref, pay, sums, so_ref, d_all
):
    tokens, inner = conv.shape
    blocks = tokens // BLOCK
    tiles = inner // TILE
    heads = TILE // HEAD_DIM
    now = None
    for b in range(blocks):
        now = entering(near, far) if b == 0 else now * expand(keep[b - 1 : b], 0, inner // HEAD_DIM) + c_ref[b - 1]
        states[b] = now.astype(BF)
    sums[...] = jnp.zeros_like(sums)
    d_all[...] = jnp.zeros_like(d_all)

    def chunk(r, carry):
        rows = pl.ds(pl.multiple_of(r * ROWS, ROWS), ROWS)
        b = r // (BLOCK // ROWS)
        read = rw[rows, STATE:]
        scale = st[4, rows, :]
        total = jnp.zeros((ROWS, 1), F32)
        cross = jnp.zeros((ROWS, 1), F32)
        for tile in range(tiles):
            lanes = slice(tile * TILE, (tile + 1) * TILE)
            raw = dot(read, states[b, :, lanes])
            so = y[rows, lanes] + raw * expand(scale, tile * heads, heads)
            so_ref[:, lanes] = so
            c = conv[rows, lanes].astype(F32)
            u = so + wide[1:2, lanes] * (c * sigmoid(c))
            g = gate[rows, lanes].astype(F32)
            gated = u * (g * sigmoid(g))
            total = total + jnp.sum(gated * gated, axis=1, keepdims=True)
            go = gout[rows, lanes].astype(F32) * wide[0:1, lanes]
            cross = cross + jnp.sum(go * gated, axis=1, keepdims=True)
        rms = lax.rsqrt(total / inner + EPS)
        cube = rms * rms * rms * (cross / inner)
        side = jnp.zeros((ROWS, LANES), F32)
        read_grad = jnp.zeros((ROWS, STATE), F32)
        for tile in range(tiles):
            lanes = slice(tile * TILE, (tile + 1) * TILE)
            so = so_ref[:, lanes]
            c = conv[rows, lanes].astype(F32)
            act = c * sigmoid(c)
            u = so + wide[1:2, lanes] * act
            g = gate[rows, lanes].astype(F32)
            sg = sigmoid(g)
            silu = g * sg
            gated = u * silu
            gain = wide[0:1, lanes]
            out = gated * rms
            out_low[rows, lanes] = (out * gain).astype(BF)
            go = gout[rows, lanes].astype(F32)
            gg = go * gain * rms - gated * cube
            q = gg * silu
            ggate[rows, lanes] = (gg * u * (sg * (1.0 + g * (1.0 - sg)))).astype(BF)
            low = q.astype(BF)
            gscan[rows, lanes] = low
            low = low.astype(F32)
            sums[0:1, lanes] += jnp.sum(go * out, axis=0, keepdims=True)
            sums[1:2, lanes] += jnp.sum(q * act, axis=0, keepdims=True)
            side = side + head_sum(low * so, head_matrix(tile * heads, TILE))
            scaled = (low * expand(scale, tile * heads, heads)).astype(BF)
            d_all[b, :, lanes] += dot_tn(read, scaled)
            read_grad = read_grad + dot_nt(scaled, states[b, :, lanes])
        rowside[rows, :] = side
        gread[rows, :] = read_grad
        return carry

    lax.fori_loop(0, tokens // ROWS, chunk, 0)
    for b in range(1, blocks):
        d_ref[b - 1] = d_all[b]
    total = d_all[blocks - 1]
    whole = keep[blocks - 1 : blocks]
    for b in range(blocks - 2, -1, -1):
        total = d_all[b] + expand(keep[b : b + 1], 0, inner // HEAD_DIM) * total
        whole = whole * keep[b : b + 1]
    pay[:STATE] = total.astype(BF)
    index = lax.broadcasted_iota(jnp.int32, (HALO, inner), 0)
    wide_keep = expand(whole, 0, inner // HEAD_DIM)
    hi = wide_keep.astype(BF).astype(F32)
    pay[STATE:] = jnp.where(index == 0, hi, jnp.where(index == 1, wide_keep - hi, 0.0)).astype(BF)


def gate_grad_kernel(place, normed, cot, out_low, ggate, tok, *refs):
    (mixed, gn), refs = refs[-9:-7], refs[:-9] + refs[-7:]
    weights, (out_a, out_b, gwg, gwo, wg, wo, sems) = refs[:-7], refs[-7:]
    load_weights(place, weights, (wg, wo), sems)
    inner = out_low.shape[1]
    low = normed[HALO:, :]
    for tile in range(inner // TILE):
        lanes = slice(tile * TILE, (tile + 1) * TILE)
        gwo[:, lanes] = dot_tn(cot[...], out_low[:, lanes]).astype(BF)
        gwg[:, lanes] = dot_tn(low, ggate[:, lanes]).astype(BF)
    wait_weights((wg, wo), sems)
    gn[...] = dot_nt(ggate[...], wg[...])
    mixed[...] = (tok[HALO:, :].astype(F32) + dot_nt(out_low[...], wo[...])).astype(BF)
    store_grads(place, (gwg, gwo), (out_a, out_b), sems)


def scan_grad_kernel(b, place, gscan, conv, st, rw, seg_col, seg_row, z, colside, gentry, gread, smask, acc, cum_t):
    inner = conv.shape[1]
    half = BLOCK // 2
    j, i = lower_matrix()
    lane = lax.broadcasted_iota(jnp.int32, (BLOCK, LANES), 1)
    rows = slice(b * BLOCK, (b + 1) * BLOCK)
    same = (i >= j) & (seg_col[rows, 0:1] == seg_row[0:1, rows])
    scores = dot_nt(rw[rows, :STATE], rw[rows, STATE:])
    smask[...] = jnp.where(same, scores, 0.0)
    cum_t[...] = st[2, rows].T
    acc[...] = jnp.zeros_like(acc)
    colside[...] = jnp.zeros((BLOCK, LANES), F32)

    def pair(p, carry):
        cum = pltpu.roll(st[2, rows], LANES - 2 * p, 1)
        step = pltpu.roll(st[1, rows], LANES - 2 * p, 1)
        lanes = pl.ds(pl.multiple_of(p * LANES, LANES), LANES)
        c = conv[rows, lanes].astype(F32)
        act = (c * sigmoid(c)).astype(BF).astype(F32)
        xs = (act * jnp.where(lane < HEAD_DIM, step[:, 0:1], step[:, 1:2])).astype(BF)
        gs = gscan[rows, lanes]
        gs_t = gs.T
        top = jnp.zeros((half, LANES), F32)
        bottom = jnp.zeros((half, LANES), F32)
        for a in range(2):
            keep = (lane < HEAD_DIM) == (a == 0)
            mine = jnp.where(keep, xs, jnp.zeros_like(xs))
            grad = jnp.where(keep, gs, jnp.zeros_like(gs))
            row = cum_t[pl.ds(2 * p + a, 1), :]
            e = jnp.exp(jnp.minimum(row - cum[:half, a : a + 1], 0.0))
            top = top + dot((smask[:half, :] * e).astype(BF), grad)
            acc[:half, :] += dot(mine[:half], gs_t) * e
            e = jnp.exp(jnp.minimum(row[:, half:] - cum[half:, a : a + 1], 0.0))
            bottom = bottom + dot((smask[half:, half:] * e).astype(BF), grad[half:])
            acc[half:, half:] += dot(mine[half:], gs_t[:, half:]) * e
        both = jnp.concatenate([top, bottom], axis=0)
        z[:, lanes] = both
        channel = lax.broadcasted_iota(jnp.int32, (LANES, LANES), 0)
        head = lax.broadcasted_iota(jnp.int32, (LANES, LANES), 1)
        matrix = (channel // HEAD_DIM + 2 * p == head).astype(BF)
        colside[...] += head_sum(both * xs.astype(F32), matrix)
        return carry

    lax.fori_loop(0, inner // LANES, pair, 0)
    low = jnp.where(same, acc[...], 0.0).astype(BF)
    gentry[...] = dot(low, rw[rows, STATE:])
    gread[...] = dot_tn(low, rw[rows, :STATE])


def input_grad_kernel(
    place, near, far, d_ref, keep, states, conv, pre, gscan, st, rw, sconv, spre, rowside, gread_a, taps,
    taps_state, par, wide, cols, *refs
):
    by_block, (low_inner, low_state, low_step, sums, sums_state, sums_head, gstates) = refs[:-7], refs[-7:]
    z, colside, gentry, gread_b = [
        jnp.concatenate([ref[...] for ref in by_block[n::4]], axis=0) if n else by_block[n::4] for n in range(4)
    ]
    tokens, inner = conv.shape
    blocks = tokens // BLOCK
    tiles = inner // TILE
    heads = TILE // HEAD_DIM
    col = cols[...]
    now = entering(near, far)
    keep_grads = [None] * blocks
    whole_matrix = head_matrix(0, inner)
    for b in range(blocks - 1, -1, -1):
        gstates[b] = now.astype(BF)
        sum_row = jnp.sum(now * states[b].astype(F32), axis=0, keepdims=True)
        keep_grads[b] = head_sum(jnp.broadcast_to(sum_row, (8, inner)), whole_matrix)[0:1]
        if b > 0:
            now = d_ref[b - 1] + expand(keep[b : b + 1], 0, inner // HEAD_DIM) * now
    step_grad = jnp.zeros((tokens, LANES), F32)
    out_side = jnp.zeros((tokens, LANES), F32)
    entry_grad = gentry
    for tile in range(tiles):
        lanes = slice(tile * TILE, (tile + 1) * TILE)
        first = tile * heads
        matrix = head_matrix(first, TILE)
        c = conv[:, lanes].astype(F32)
        sg = sigmoid(c)
        act = (c * sg).astype(BF).astype(F32)
        step = expand(st[1], first, heads)
        out = expand(st[3], first, heads)
        scaled = (act * (step * out)).astype(BF)
        grads = []
        entries = []
        for b in range(blocks):
            rows = slice(b * BLOCK, (b + 1) * BLOCK)
            grads.append(dot(rw[rows, :STATE], gstates[b, :, lanes]))
            entries.append(dot_nt(scaled[rows], gstates[b, :, lanes]))
        grad_scaled = jnp.concatenate(grads, axis=0)
        entry_grad = entry_grad + jnp.concatenate(entries, axis=0)
        w = jnp.concatenate([ref[:, lanes] for ref in z], axis=0) + out * grad_scaled
        step_grad = step_grad + head_sum(act * w, matrix)
        out_side = out_side + head_sum(scaled.astype(F32) * grad_scaled, matrix)
        grad = wide[1:2, lanes] * gscan[:, lanes].astype(F32) + step * w
        grad = grad * (sg * (1.0 + c * (1.0 - sg)))
        back, rows_sum = conv_backward(grad, pre[:, lanes].astype(F32), taps[:, lanes], col)
        low = back.astype(BF)
        low_inner[:, lanes] = low
        sums[:, lanes] = put_rows(rows_sum, TILE)
    sc = sconv[...]
    sg = sigmoid(sc)
    grad = jnp.concatenate([entry_grad, gread_a[...] + gread_b], axis=1)
    grad = grad * (sg * (1.0 + sc * (1.0 - sg)))
    back, rows_sum = conv_backward(grad, spre[...], taps_state, col)
    low = back.astype(BF)
    low_state[...] = low
    sums_state[...] = put_rows(rows_sum, 2 * STATE)
    i, j = lower_matrix()
    upper = (i <= j).astype(F32)
    at_end = lax.broadcasted_iota(jnp.int32, (BLOCK, LANES), 0) == BLOCK - 1
    decays = []
    for b in range(blocks):
        rows = slice(b * BLOCK, (b + 1) * BLOCK)
        side = out_side[rows]
        last = jnp.sum(side, axis=0, keepdims=True) + keep_grads[b] * keep[b : b + 1]
        cum_grad = rowside[rows, :] - colside[rows] - side + jnp.where(at_end, last, 0.0)
        decays.append(dot_high(upper, cum_grad))
    decay_grad = jnp.concatenate(decays, axis=0)
    rate = par[1:2]
    step_grad = (step_grad + decay_grad * rate) * sigmoid(st[0])
    rows_head = [
        jnp.sum(step_grad, axis=0, keepdims=True),
        jnp.sum(decay_grad * st[1] * rate, axis=0, keepdims=True),
    ]
    sums_head[...] = put_rows(rows_head, LANES)
    low = jnp.concatenate([jnp.zeros((HALO, LANES), F32), step_grad], axis=0).astype(BF)
    low_step[...] = low


def weight_grad_kernel(place, normed, low_inner, low_state, low_step, *refs):
    grad_outs, (gwi, gws, gwp, sems) = refs[:-4], refs[-4:]
    x = normed[...]
    for tile in range(low_inner.shape[1] // TILE):
        lanes = slice(tile * TILE, (tile + 1) * TILE)
        gwi[:, lanes] = dot_tn(x, low_inner[:, lanes]).astype(BF)
    gws[...] = dot_tn(x, low_state[...]).astype(BF)
    gwp[...] = dot_tn(x, low_step[...]).astype(BF)
    store_grads(place, (gwi, gws, gwp), grad_outs, sems)


def token_grad_kernel(
    place, low_inner, low_state, low_step, gn_gate, tok, cot, gain, sums_in, sums_out, sums_state, sums_head, *refs
):
    weights, (grad, back, pack, win, wst, wsp, sems) = refs[:-7], refs[-7:]
    load_weights(place, weights, (win, wst, wsp), sems)
    wait_weights((win, wst, wsp), sems)
    width = tok.shape[1]
    gn = dot_nt(low_inner[...], win[...]) + dot_nt(low_state[...], wst[...])
    gn = gn + dot_nt(low_step[...], wsp[...])
    gn = gn + jnp.concatenate([jnp.zeros((HALO, width), F32), gn_gate[...]], axis=0)
    t = tok[...].astype(F32)
    r = lax.rsqrt(jnp.mean(t * t, axis=1, keepdims=True) + EPS)
    scaled = t * r
    inner = pack.shape[1]
    pack[0 : KW + 1, :] = sums_in[: KW + 1]
    pack[KW + 1 : KW + 2, :] = sums_out[0:1]
    pack[KW + 2 :, :] = jnp.zeros((8 - KW - 2, inner), F32)
    pack[KW + 2 : KW + 3, :width] = jnp.sum(gn * scaled, axis=0, keepdims=True)
    pack[KW + 2 : KW + 3, width : width + LANES] = sums_head[0:1]
    pack[KW + 2 : KW + 3, width + LANES : width + 2 * LANES] = sums_head[1:2]
    skips = head_sum(sums_out[...], head_matrix(0, inner))
    pack[KW + 2 : KW + 3, width + 2 * LANES : width + 3 * LANES] = skips[1:2]
    for k in range(KW + 1):
        pack[KW + 3 : KW + 4, 2 * STATE * k : 2 * STATE * (k + 1)] = sums_state[k : k + 1]
    gg = gn * gain[0:1]
    result = gg * r - t * (r * r * r * jnp.mean(gg * t, axis=1, keepdims=True))
    back[...] = result[:HALO]
    grad[...] = result[HALO:] + cot[...].astype(F32)


def finish_kernel(place, a, b, c, d, own, norm, state, head, whole):
    span = own.shape[1]
    width = norm.shape[1]
    per = span // HEAD_DIM
    total = a[...] + b[...] + c[...] + d[...]
    whole[...] = total
    own[...] = whole[:, pl.ds(aligned(place[1], span), span)]
    norm[...] = total[KW + 2 : KW + 3, :width]
    state[...] = put_rows([total[KW + 3 : KW + 4, 2 * STATE * k : 2 * STATE * (k + 1)] for k in range(KW + 1)], 2 * STATE)
    rows = [total[KW + 2 : KW + 3, width + LANES * n : width + LANES * (n + 1)] for n in range(3)]
    head[...] = pltpu.roll(put_rows(rows, LANES), lax.rem(LANES - place[1] * per, LANES), 1)


def line(shift, size):
    return [(i, i + shift) for i in range(size) if 0 <= i + shift < size]


def pass_first(payload, size, sign):
    return lax.ppermute(payload, "tensor", line(sign, size))


def pass_states(payload, came, size, sign, first=()):
    own = payload[:STATE].astype(F32)
    factor = payload[STATE].astype(F32) + payload[STATE + 1].astype(F32)
    near, far, send = came, jnp.zeros_like(came[:STATE]), came
    reach = 2
    while reach < size:
        near_factor = near[STATE].astype(F32) + near[STATE + 1].astype(F32)
        total = near[:STATE].astype(F32)
        if reach > 2:
            total = total + last_factor[None] * far[:STATE].astype(F32)
        send = (own + factor[None] * total).astype(BF)
        if 2 * reach < size:
            both = factor * near_factor
            hi = both.astype(BF)
            lo = (both - hi.astype(F32)).astype(BF)
            send = jnp.concatenate([send, hi[None], lo[None]], axis=0)
        send = after(send, *first)
        far = lax.ppermute(send, "tensor", line(sign * reach, size))
        last_factor = near_factor
        if 2 * reach < size:
            total = near[:STATE].astype(F32) + near_factor[None] * far[:STATE].astype(F32)
            both = near_factor * (far[STATE].astype(F32) + far[STATE + 1].astype(F32))
            hi = both.astype(BF)
            lo = (both - hi.astype(F32)).astype(BF)
            near = jnp.concatenate([total.astype(BF), hi[None], lo[None]], axis=0)
            near = jnp.pad(near, ((0, HALO - 2), (0, 0)))
            far = jnp.zeros_like(far)
        reach = 2 * reach
    return near, far[:STATE], send


def entering(near, far):
    rows = near[STATE:, :].astype(F32)
    return near[:STATE, :].astype(F32) + (rows[0:1] + rows[1:2]) * far[...].astype(F32)


def swap(values, mask):
    return lax.ppermute(values, "dp", [(i, i ^ mask) for i in range(8)])


def turn(values, shift):
    return lax.ppermute(values, "tensor", [(i, (i + shift) % 4) for i in range(4)])


def ring(values):
    return [values] + [turn(values, -m) for m in range(1, 4)]


def gather_pieces(column, first=()):
    same = [column] + [swap(column, k) for k in ORDER[1:4]]
    return same + [swap(column, 1)] + [swap(after(v, *first), 1) for v in same[1:]]


def sum_pair_kernel(place, mine, came, *outs):
    for n, out in enumerate(outs):
        out[...] = mine[n] + came[n]


def sum_column_kernel(place, a, b, c, d, *outs):
    def total(m):
        return (a[m].astype(F32) + b[m].astype(F32) + c[m].astype(F32) + d[m].astype(F32)).astype(BF)

    for m, out in enumerate(outs):
        if len(a.shape) == 4:
            out[...] = total(m)
        else:
            out[0] = total(m)
            out[1] = total(4)


def sum_last_kernel(place, a, b, c, d, first, second):
    for n, out in enumerate((first, second)):
        out[...] = a[n].astype(F32) + b[n].astype(F32) + c[n].astype(F32) + d[n].astype(F32)


def reduce_core(where, mine, other):
    came = swap(other, 1)
    return call(sum_pair_kernel, [sds(mine.shape[1:], BF)] * 4, (where, mine, came), name="sum_pair")


def reduce_plane(where, parts):
    came = [swap(parts[n], ORDER[n]) for n in range(1, 4)]
    shape = (2, *parts[0].shape[-2:])
    return call(sum_column_kernel, [sds(shape, BF)] * 4, (where, parts[0], *came), name="sum_column")


def reduce_line(where, parts):
    came = [turn(parts[m], m) for m in range(1, 4)]
    return call(
        sum_last_kernel, [sds(parts[0].shape[1:], F32)] * 2, (where, parts[0], *came), name="sum_last"
    )


def after(value, *others):
    return lax.optimization_barrier((value, *others))[0]


def gather(shard):
    return lax.all_gather(
        lax.all_gather(shard, "tensor", axis=1, tiled=True), "dp", axis=0, tiled=True
    )


def scatter(grad):
    part = lax.psum_scatter(grad, "dp", scatter_dimension=0, tiled=True)
    return lax.psum_scatter(part, "tensor", scatter_dimension=1, tiled=True).astype(F32)


def make_shards(mesh):
    size = mesh.shape["tensor"]
    blocked = size == 4 and mesh.shape["dp"] == 8

    def shards(
        tokens, segments, cotangent, norm_gain, w_gate, w_inner, w_step, w_state, conv_inner, conv_state,
        step_bias, decay_log, skip_gain, out_gain, w_out,
    ):
        count, width = tokens.shape
        place = lax.axis_index("tensor")
        blocks = count // BLOCK
        inner = w_inner.shape[1] * size
        heads = w_step.shape[1] * size

        halo = lax.ppermute(tokens[count - HALO :], "tensor", line(1, size))
        tok = jnp.concatenate([halo, tokens], axis=0)
        wide_tok = tok.astype(F32)
        gain = norm_gain.astype(F32)
        rms = lax.rsqrt(jnp.mean(wide_tok * wide_tok, axis=1, keepdims=True) + EPS)
        normed = (wide_tok * rms * gain).astype(BF)

        padded = jnp.concatenate([jnp.full((HALO,), -1, jnp.int32), segments])
        near = lax.dynamic_slice(padded, (place * count,), (HALO + count,))
        seg = near[HALO:]
        masks = [near[HALO - k : HALO - k + count] == seg for k in range(1, KW)]
        grid = seg.reshape(blocks, BLOCK)
        prev = near[HALO - 1 : HALO - 1 + count].reshape(blocks, BLOCK)[:, :1]
        from_prev = (grid == prev).reshape(-1)
        at_last = (grid == grid[:, BLOCK - 1 :]).reshape(-1)
        cols = jnp.stack([*masks, from_prev, at_last], axis=1).astype(F32)
        seg_col = seg.astype(F32)[:, None]
        seg_row = seg.astype(F32)[None]

        def pad_heads(row):
            return jnp.pad(row, ((0, 0), (0, LANES - heads)))

        where = jnp.stack([lax.axis_index("dp"), place]).astype(jnp.int32)
        depth, span = w_inner.shape
        per = heads // size
        if blocked:
            tall = HALO + depth

            def place_at(block, row, lane):
                rows = (row, tall - row - block.shape[0])
                return jnp.pad(block, (rows, (lane, span + LANES - lane - block.shape[1])))

            pack = place_at(w_inner, 0, 0) + place_at(w_step, 0, span)
            pack = pack + place_at(conv_inner, depth, 0) + place_at(out_gain[None], depth + KW + 1, 0)
            for n, row in enumerate((step_bias, decay_log, skip_gain)):
                pack = pack + place_at(row[None], depth + KW + 2, n * per)
            came = ring(pack)
            came_out = ring(after(jnp.stack([w_gate, w_out]), *came[1:]))

            column, taps, par, wide = call(
                unpack_kernel,
                [
                    sds((5, depth, span), BF),
                    sds((8, inner), F32),
                    sds((8, LANES), F32),
                    sds((8, inner), F32),
                ],
                (where, *came, w_state),
                name="unpack",
            )
            pieces = gather_pieces(column, came_out[1:])
            pieces_out = gather_pieces(after(jnp.stack(came_out), *pieces[1:4]))
        else:
            conv_whole, head_whole, gain_whole = [
                lax.all_gather(v, "tensor", axis=v.ndim - 1, tiled=True).astype(F32)
                for v in (conv_inner, jnp.stack([step_bias, decay_log, skip_gain]), out_gain)
            ]
            pieces = [gather(w_inner), lax.all_gather(w_state, "dp", axis=0, tiled=True), pad_heads(gather(w_step))]
            pieces_out = [gather(w_gate), gather(w_out)]
            taps = jnp.pad(conv_whole, ((0, 8 - KW - 1), (0, 0)))
            bias, rate, skip = head_whole[0], -jnp.exp(head_whole[1]), head_whole[2]
            par = pad_heads(jnp.pad(jnp.stack([bias, rate]), ((0, 6), (0, 0))))
            wide = jnp.pad(jnp.stack([gain_whole, jnp.repeat(skip, HEAD_DIM)]), ((0, 6), (0, 0)))
        taps_state = jnp.pad(conv_state.astype(F32), ((0, 8 - KW - 1), (0, 0)))
        in_scratch = [
            pltpu.VMEM((width, inner), BF),
            pltpu.VMEM((width, 2 * STATE), BF),
            pltpu.VMEM((width, LANES), BF),
            pltpu.SemaphoreType.DMA((3,)),
        ]
        out_scratch = [
            pltpu.VMEM((width, inner), BF),
            pltpu.VMEM((width, inner), BF),
            pltpu.SemaphoreType.DMA((2,)),
        ]

        def last_args(fixed, arrays):
            return {"args": (where, *fixed, *arrays), "far": range(1 + len(fixed), 1 + len(fixed) + len(arrays))}

        pre, conv, spre, sconv, rw, st, keep, c_ref, pay = call(
            project_kernel,
            [
                sds((HALO + count, inner), BF),
                sds((count, inner), F32),
                sds((HALO + count, 2 * STATE), F32),
                sds((count, 2 * STATE), F32),
                sds((count, 2 * STATE), BF),
                sds((5, count, LANES), F32),
                sds((8, LANES), F32),
                sds((max(1, blocks - 1), STATE, inner), F32),
                sds((STATE + HALO, inner), BF),
            ],
            scratch=in_scratch,
            **last_args((normed, taps, taps_state, par, cols), pieces),
            name="project",
            micros=9.5,
        )
        y = call(
            scan_kernel,
            [sds((count, inner), F32)],
            (where, conv, st, rw, seg_col, seg_row),
            [pltpu.VMEM((BLOCK, BLOCK), F32), pltpu.VMEM((LANES, BLOCK), F32)],
            name="scan",
            micros=10,
        )[0]
        *enter, sent = pass_states(pay, pass_first(pay, size, 1), size, 1, (y,))
        gate, gout = call(
            gate_kernel,
            [sds((count, inner), F32)] * 2,
            scratch=out_scratch,
            **last_args((after(normed, sent), cotangent), pieces_out),
            name="gate",
            micros=6,
        )
        out_low, ggate, gscan, rowside, gread_a, states, d_ref, pay, sums = call(
            output_kernel,
            [
                sds((count, inner), BF),
                sds((count, inner), BF),
                sds((count, inner), BF),
                sds((count, LANES), F32),
                sds((count, STATE), F32),
                sds((blocks, STATE, inner), BF),
                sds((max(1, blocks - 1), STATE, inner), F32),
                sds((STATE + HALO, inner), BF),
                sds((8, inner), F32),
            ],
            (where, *enter, c_ref, keep, gate, gout, y, conv, rw, st, wide),
            [pltpu.VMEM((ROWS, inner), F32), pltpu.VMEM((blocks, STATE, inner), F32)],
            name="output",
            micros=9.5,
        )
        if blocked:
            shapes_out = [sds((4, 4, 2, depth, span), BF)] * 2
            shapes_in = [sds((4, 5, depth, span), BF)] * 2
        else:
            shapes_out = [sds((width, inner), BF)] * 2
            shapes_in = [sds((width, inner), BF), sds((width, 2 * STATE), BF), sds((width, LANES), BF)]
        mixed, gn_gate, *grads_out = call(
            gate_grad_kernel,
            [sds((count, width), BF), sds((count, width), F32), *shapes_out],
            far_outs=(2, 3),
            scratch=[
                pltpu.VMEM((width, inner), BF),
                pltpu.VMEM((width, inner), BF),
                *out_scratch,
            ],
            **last_args((normed, cotangent, out_low, ggate, tok), pieces_out),
            name="gate_grad",
            micros=8.3,
        )
        came_pay = pass_first(pay, size, -1)
        if blocked:
            mine_out, other_out = grads_out
            parts_out = reduce_core(where, mine_out, after(other_out, came_pay))
        else:
            parts_out = ()
        *leave, sent = pass_states(pay, came_pay, size, -1)
        by_block = [
            call(
                functools.partial(scan_grad_kernel, b),
                [sds((BLOCK, inner), F32), sds((BLOCK, LANES), F32), *[sds((BLOCK, STATE), F32)] * 2],
                (where, after(gscan, sent, *parts_out), conv, st, rw, seg_col, seg_row),
                [
                    pltpu.VMEM((BLOCK, BLOCK), F32),
                    pltpu.VMEM((BLOCK, BLOCK), F32),
                    pltpu.VMEM((LANES, BLOCK), F32),
                ],
                name=f"scan_grad_{b}",
                micros=9,
            )
            for b in range(blocks)
        ]
        low_inner, low_state, low_step, sums_in, sums_state, sums_head = call(
            input_grad_kernel,
            [
                sds((HALO + count, inner), BF),
                sds((HALO + count, 2 * STATE), BF),
                sds((HALO + count, LANES), BF),
                sds((8, inner), F32),
                sds((8, 2 * STATE), F32),
                sds((8, LANES), F32),
            ],
            (
                where, *leave, d_ref, keep, states, conv, pre, gscan, st, rw, sconv, spre, rowside, gread_a, taps,
                taps_state, par, wide, cols, *[v for part in by_block for v in part],
            ),
            [pltpu.VMEM((blocks, STATE, inner), BF)],
            name="input_grad",
            micros=9,
        )
        low_next = low_inner
        if blocked:
            lines_out = reduce_plane(where, parts_out)
            low_next = after(low_inner, *lines_out)
        grads_in = call(
            weight_grad_kernel,
            shapes_in,
            (where, normed, low_next, low_state, low_step),
            scratch=in_scratch,
            far_outs=range(len(shapes_in)),
            name="weight_grad",
            micros=5,
        )
        if blocked:
            grad_gate, grad_out = reduce_line(where, lines_out)
            mine_in, other_in = grads_in
            parts_in = reduce_core(where, mine_in, other_in)
            low_inner = after(low_inner, other_in)
        grad, back, pack = call(
            token_grad_kernel,
            [sds((count, width), F32), sds((HALO, width), F32), sds((8, inner), F32)],
            scratch=in_scratch,
            **last_args((low_inner, low_state, low_step, gn_gate, tok, cotangent, gain[None], sums_in, sums, sums_state, sums_head), pieces),
            name="token_grad",
            micros=5,
        )
        if blocked:
            back = after(back, *parts_in)
            pack = after(pack, *parts_in)
        back = lax.ppermute(back, "tensor", line(-1, size))
        grad = grad.at[count - HALO :].add(back)

        if blocked:
            grad_inner, last = reduce_line(where, reduce_plane(where, parts_in))
            grad_state = last[:, : 2 * STATE]
            grad_step = lax.dynamic_slice(last, (0, 2 * STATE + place * per), (depth, per))
            pack = pack + swap(pack, 1)
            pack = pack + swap(pack, 2) + swap(pack, 4) + swap(pack, 6)
            own, norm, state, head = call(
                finish_kernel,
                [sds((8, span), F32), sds((1, width), F32), sds((8, 2 * STATE), F32), sds((8, LANES), F32)],
                (where, pack, turn(pack, 1), turn(pack, 2), turn(pack, 3)),
                [pltpu.VMEM((8, inner), F32)],
                name="finish",
            )
            norm = norm[0]
            head_grads = [head[n, :per] for n in range(3)]
        else:
            pack = lax.psum(pack, ("dp", "tensor"))
            own = lax.dynamic_slice(pack, (0, place * span), (KW + 2, span))
            norm = pack[KW + 2, :width]
            state = pack[KW + 3, : (KW + 1) * 2 * STATE].reshape(KW + 1, 2 * STATE)
            head_grads = [
                lax.dynamic_slice(pack[KW + 2], (width + LANES * n + place * per,), (per,)) for n in range(3)
            ]
            grad_gate, grad_out, grad_inner, grad_step = [
                scatter(v) for v in (*grads_out, grads_in[0], grads_in[2][:, :heads])
            ]
            grad_state = lax.psum_scatter(grads_in[1], "dp", scatter_dimension=0, tiled=True)
            grad_state = lax.psum(grad_state, "tensor").astype(F32)
        return (
            mixed,
            grad,
            norm,
            grad_gate,
            grad_inner,
            grad_step,
            grad_state,
            own[: KW + 1],
            state[: KW + 1],
            *head_grads,
            own[KW + 1],
            grad_out,
        )

    return shards


def solution(mesh):
    in_specs = (
        P(("dp", "tensor"), None),
        P("dp"),
        P(("dp", "tensor"), None),
        P(),
        P("dp", "tensor"),
        P("dp", "tensor"),
        P("dp", "tensor"),
        P("dp", None),
        P(None, "tensor"),
        P(),
        P("tensor"),
        P("tensor"),
        P("tensor"),
        P("tensor"),
        P("dp", "tensor"),
    )
    out_specs = (
        P(("dp", "tensor"), None),
        P(("dp", "tensor"), None),
        P(),
        P("dp", "tensor"),
        P("dp", "tensor"),
        P("dp", "tensor"),
        P("dp", None),
        P(None, "tensor"),
        P(),
        P("tensor"),
        P("tensor"),
        P("tensor"),
        P("tensor"),
        P("dp", "tensor"),
    )
    return jax.shard_map(
        make_shards(mesh), mesh=mesh, in_specs=in_specs, out_specs=out_specs, check_vma=False
    )
```

```python
import functools
import math

import jax
import jax.numpy as jnp
from jax import lax
from jax.experimental import pallas as pl
from jax.experimental.pallas import tpu as pltpu
from jax.sharding import PartitionSpec as P

HEAD_DIM = 64
STATE = 128
KW = 4
BLOCK = 256
HALO = 16
LANES = 128
TILE = 256
ROWS = 128
EPS = 1e-05
F32 = jnp.float32
BF = jnp.bfloat16
HIGH = lax.Precision.HIGHEST
SPARE = 3 * 2**20
ORDER = (0, 2, 4, 6, 1, 3, 5, 7)


def dot(a, b):
    return lax.dot_general(a, b, (((1,), (0,)), ((), ())), preferred_element_type=F32)


def dot_nt(a, b):
    return lax.dot_general(a, b, (((1,), (1,)), ((), ())), preferred_element_type=F32)


def dot_tn(a, b):
    return lax.dot_general(a, b, (((0,), (0,)), ((), ())), preferred_element_type=F32)


def dot_high(a, b):
    return lax.dot_general(
        a, b, (((1,), (0,)), ((), ())), precision=HIGH, preferred_element_type=F32
    )


def sigmoid(x):
    return 0.5 * jnp.tanh(0.5 * x) + 0.5


def expand(x, first, count):
    lane = lax.broadcasted_iota(jnp.int32, (x.shape[0], LANES), 1)
    return jnp.concatenate(
        [
            jnp.where(lane < HEAD_DIM, x[:, h : h + 1], x[:, h + 1 : h + 2])
            for h in range(first, first + count, 2)
        ],
        axis=1,
    )


def head_matrix(first, channels):
    channel = lax.broadcasted_iota(jnp.int32, (channels, LANES), 0)
    head = lax.broadcasted_iota(jnp.int32, (channels, LANES), 1)
    return (channel // HEAD_DIM + first == head).astype(BF)


def head_sum(x, matrix):
    hi = x.astype(BF)
    lo = (x - hi.astype(F32)).astype(BF)
    return dot(hi, matrix) + dot(lo, matrix)


def lower_matrix():
    i = lax.broadcasted_iota(jnp.int32, (BLOCK, BLOCK), 0)
    j = lax.broadcasted_iota(jnp.int32, (BLOCK, BLOCK), 1)
    return i, j


def conv_forward(values, taps, cols):
    result = taps[KW : KW + 1] + taps[0:1] * values[HALO:]
    for k in range(1, KW):
        result = result + taps[k : k + 1] * pltpu.roll(values, k, 0)[HALO:] * cols[:, k - 1 : k]
    return result


def conv_backward(grad, values, taps, cols):
    width = grad.shape[1]
    whole = HALO + grad.shape[0]
    zero = jnp.zeros((HALO, width), F32)
    base = jnp.concatenate([zero, grad], axis=0)
    result = taps[0:1] * base
    sums = [jnp.sum(grad * values[HALO:], axis=0, keepdims=True)]
    for k in range(1, KW):
        masked = jnp.concatenate([zero, grad * cols[:, k - 1 : k]], axis=0)
        back = pltpu.roll(masked, whole - k, 0)
        result = result + taps[k : k + 1] * back
        sums.append(jnp.sum(back * values, axis=0, keepdims=True))
    sums.append(jnp.sum(grad, axis=0, keepdims=True))
    return result, sums


def put_rows(rows, width):
    index = lax.broadcasted_iota(jnp.int32, (8, width), 0)
    result = jnp.zeros((8, width), F32)
    for i, row in enumerate(rows):
        result = jnp.where(index == i, row, result)
    return result


def call(kernel, outs, args, scratch=(), name=None, micros=1.0, far=(), far_outs=()):
    size = 1 << 20

    held = [a for i, a in enumerate(args) if i > 0 and i not in far]
    held += [o for i, o in enumerate(outs) if i not in far_outs]
    limit = SPARE + sum(a.size * a.dtype.itemsize for a in held)
    for item in scratch:
        if len(item.shape) > 1:
            limit += math.prod(item.shape) * jnp.dtype(item.dtype).itemsize

    def spec(space):
        return pl.BlockSpec(memory_space=space)

    ins = [
        spec(pltpu.SMEM if i == 0 else pltpu.HBM if i in far else pltpu.VMEM) for i in range(len(args))
    ]
    return pl.pallas_call(
        kernel,
        out_shape=outs,
        in_specs=ins,
        out_specs=[spec(pl.ANY if i in far_outs else pltpu.VMEM) for i in range(len(outs))],
        scratch_shapes=list(scratch),
        compiler_params=pltpu.CompilerParams(vmem_limit_bytes=limit),
        cost_estimate=pl.CostEstimate(flops=int(micros * 1.15e9), bytes_accessed=size, transcendentals=0),
        name=name,
    )(*args)


def sds(shape, dtype):
    return jax.ShapeDtypeStruct(shape, dtype)


def aligned(value, size):
    return pl.multiple_of(value * size, size)


def load_weights(place, refs, targets, sems):
    if len(refs[0].shape) == 2:
        copies = [pltpu.make_async_copy(r, t, sems.at[n]) for n, (r, t) in enumerate(zip(refs, targets))]
        for copy in copies:
            copy.start()
        return
    split = refs[0].shape[0] == 5
    depth, span = refs[0].shape[-2:]
    for n, k in enumerate(ORDER):
        row = pl.ds(aligned(place[0] ^ k, depth), depth)
        for m in range(4):
            who = (place[1] + m) % 4 if split else place[1] ^ m
            column = pl.ds(aligned(who, span), span)
            for g in range(1 if split else 2):
                source = refs[n].at[m] if split else refs[n].at[m, g]
                pltpu.make_async_copy(source, targets[g].at[row, column], sems.at[g]).start()
        if split:
            wide = targets[1].shape[1]
            pltpu.make_async_copy(refs[n].at[4, :, :wide], targets[1].at[row, :], sems.at[1]).start()
            pltpu.make_async_copy(refs[n].at[4, :, wide:], targets[2].at[row, :], sems.at[2]).start()


def wait_weights(targets, sems):
    for n, target in enumerate(targets):
        pltpu.make_async_copy(target, target, sems.at[n]).wait()


def store_grads(place, sources, outs, sems):
    if len(outs[0].shape) == 2:
        copies = [pltpu.make_async_copy(s, o, sems.at[n]) for n, (s, o) in enumerate(zip(sources, outs))]
        for copy in copies:
            copy.start()
    else:
        split = outs[0].shape[1] == 5
        depth, span = outs[0].shape[-2:]
        for n, k in enumerate(ORDER):
            out = outs[n // 4].at[n % 4]
            sem = sems.at[n // 4]
            row = pl.ds(aligned(place[0] ^ k, depth), depth)
            for m in range(4):
                column = pl.ds(aligned((place[1] + m) % 4, span), span)
                for g in range(1 if split else 2):
                    target = out.at[m] if split else out.at[m, g]
                    pltpu.make_async_copy(sources[g].at[row, column], target, sem).start()
            if split:
                wide = sources[1].shape[1]
                pltpu.make_async_copy(sources[1].at[row, :], out.at[4, :, :wide], sem).start()
                pltpu.make_async_copy(sources[2].at[row, :], out.at[4, :, wide:], sem).start()
    for n, out in enumerate(outs):
        pltpu.make_async_copy(out, out, sems.at[n]).wait()


def unpack_kernel(place, *refs):
    parts, (state, column, taps, par, wide) = refs[:4], refs[4:]
    depth, span = column.shape[1:]
    per = span // HEAD_DIM
    heads = wide.shape[1] // HEAD_DIM
    lane = lax.broadcasted_iota(jnp.int32, (8, LANES), 1)
    step = jnp.zeros((LANES, LANES), F32)
    rows = [jnp.zeros((8, LANES), F32)] * 3
    for m, part in enumerate(parts):
        who = (place[1] + m) % 4
        lanes = pl.ds(aligned(who, span), span)
        column[m] = part[:depth, :]
        low = part[depth:, :].astype(F32)
        tall = jnp.concatenate([low[:, :LANES], jnp.zeros((LANES - HALO, LANES), F32)], axis=0)
        tall = pltpu.roll(tall, LANES - KW - 3, 0)
        tall = jnp.where(lax.broadcasted_iota(jnp.int32, (LANES, LANES), 0) < per, tall, 0.0)
        step = step + pltpu.roll(tall, who * per, 0)
        taps[:, lanes] = low[:8]
        wide[0:1, lanes] = low[KW + 1 : KW + 2]
        row = jnp.broadcast_to(low[KW + 2 : KW + 3, :LANES], (8, LANES))
        for n in range(3):
            own = pltpu.roll(row, LANES - n * per, 1) if n else row
            rows[n] = rows[n] + pltpu.roll(jnp.where(lane < per, own, 0.0), who * per, 1)
    column[4] = jnp.concatenate([state[...], step.T[:depth].astype(BF)], axis=1)
    par[...] = put_rows([rows[0][0:1], jnp.where(lane < heads, -jnp.exp(rows[1]), 0.0)[0:1]], LANES)
    wide[1:2, :] = expand(rows[2], 0, heads)[0:1]


def project_kernel(
    place, *refs
):
    (normed, taps, taps_state, par, cols), refs = refs[:5], refs[5:]
    weights, refs = refs[:-13], refs[-13:]
    pre, conv, spre, sconv, rw, st, keep, c_ref, pay, win, wst, wsp, sems = refs
    load_weights(place, weights, (win, wst, wsp), sems)
    wait_weights((win, wst, wsp), sems)
    project(normed, win, wst, wsp, taps, taps_state, par, cols, pre, conv, spre, sconv, rw, st, keep, c_ref, pay)


def project(
    normed, win, wst, wsp, taps, taps_state, par, cols, pre, conv, spre, sconv, rw, st, keep, c_ref, pay
):
    tokens = conv.shape[0]
    inner = conv.shape[1]
    blocks = tokens // BLOCK
    x = normed[...]
    low = x[HALO:]
    col = cols[...]
    sp = dot(low, wsp[...]) + par[0:1]
    step = jnp.maximum(sp, 0.0) + jnp.log1p(jnp.exp(-jnp.abs(sp)))
    decay = step * par[1:2]
    i, j = lower_matrix()
    lower = (i >= j).astype(F32)
    st[0] = sp
    st[1] = step
    keeps = []
    outs = []
    for b in range(blocks):
        rows = slice(b * BLOCK, (b + 1) * BLOCK)
        cum = dot_high(lower, decay[rows])
        last = cum[BLOCK - 1 : BLOCK]
        from_prev = col[rows, 3:4]
        out = jnp.exp(last - cum) * col[rows, 4:5]
        st[2, rows] = cum
        st[3, rows] = out
        st[4, rows] = jnp.exp(cum) * from_prev
        keeps.append(jnp.exp(last) * from_prev[BLOCK - 1 : BLOCK])
        outs.append(out * step[rows])
    keep[...] = put_rows(keeps, LANES)
    whole = keeps[0]
    for b in range(1, blocks):
        whole = whole * keeps[b]
    state = dot(x, wst[...])
    spre[...] = state
    sc = conv_forward(state, taps_state, col)
    sconv[...] = sc
    rw[...] = (sc * sigmoid(sc)).astype(BF)
    entry = rw[:, :STATE]
    index = lax.broadcasted_iota(jnp.int32, (HALO, TILE), 0)
    for tile in range(inner // TILE):
        lanes = slice(tile * TILE, (tile + 1) * TILE)
        heads = TILE // HEAD_DIM
        first = tile * heads
        value = dot(x, win[:, lanes])
        pre[:, lanes] = value.astype(BF)
        c = conv_forward(value, taps[:, lanes], col)
        conv[:, lanes] = c
        c = c.astype(F32)
        act = (c * sigmoid(c)).astype(BF).astype(F32)
        total = None
        for b in range(blocks):
            rows = slice(b * BLOCK, (b + 1) * BLOCK)
            scaled = (act[rows] * expand(outs[b], first, heads)).astype(BF)
            part = dot_tn(entry[rows], scaled)
            if b < blocks - 1:
                c_ref[b, :, lanes] = part
            total = part if b == 0 else total * expand(keeps[b], first, heads) + part
        pay[:STATE, lanes] = total.astype(BF)
        wide = expand(whole, first, heads)
        hi = wide.astype(BF).astype(F32)
        pay[STATE:, lanes] = jnp.where(index == 0, hi, jnp.where(index == 1, wide - hi, 0.0)).astype(BF)


def gate_kernel(place, normed, cot, *refs):
    weights, (gate, gout, wg, wo, sems) = refs[:-5], refs[-5:]
    load_weights(place, weights, (wg, wo), sems)
    wait_weights((wg, wo), sems)
    for tile in range(gate.shape[1] // TILE):
        lanes = slice(tile * TILE, (tile + 1) * TILE)
        gate[:, lanes] = dot(normed[HALO:, :], wg[:, lanes])
        gout[:, lanes] = dot(cot[...], wo[:, lanes])


def scan_kernel(place, conv, st, rw, seg_col, seg_row, y, smask, cum_t):
    tokens, inner = conv.shape
    blocks = tokens // BLOCK
    half = BLOCK // 2
    i, j = lower_matrix()
    lane = lax.broadcasted_iota(jnp.int32, (BLOCK, LANES), 1)
    for b in range(blocks):
        rows = slice(b * BLOCK, (b + 1) * BLOCK)
        scores = dot_nt(rw[rows, STATE:], rw[rows, :STATE])
        same = (i >= j) & (seg_col[rows, 0:1] == seg_row[0:1, rows])
        smask[...] = jnp.where(same, scores, 0.0)
        cum_t[...] = st[2, rows].T

        def pair(p, carry):
            cum = pltpu.roll(st[2, rows], LANES - 2 * p, 1)
            step = pltpu.roll(st[1, rows], LANES - 2 * p, 1)
            lanes = pl.ds(pl.multiple_of(p * LANES, LANES), LANES)
            c = conv[rows, lanes].astype(F32)
            act = (c * sigmoid(c)).astype(BF).astype(F32)
            xs = (act * jnp.where(lane < HEAD_DIM, step[:, 0:1], step[:, 1:2])).astype(BF)
            top = jnp.zeros((half, LANES), F32)
            bottom = jnp.zeros((half, LANES), F32)
            for a in range(2):
                mine = jnp.where((lane < HEAD_DIM) == (a == 0), xs, jnp.zeros_like(xs))
                row = cum_t[pl.ds(2 * p + a, 1), :]
                e = jnp.exp(jnp.minimum(cum[:half, a : a + 1] - row[:, :half], 0.0))
                top = top + dot((smask[:half, :half] * e).astype(BF), mine[:half])
                e = jnp.exp(jnp.minimum(cum[half:, a : a + 1] - row, 0.0))
                bottom = bottom + dot((smask[half:, :] * e).astype(BF), mine)
            y[b * BLOCK : b * BLOCK + half, lanes] = top
            y[b * BLOCK + half : (b + 1) * BLOCK, lanes] = bottom
            return carry

        lax.fori_loop(0, inner // LANES, pair, 0, unroll=6)


def output_kernel(
    place, near, far, c_ref, keep, gate, gout, y, conv, rw, st, wide, out_low, ggate, gscan, rowside, gread, states,
    d_ref, pay, sums, so_ref, d_all
):
    tokens, inner = conv.shape
    blocks = tokens // BLOCK
    tiles = inner // TILE
    heads = TILE // HEAD_DIM
    now = None
    for b in range(blocks):
        now = entering(near, far) if b == 0 else now * expand(keep[b - 1 : b], 0, inner // HEAD_DIM) + c_ref[b - 1]
        states[b] = now.astype(BF)
    sums[...] = jnp.zeros_like(sums)
    d_all[...] = jnp.zeros_like(d_all)

    def chunk(r, carry):
        rows = pl.ds(pl.multiple_of(r * ROWS, ROWS), ROWS)
        b = r // (BLOCK // ROWS)
        read = rw[rows, STATE:]
        scale = st[4, rows, :]
        total = jnp.zeros((ROWS, 1), F32)
        cross = jnp.zeros((ROWS, 1), F32)
        for tile in range(tiles):
            lanes = slice(tile * TILE, (tile + 1) * TILE)
            raw = dot(read, states[b, :, lanes])
            so = y[rows, lanes] + raw * expand(scale, tile * heads, heads)
            so_ref[:, lanes] = so
            c = conv[rows, lanes].astype(F32)
            u = so + wide[1:2, lanes] * (c * sigmoid(c))
            g = gate[rows, lanes].astype(F32)
            gated = u * (g * sigmoid(g))
            total = total + jnp.sum(gated * gated, axis=1, keepdims=True)
            go = gout[rows, lanes].astype(F32) * wide[0:1, lanes]
            cross = cross + jnp.sum(go * gated, axis=1, keepdims=True)
        rms = lax.rsqrt(total / inner + EPS)
        cube = rms * rms * rms * (cross / inner)
        side = jnp.zeros((ROWS, LANES), F32)
        read_grad = jnp.zeros((ROWS, STATE), F32)
        for tile in range(tiles):
            lanes = slice(tile * TILE, (tile + 1) * TILE)
            so = so_ref[:, lanes]
            c = conv[rows, lanes].astype(F32)
            act = c * sigmoid(c)
            u = so + wide[1:2, lanes] * act
            g = gate[rows, lanes].astype(F32)
            sg = sigmoid(g)
            silu = g * sg
            gated = u * silu
            gain = wide[0:1, lanes]
            out = gated * rms
            out_low[rows, lanes] = (out * gain).astype(BF)
            go = gout[rows, lanes].astype(F32)
            gg = go * gain * rms - gated * cube
            q = gg * silu
            ggate[rows, lanes] = (gg * u * (sg * (1.0 + g * (1.0 - sg)))).astype(BF)
            low = q.astype(BF)
            gscan[rows, lanes] = low
            low = low.astype(F32)
            sums[0:1, lanes] += jnp.sum(go * out, axis=0, keepdims=True)
            sums[1:2, lanes] += jnp.sum(q * act, axis=0, keepdims=True)
            side = side + head_sum(low * so, head_matrix(tile * heads, TILE))
            scaled = (low * expand(scale, tile * heads, heads)).astype(BF)
            d_all[b, :, lanes] += dot_tn(read, scaled)
            read_grad = read_grad + dot_nt(scaled, states[b, :, lanes])
        rowside[rows, :] = side
        gread[rows, :] = read_grad
        return carry

    lax.fori_loop(0, tokens // ROWS, chunk, 0)
    for b in range(1, blocks):
        d_ref[b - 1] = d_all[b]
    total = d_all[blocks - 1]
    whole = keep[blocks - 1 : blocks]
    for b in range(blocks - 2, -1, -1):
        total = d_all[b] + expand(keep[b : b + 1], 0, inner // HEAD_DIM) * total
        whole = whole * keep[b : b + 1]
    pay[:STATE] = total.astype(BF)
    index = lax.broadcasted_iota(jnp.int32, (HALO, inner), 0)
    wide_keep = expand(whole, 0, inner // HEAD_DIM)
    hi = wide_keep.astype(BF).astype(F32)
    pay[STATE:] = jnp.where(index == 0, hi, jnp.where(index == 1, wide_keep - hi, 0.0)).astype(BF)


def gate_grad_kernel(place, normed, cot, out_low, ggate, tok, *refs):
    (mixed, gn), refs = refs[-9:-7], refs[:-9] + refs[-7:]
    weights, (out_a, out_b, gwg, gwo, wg, wo, sems) = refs[:-7], refs[-7:]
    load_weights(place, weights, (wg, wo), sems)
    inner = out_low.shape[1]
    low = normed[HALO:, :]
    for tile in range(inner // TILE):
        lanes = slice(tile * TILE, (tile + 1) * TILE)
        gwo[:, lanes] = dot_tn(cot[...], out_low[:, lanes]).astype(BF)
        gwg[:, lanes] = dot_tn(low, ggate[:, lanes]).astype(BF)
    wait_weights((wg, wo), sems)
    gn[...] = dot_nt(ggate[...], wg[...])
    mixed[...] = (tok[HALO:, :].astype(F32) + dot_nt(out_low[...], wo[...])).astype(BF)
    store_grads(place, (gwg, gwo), (out_a, out_b), sems)


def scan_grad_kernel(b, place, gscan, conv, st, rw, seg_col, seg_row, z, colside, gentry, gread, smask, acc, cum_t):
    inner = conv.shape[1]
    half = BLOCK // 2
    j, i = lower_matrix()
    lane = lax.broadcasted_iota(jnp.int32, (BLOCK, LANES), 1)
    rows = slice(b * BLOCK, (b + 1) * BLOCK)
    same = (i >= j) & (seg_col[rows, 0:1] == seg_row[0:1, rows])
    scores = dot_nt(rw[rows, :STATE], rw[rows, STATE:])
    smask[...] = jnp.where(same, scores, 0.0)
    cum_t[...] = st[2, rows].T
    acc[...] = jnp.zeros_like(acc)
    colside[...] = jnp.zeros((BLOCK, LANES), F32)

    def pair(p, carry):
        cum = pltpu.roll(st[2, rows], LANES - 2 * p, 1)
        step = pltpu.roll(st[1, rows], LANES - 2 * p, 1)
        lanes = pl.ds(pl.multiple_of(p * LANES, LANES), LANES)
        c = conv[rows, lanes].astype(F32)
        act = (c * sigmoid(c)).astype(BF).astype(F32)
        xs = (act * jnp.where(lane < HEAD_DIM, step[:, 0:1], step[:, 1:2])).astype(BF)
        gs = gscan[rows, lanes]
        gs_t = gs.T
        top = jnp.zeros((half, LANES), F32)
        bottom = jnp.zeros((half, LANES), F32)
        for a in range(2):
            keep = (lane < HEAD_DIM) == (a == 0)
            mine = jnp.where(keep, xs, jnp.zeros_like(xs))
            grad = jnp.where(keep, gs, jnp.zeros_like(gs))
            row = cum_t[pl.ds(2 * p + a, 1), :]
            e = jnp.exp(jnp.minimum(row - cum[:half, a : a + 1], 0.0))
            top = top + dot((smask[:half, :] * e).astype(BF), grad)
            acc[:half, :] += dot(mine[:half], gs_t) * e
            e = jnp.exp(jnp.minimum(row[:, half:] - cum[half:, a : a + 1], 0.0))
            bottom = bottom + dot((smask[half:, half:] * e).astype(BF), grad[half:])
            acc[half:, half:] += dot(mine[half:], gs_t[:, half:]) * e
        both = jnp.concatenate([top, bottom], axis=0)
        z[:, lanes] = both
        channel = lax.broadcasted_iota(jnp.int32, (LANES, LANES), 0)
        head = lax.broadcasted_iota(jnp.int32, (LANES, LANES), 1)
        matrix = (channel // HEAD_DIM + 2 * p == head).astype(BF)
        colside[...] += head_sum(both * xs.astype(F32), matrix)
        return carry

    lax.fori_loop(0, inner // LANES, pair, 0, unroll=6)
    low = jnp.where(same, acc[...], 0.0).astype(BF)
    gentry[...] = dot(low, rw[rows, STATE:])
    gread[...] = dot_tn(low, rw[rows, :STATE])


def input_grad_kernel(
    place, near, far, d_ref, keep, states, conv, pre, gscan, st, rw, sconv, spre, rowside, gread_a, taps,
    taps_state, par, wide, cols, *refs
):
    by_block, (low_inner, low_state, low_step, sums, sums_state, sums_head, gstates) = refs[:-7], refs[-7:]
    z, colside, gentry, gread_b = [
        jnp.concatenate([ref[...] for ref in by_block[n::4]], axis=0) if n else by_block[n::4] for n in range(4)
    ]
    tokens, inner = conv.shape
    blocks = tokens // BLOCK
    tiles = inner // TILE
    heads = TILE // HEAD_DIM
    col = cols[...]
    now = entering(near, far)
    keep_grads = [None] * blocks
    whole_matrix = head_matrix(0, inner)
    for b in range(blocks - 1, -1, -1):
        gstates[b] = now.astype(BF)
        sum_row = jnp.sum(now * states[b].astype(F32), axis=0, keepdims=True)
        keep_grads[b] = head_sum(jnp.broadcast_to(sum_row, (8, inner)), whole_matrix)[0:1]
        if b > 0:
            now = d_ref[b - 1] + expand(keep[b : b + 1], 0, inner // HEAD_DIM) * now
    step_grad = jnp.zeros((tokens, LANES), F32)
    out_side = jnp.zeros((tokens, LANES), F32)
    entry_grad = gentry
    for tile in range(tiles):
        lanes = slice(tile * TILE, (tile + 1) * TILE)
        first = tile * heads
        matrix = head_matrix(first, TILE)
        c = conv[:, lanes].astype(F32)
        sg = sigmoid(c)
        act = (c * sg).astype(BF).astype(F32)
        step = expand(st[1], first, heads)
        out = expand(st[3], first, heads)
        scaled = (act * (step * out)).astype(BF)
        grads = []
        entries = []
        for b in range(blocks):
            rows = slice(b * BLOCK, (b + 1) * BLOCK)
            grads.append(dot(rw[rows, :STATE], gstates[b, :, lanes]))
            entries.append(dot_nt(scaled[rows], gstates[b, :, lanes]))
        grad_scaled = jnp.concatenate(grads, axis=0)
        entry_grad = entry_grad + jnp.concatenate(entries, axis=0)
        w = jnp.concatenate([ref[:, lanes] for ref in z], axis=0) + out * grad_scaled
        step_grad = step_grad + head_sum(act * w, matrix)
        out_side = out_side + head_sum(scaled.astype(F32) * grad_scaled, matrix)
        grad = wide[1:2, lanes] * gscan[:, lanes].astype(F32) + step * w
        grad = grad * (sg * (1.0 + c * (1.0 - sg)))
        back, rows_sum = conv_backward(grad, pre[:, lanes].astype(F32), taps[:, lanes], col)
        low = back.astype(BF)
        low_inner[:, lanes] = low
        sums[:, lanes] = put_rows(rows_sum, TILE)
    sc = sconv[...]
    sg = sigmoid(sc)
    grad = jnp.concatenate([entry_grad, gread_a[...] + gread_b], axis=1)
    grad = grad * (sg * (1.0 + sc * (1.0 - sg)))
    back, rows_sum = conv_backward(grad, spre[...], taps_state, col)
    low = back.astype(BF)
    low_state[...] = low
    sums_state[...] = put_rows(rows_sum, 2 * STATE)
    i, j = lower_matrix()
    upper = (i <= j).astype(F32)
    at_end = lax.broadcasted_iota(jnp.int32, (BLOCK, LANES), 0) == BLOCK - 1
    decays = []
    for b in range(blocks):
        rows = slice(b * BLOCK, (b + 1) * BLOCK)
        side = out_side[rows]
        last = jnp.sum(side, axis=0, keepdims=True) + keep_grads[b] * keep[b : b + 1]
        cum_grad = rowside[rows, :] - colside[rows] - side + jnp.where(at_end, last, 0.0)
        decays.append(dot_high(upper, cum_grad))
    decay_grad = jnp.concatenate(decays, axis=0)
    rate = par[1:2]
    step_grad = (step_grad + decay_grad * rate) * sigmoid(st[0])
    rows_head = [
        jnp.sum(step_grad, axis=0, keepdims=True),
        jnp.sum(decay_grad * st[1] * rate, axis=0, keepdims=True),
    ]
    sums_head[...] = put_rows(rows_head, LANES)
    low = jnp.concatenate([jnp.zeros((HALO, LANES), F32), step_grad], axis=0).astype(BF)
    low_step[...] = low


def weight_grad_kernel(place, normed, low_inner, low_state, low_step, *refs):
    grad_outs, (gwi, gws, gwp, sems) = refs[:-4], refs[-4:]
    x = normed[...]
    for tile in range(low_inner.shape[1] // TILE):
        lanes = slice(tile * TILE, (tile + 1) * TILE)
        gwi[:, lanes] = dot_tn(x, low_inner[:, lanes]).astype(BF)
    gws[...] = dot_tn(x, low_state[...]).astype(BF)
    gwp[...] = dot_tn(x, low_step[...]).astype(BF)
    store_grads(place, (gwi, gws, gwp), grad_outs, sems)


def token_grad_kernel(
    place, low_inner, low_state, low_step, gn_gate, tok, cot, gain, sums_in, sums_out, sums_state, sums_head, *refs
):
    weights, (grad, back, pack, win, wst, wsp, sems) = refs[:-7], refs[-7:]
    load_weights(place, weights, (win, wst, wsp), sems)
    wait_weights((win, wst, wsp), sems)
    width = tok.shape[1]
    gn = dot_nt(low_inner[...], win[...]) + dot_nt(low_state[...], wst[...])
    gn = gn + dot_nt(low_step[...], wsp[...])
    gn = gn + jnp.concatenate([jnp.zeros((HALO, width), F32), gn_gate[...]], axis=0)
    t = tok[...].astype(F32)
    r = lax.rsqrt(jnp.mean(t * t, axis=1, keepdims=True) + EPS)
    scaled = t * r
    inner = pack.shape[1]
    pack[0 : KW + 1, :] = sums_in[: KW + 1]
    pack[KW + 1 : KW + 2, :] = sums_out[0:1]
    pack[KW + 2 :, :] = jnp.zeros((8 - KW - 2, inner), F32)
    pack[KW + 2 : KW + 3, :width] = jnp.sum(gn * scaled, axis=0, keepdims=True)
    pack[KW + 2 : KW + 3, width : width + LANES] = sums_head[0:1]
    pack[KW + 2 : KW + 3, width + LANES : width + 2 * LANES] = sums_head[1:2]
    skips = head_sum(sums_out[...], head_matrix(0, inner))
    pack[KW + 2 : KW + 3, width + 2 * LANES : width + 3 * LANES] = skips[1:2]
    for k in range(KW + 1):
        pack[KW + 3 : KW + 4, 2 * STATE * k : 2 * STATE * (k + 1)] = sums_state[k : k + 1]
    gg = gn * gain[0:1]
    result = gg * r - t * (r * r * r * jnp.mean(gg * t, axis=1, keepdims=True))
    back[...] = result[:HALO]
    grad[...] = result[HALO:] + cot[...].astype(F32)


def finish_kernel(place, a, b, c, d, inner, state, step, conv, conv_state, norm, gain, *heads):
    depth, span = inner.shape
    per = span // HEAD_DIM

    def total(first, count):
        rows = slice(first, first + count)
        return a[rows].astype(F32) + b[rows].astype(F32) + c[rows].astype(F32) + d[rows].astype(F32)

    inner[...] = total(0, depth)
    last = total(depth, depth)
    state[...] = last[:, : 2 * STATE]
    turn_heads = lax.rem(LANES - place[1] * per, LANES)
    step[...] = pltpu.roll(last[:, 2 * STATE :], turn_heads, 1)[:, :per]
    small = total(2 * depth, 2 * 8)
    conv[...] = small[: KW + 1]
    gain[...] = small[KW + 1]
    whole = [
        jnp.concatenate([small[8 + 2 * q + n : 9 + 2 * q + n] for q in range(4)], axis=1) for n in range(2)
    ]
    width = norm.shape[0]
    norm[...] = whole[0][0, :width]
    rows = [whole[1][:, 2 * STATE * k : 2 * STATE * (k + 1)] for k in range(KW + 1)]
    conv_state[...] = put_rows(rows, 2 * STATE)[: KW + 1]
    rows = [whole[0][:, width + LANES * n : width + LANES * (n + 1)] for n in range(3)]
    rows = pltpu.roll(put_rows(rows, LANES), turn_heads, 1)
    for n, head in enumerate(heads):
        head[...] = rows[n, :per]


def line(shift, size):
    return [(i, i + shift) for i in range(size) if 0 <= i + shift < size]


def pass_first(payload, size, sign):
    return lax.ppermute(payload, "tensor", line(sign, size))


def pass_states(payload, came, size, sign, first=()):
    own = payload[:STATE].astype(F32)
    factor = payload[STATE].astype(F32) + payload[STATE + 1].astype(F32)
    near, far, send = came, jnp.zeros_like(came[:STATE]), came
    reach = 2
    while reach < size:
        near_factor = near[STATE].astype(F32) + near[STATE + 1].astype(F32)
        total = near[:STATE].astype(F32)
        if reach > 2:
            total = total + last_factor[None] * far[:STATE].astype(F32)
        send = (own + factor[None] * total).astype(BF)
        if 2 * reach < size:
            both = factor * near_factor
            hi = both.astype(BF)
            lo = (both - hi.astype(F32)).astype(BF)
            send = jnp.concatenate([send, hi[None], lo[None]], axis=0)
        send = after(send, *first)
        far = lax.ppermute(send, "tensor", line(sign * reach, size))
        last_factor = near_factor
        if 2 * reach < size:
            total = near[:STATE].astype(F32) + near_factor[None] * far[:STATE].astype(F32)
            both = near_factor * (far[STATE].astype(F32) + far[STATE + 1].astype(F32))
            hi = both.astype(BF)
            lo = (both - hi.astype(F32)).astype(BF)
            near = jnp.concatenate([total.astype(BF), hi[None], lo[None]], axis=0)
            near = jnp.pad(near, ((0, HALO - 2), (0, 0)))
            far = jnp.zeros_like(far)
        reach = 2 * reach
    return near, far[:STATE], send


def entering(near, far):
    rows = near[STATE:, :].astype(F32)
    return near[:STATE, :].astype(F32) + (rows[0:1] + rows[1:2]) * far[...].astype(F32)


def swap(values, mask):
    return lax.ppermute(values, "dp", [(i, i ^ mask) for i in range(8)])


def turn(values, shift):
    return lax.ppermute(values, "tensor", [(i, (i + shift) % 4) for i in range(4)])


def cross(values, mask):
    return lax.ppermute(values, "tensor", [(i, i ^ mask) for i in range(4)])


def ring(values):
    return [values] + [turn(values, -m) for m in range(1, 4)]


def gather_pieces(column, first=()):
    same = [column] + [swap(column, k) for k in ORDER[1:4]]
    return same + [swap(column, 1)] + [swap(after(v, *first), 1) for v in same[1:]]


def sum_pair_kernel(place, mine, came, *outs):
    for n, out in enumerate(outs):
        out[...] = mine[n] + came[n]


def sum_pair_pack_kernel(place, mine, came, pack, came_pack, *outs):
    slots, depth, span = mine.shape[1:]
    total = pack[...] + came_pack[...]
    rows = jnp.concatenate([total[:, q * span : (q + 1) * span] for q in range(4)], axis=0).astype(BF)
    for n, out in enumerate(outs):
        for m in range(slots):
            out[m * depth : (m + 1) * depth, :] = mine[n, m] + came[n, m]
        out[slots * depth :, :] = rows


def sum_column_pack_kernel(place, a, b, c, d, *refs):
    outs, rows = refs[:4], refs[4]
    depth = (a.shape[0] - 32) // 5

    def total(first, count):
        part = slice(first, first + count)
        return a[part].astype(F32) + b[part].astype(F32) + c[part].astype(F32) + d[part].astype(F32)

    rows[...] = total(5 * depth, 32)
    last = total(4 * depth, depth).astype(BF)
    rest = jnp.concatenate([rows[8 * q + KW + 2 : 8 * q + KW + 4] for q in range(4)], axis=0)
    for m, out in enumerate(outs):
        out[:depth, :] = total(m * depth, depth).astype(BF)
        out[depth : 2 * depth, :] = last
        own = rows[pl.ds(aligned((place[1] + m) % 4, 8), 8), :]
        out[2 * depth :, :] = jnp.concatenate([own, rest], axis=0).astype(BF)


def sum_column_kernel(place, a, b, c, d, *outs):
    for m, out in enumerate(outs):
        total = a[m].astype(F32) + b[m].astype(F32) + c[m].astype(F32) + d[m].astype(F32)
        out[...] = total.astype(BF)


def sum_last_kernel(place, a, b, c, d, first, second):
    for n, out in enumerate((first, second)):
        out[...] = a[n].astype(F32) + b[n].astype(F32) + c[n].astype(F32) + d[n].astype(F32)


def reduce_core(where, mine, other):
    came = swap(other, 1)
    return call(sum_pair_kernel, [sds(mine.shape[1:], BF)] * 4, (where, mine, came), name="sum_pair")


def reduce_plane(where, parts):
    came = [swap(parts[n], ORDER[n]) for n in range(1, 4)]
    shape = (2, *parts[0].shape[-2:])
    return call(sum_column_kernel, [sds(shape, BF)] * 4, (where, parts[0], *came), name="sum_column")


def reduce_line(where, parts):
    came = [turn(parts[m], m) for m in range(1, 4)]
    return call(
        sum_last_kernel, [sds(parts[0].shape[1:], F32)] * 2, (where, parts[0], *came), name="sum_last"
    )


def after_all(values, *others):
    return lax.optimization_barrier((*values, *others))[: len(values)]


def after(value, *others):
    return lax.optimization_barrier((value, *others))[0]


def gather(shard):
    return lax.all_gather(
        lax.all_gather(shard, "tensor", axis=1, tiled=True), "dp", axis=0, tiled=True
    )


def scatter(grad):
    part = lax.psum_scatter(grad, "dp", scatter_dimension=0, tiled=True)
    return lax.psum_scatter(part, "tensor", scatter_dimension=1, tiled=True).astype(F32)


def make_shards(mesh):
    size = mesh.shape["tensor"]
    blocked = size == 4 and mesh.shape["dp"] == 8

    def shards(
        tokens, segments, cotangent, norm_gain, w_gate, w_inner, w_step, w_state, conv_inner, conv_state,
        step_bias, decay_log, skip_gain, out_gain, w_out,
    ):
        count, width = tokens.shape
        place = lax.axis_index("tensor")
        blocks = count // BLOCK
        inner = w_inner.shape[1] * size
        heads = w_step.shape[1] * size

        halo = lax.ppermute(tokens[count - HALO :], "tensor", line(1, size))
        tok = jnp.concatenate([halo, tokens], axis=0)
        wide_tok = tok.astype(F32)
        gain = norm_gain.astype(F32)
        rms = lax.rsqrt(jnp.mean(wide_tok * wide_tok, axis=1, keepdims=True) + EPS)
        normed = (wide_tok * rms * gain).astype(BF)

        padded = jnp.concatenate([jnp.full((HALO,), -1, jnp.int32), segments])
        near = lax.dynamic_slice(padded, (place * count,), (HALO + count,))
        seg = near[HALO:]
        masks = [near[HALO - k : HALO - k + count] == seg for k in range(1, KW)]
        grid = seg.reshape(blocks, BLOCK)
        prev = near[HALO - 1 : HALO - 1 + count].reshape(blocks, BLOCK)[:, :1]
        from_prev = (grid == prev).reshape(-1)
        at_last = (grid == grid[:, BLOCK - 1 :]).reshape(-1)
        cols = jnp.stack([*masks, from_prev, at_last], axis=1).astype(F32)
        seg_col = seg.astype(F32)[:, None]
        seg_row = seg.astype(F32)[None]

        def pad_heads(row):
            return jnp.pad(row, ((0, 0), (0, LANES - heads)))

        where = jnp.stack([lax.axis_index("dp"), place]).astype(jnp.int32)
        depth, span = w_inner.shape
        per = heads // size
        if blocked:
            tall = HALO + depth

            def place_at(block, row, lane):
                rows = (row, tall - row - block.shape[0])
                return jnp.pad(block, (rows, (lane, span - lane - block.shape[1])))

            pack = place_at(w_inner, 0, 0) + place_at(w_step.T, depth + KW + 3, 0)
            pack = pack + place_at(conv_inner, depth, 0) + place_at(out_gain[None], depth + KW + 1, 0)
            for n, row in enumerate((step_bias, decay_log, skip_gain)):
                pack = pack + place_at(row[None], depth + KW + 2, n * per)
            came = ring(pack)
            pair_out = jnp.stack([w_gate, w_out])[None]
            pair_out = jnp.concatenate([pair_out, cross(pair_out, 1)])
            came_out = jnp.concatenate([pair_out, cross(pair_out, 2)])

            column, taps, par, wide = call(
                unpack_kernel,
                [
                    sds((5, depth, span), BF),
                    sds((8, inner), F32),
                    sds((8, LANES), F32),
                    sds((8, inner), F32),
                ],
                (where, *came, w_state),
                name="unpack",
            )
            pieces = gather_pieces(column, (came_out,))
            pieces_out = gather_pieces(after(came_out, *pieces[1:4]))
        else:
            conv_whole, head_whole, gain_whole = [
                lax.all_gather(v, "tensor", axis=v.ndim - 1, tiled=True).astype(F32)
                for v in (conv_inner, jnp.stack([step_bias, decay_log, skip_gain]), out_gain)
            ]
            pieces = [gather(w_inner), lax.all_gather(w_state, "dp", axis=0, tiled=True), pad_heads(gather(w_step))]
            pieces_out = [gather(w_gate), gather(w_out)]
            taps = jnp.pad(conv_whole, ((0, 8 - KW - 1), (0, 0)))
            bias, rate, skip = head_whole[0], -jnp.exp(head_whole[1]), head_whole[2]
            par = pad_heads(jnp.pad(jnp.stack([bias, rate]), ((0, 6), (0, 0))))
            wide = jnp.pad(jnp.stack([gain_whole, jnp.repeat(skip, HEAD_DIM)]), ((0, 6), (0, 0)))
        taps_state = jnp.pad(conv_state.astype(F32), ((0, 8 - KW - 1), (0, 0)))
        in_scratch = [
            pltpu.VMEM((width, inner), BF),
            pltpu.VMEM((width, 2 * STATE), BF),
            pltpu.VMEM((width, LANES), BF),
            pltpu.SemaphoreType.DMA((3,)),
        ]
        out_scratch = [
            pltpu.VMEM((width, inner), BF),
            pltpu.VMEM((width, inner), BF),
            pltpu.SemaphoreType.DMA((2,)),
        ]

        def last_args(fixed, arrays):
            return {"args": (where, *fixed, *arrays), "far": range(1 + len(fixed), 1 + len(fixed) + len(arrays))}

        pre, conv, spre, sconv, rw, st, keep, c_ref, pay = call(
            project_kernel,
            [
                sds((HALO + count, inner), BF),
                sds((count, inner), F32),
                sds((HALO + count, 2 * STATE), F32),
                sds((count, 2 * STATE), F32),
                sds((count, 2 * STATE), BF),
                sds((5, count, LANES), F32),
                sds((8, LANES), F32),
                sds((max(1, blocks - 1), STATE, inner), F32),
                sds((STATE + HALO, inner), BF),
            ],
            scratch=in_scratch,
            **last_args((normed, taps, taps_state, par, cols), pieces),
            name="project",
            micros=9.5,
        )
        y = call(
            scan_kernel,
            [sds((count, inner), F32)],
            (where, conv, st, rw, seg_col, seg_row),
            [pltpu.VMEM((BLOCK, BLOCK), F32), pltpu.VMEM((LANES, BLOCK), F32)],
            name="scan",
            micros=10,
        )[0]
        *enter, sent = pass_states(pay, pass_first(pay, size, 1), size, 1, (y,))
        gate, gout = call(
            gate_kernel,
            [sds((count, inner), F32)] * 2,
            scratch=out_scratch,
            **last_args((after(normed, sent), cotangent), pieces_out),
            name="gate",
            micros=6,
        )
        out_low, ggate, gscan, rowside, gread_a, states, d_ref, pay, sums = call(
            output_kernel,
            [
                sds((count, inner), BF),
                sds((count, inner), BF),
                sds((count, inner), BF),
                sds((count, LANES), F32),
                sds((count, STATE), F32),
                sds((blocks, STATE, inner), BF),
                sds((max(1, blocks - 1), STATE, inner), F32),
                sds((STATE + HALO, inner), BF),
                sds((8, inner), F32),
            ],
            (where, *enter, c_ref, keep, gate, gout, y, conv, rw, st, wide),
            [pltpu.VMEM((ROWS, inner), F32), pltpu.VMEM((blocks, STATE, inner), F32)],
            name="output",
            micros=9.5,
        )
        if blocked:
            shapes_out = [sds((4, 4, 2, depth, span), BF)] * 2
            shapes_in = [sds((4, 5, depth, span), BF)] * 2
        else:
            shapes_out = [sds((width, inner), BF)] * 2
            shapes_in = [sds((width, inner), BF), sds((width, 2 * STATE), BF), sds((width, LANES), BF)]
        mixed, gn_gate, *grads_out = call(
            gate_grad_kernel,
            [sds((count, width), BF), sds((count, width), F32), *shapes_out],
            far_outs=(2, 3),
            scratch=[
                pltpu.VMEM((width, inner), BF),
                pltpu.VMEM((width, inner), BF),
                *out_scratch,
            ],
            **last_args((normed, cotangent, out_low, ggate, tok), pieces_out),
            name="gate_grad",
            micros=8.3,
        )
        came_pay = pass_first(pay, size, -1)
        if blocked:
            mine_out, other_out = grads_out
            parts_out = reduce_core(where, mine_out, after(other_out, came_pay))
        else:
            parts_out = ()
        *leave, sent = pass_states(pay, came_pay, size, -1)
        by_block = [
            call(
                functools.partial(scan_grad_kernel, b),
                [sds((BLOCK, inner), F32), sds((BLOCK, LANES), F32), *[sds((BLOCK, STATE), F32)] * 2],
                (where, after(gscan, sent, *parts_out), conv, st, rw, seg_col, seg_row),
                [
                    pltpu.VMEM((BLOCK, BLOCK), F32),
                    pltpu.VMEM((BLOCK, BLOCK), F32),
                    pltpu.VMEM((LANES, BLOCK), F32),
                ],
                name=f"scan_grad_{b}",
                micros=9,
            )
            for b in range(blocks)
        ]
        low_inner, low_state, low_step, sums_in, sums_state, sums_head = call(
            input_grad_kernel,
            [
                sds((HALO + count, inner), BF),
                sds((HALO + count, 2 * STATE), BF),
                sds((HALO + count, LANES), BF),
                sds((8, inner), F32),
                sds((8, 2 * STATE), F32),
                sds((8, LANES), F32),
            ],
            (
                where, *leave, d_ref, keep, states, conv, pre, gscan, st, rw, sconv, spre, rowside, gread_a, taps,
                taps_state, par, wide, cols, *[v for part in by_block for v in part],
            ),
            [pltpu.VMEM((blocks, STATE, inner), BF)],
            name="input_grad",
            micros=9,
        )
        low_next = low_inner
        if blocked:
            lines_out = reduce_plane(where, parts_out)
            low_next = after(low_inner, *lines_out)
        grads_in = call(
            weight_grad_kernel,
            shapes_in,
            (where, normed, low_next, low_state, low_step),
            scratch=in_scratch,
            far_outs=range(len(shapes_in)),
            name="weight_grad",
            micros=5,
        )
        if blocked:
            mine_in, other_in = grads_in
            came_in = swap(other_in, 1)
            low_inner = after(low_inner, other_in)
        grad, back, pack = call(
            token_grad_kernel,
            [sds((count, width), F32), sds((HALO, width), F32), sds((8, inner), F32)],
            scratch=in_scratch,
            **last_args((low_inner, low_state, low_step, gn_gate, tok, cotangent, gain[None], sums_in, sums, sums_state, sums_head), pieces),
            name="token_grad",
            micros=5,
        )
        if blocked:
            tall = 5 * depth + 32
            parts_in = call(
                sum_pair_pack_kernel,
                [sds((tall, span), BF)] * 4,
                (where, mine_in, came_in, pack, swap(pack, 1)),
                name="sum_pair_pack",
            )
            lines_out = after_all(lines_out, *parts_in)
            grad_gate, grad_out = reduce_line(where, lines_out)
        if blocked:
            came_in = [swap(parts_in[n], ORDER[n]) for n in range(1, 4)]
            lines_in = call(
                sum_column_pack_kernel,
                [sds((2 * depth + 2 * 8, span), BF)] * 4,
                (where, parts_in[0], *came_in),
                [pltpu.VMEM((32, span), F32)],
                name="sum_column_pack",
            )
            back = after(back, lines_in[0])
            grad_inner, grad_state, grad_step, grad_conv, grad_conv_state, norm, grad_gain, *head_grads = call(
                finish_kernel,
                [
                    sds((depth, span), F32),
                    sds((depth, 2 * STATE), F32),
                    sds((depth, per), F32),
                    sds((KW + 1, span), F32),
                    sds((KW + 1, 2 * STATE), F32),
                    sds((width,), F32),
                    sds((span,), F32),
                    *[sds((per,), F32)] * 3,
                ],
                (where, lines_in[0], *[turn(lines_in[m], m) for m in range(1, 4)]),
                name="finish",
            )
        else:
            pack = lax.psum(pack, ("dp", "tensor"))
            own = lax.dynamic_slice(pack, (0, place * span), (KW + 2, span))
            norm = pack[KW + 2, :width]
            grad_conv, grad_gain = own[: KW + 1], own[KW + 1]
            grad_conv_state = pack[KW + 3, : (KW + 1) * 2 * STATE].reshape(KW + 1, 2 * STATE)
            head_grads = [
                lax.dynamic_slice(pack[KW + 2], (width + LANES * n + place * per,), (per,)) for n in range(3)
            ]
            grad_gate, grad_out, grad_inner, grad_step = [
                scatter(v) for v in (*grads_out, grads_in[0], grads_in[2][:, :heads])
            ]
            grad_state = lax.psum_scatter(grads_in[1], "dp", scatter_dimension=0, tiled=True)
            grad_state = lax.psum(grad_state, "tensor").astype(F32)
        back = lax.ppermute(back, "tensor", line(-1, size))
        grad = grad.at[count - HALO :].add(back)
        return (
            mixed,
            grad,
            norm,
            grad_gate,
            grad_inner,
            grad_step,
            grad_state,
            grad_conv,
            grad_conv_state,
            *head_grads,
            grad_gain,
            grad_out,
        )

    return shards


def solution(mesh):
    in_specs = (
        P(("dp", "tensor"), None),
        P("dp"),
        P(("dp", "tensor"), None),
        P(),
        P("dp", "tensor"),
        P("dp", "tensor"),
        P("dp", "tensor"),
        P("dp", None),
        P(None, "tensor"),
        P(),
        P("tensor"),
        P("tensor"),
        P("tensor"),
        P("tensor"),
        P("dp", "tensor"),
    )
    out_specs = (
        P(("dp", "tensor"), None),
        P(("dp", "tensor"), None),
        P(),
        P("dp", "tensor"),
        P("dp", "tensor"),
        P("dp", "tensor"),
        P("dp", None),
        P(None, "tensor"),
        P(),
        P("tensor"),
        P("tensor"),
        P("tensor"),
        P("tensor"),
        P("dp", "tensor"),
    )
    return jax.shard_map(
        make_shards(mesh), mesh=mesh, in_specs=in_specs, out_specs=out_specs, check_vma=False
    )
```

```python
import functools
import math

import jax
import jax.numpy as jnp
from jax import lax
from jax.experimental import pallas as pl
from jax.experimental.pallas import tpu as pltpu
from jax.sharding import PartitionSpec as P

HEAD_DIM = 64
STATE = 128
KW = 4
BLOCK = 256
HALO = 16
LANES = 128
TILE = 256
ROWS = 128
HALVES = 2
EPS = 1e-05
F32 = jnp.float32
BF = jnp.bfloat16
HIGH = lax.Precision.HIGHEST
SPARE = 3 * 2**20
ORDER = (0, 2, 4, 6, 1, 3, 5, 7)


def dot(a, b):
    return lax.dot_general(a, b, (((1,), (0,)), ((), ())), preferred_element_type=F32)


def dot_nt(a, b):
    return lax.dot_general(a, b, (((1,), (1,)), ((), ())), preferred_element_type=F32)


def dot_tn(a, b):
    return lax.dot_general(a, b, (((0,), (0,)), ((), ())), preferred_element_type=F32)


def dot_high(a, b):
    return lax.dot_general(
        a, b, (((1,), (0,)), ((), ())), precision=HIGH, preferred_element_type=F32
    )


def sigmoid(x):
    return 0.5 * jnp.tanh(0.5 * x) + 0.5


def expand(x, first, count):
    lane = lax.broadcasted_iota(jnp.int32, (x.shape[0], LANES), 1)
    return jnp.concatenate(
        [
            jnp.where(lane < HEAD_DIM, x[:, h : h + 1], x[:, h + 1 : h + 2])
            for h in range(first, first + count, 2)
        ],
        axis=1,
    )


def halved(tile, inner):
    first = tile * TILE % (inner // HALVES)
    return tile * TILE // (inner // HALVES), slice(first, first + TILE)


def head_matrix(first, channels):
    channel = lax.broadcasted_iota(jnp.int32, (channels, LANES), 0)
    head = lax.broadcasted_iota(jnp.int32, (channels, LANES), 1)
    return (channel // HEAD_DIM + first == head).astype(BF)


def head_sum(x, matrix):
    hi = x.astype(BF)
    lo = (x - hi.astype(F32)).astype(BF)
    return dot(hi, matrix) + dot(lo, matrix)


def lower_matrix():
    i = lax.broadcasted_iota(jnp.int32, (BLOCK, BLOCK), 0)
    j = lax.broadcasted_iota(jnp.int32, (BLOCK, BLOCK), 1)
    return i, j


def conv_forward(values, taps, cols):
    result = taps[KW : KW + 1] + taps[0:1] * values[HALO:]
    for k in range(1, KW):
        result = result + taps[k : k + 1] * pltpu.roll(values, k, 0)[HALO:] * cols[:, k - 1 : k]
    return result


def conv_backward(grad, values, taps, cols):
    width = grad.shape[1]
    whole = HALO + grad.shape[0]
    zero = jnp.zeros((HALO, width), F32)
    base = jnp.concatenate([zero, grad], axis=0)
    result = taps[0:1] * base
    sums = [jnp.sum(grad * values[HALO:], axis=0, keepdims=True)]
    for k in range(1, KW):
        masked = jnp.concatenate([zero, grad * cols[:, k - 1 : k]], axis=0)
        back = pltpu.roll(masked, whole - k, 0)
        result = result + taps[k : k + 1] * back
        sums.append(jnp.sum(back * values, axis=0, keepdims=True))
    sums.append(jnp.sum(grad, axis=0, keepdims=True))
    return result, sums


def put_rows(rows, width):
    index = lax.broadcasted_iota(jnp.int32, (8, width), 0)
    result = jnp.zeros((8, width), F32)
    for i, row in enumerate(rows):
        result = jnp.where(index == i, row, result)
    return result


def call(kernel, outs, args, scratch=(), name=None, micros=1.0, far=(), far_outs=()):
    size = 1 << 20

    held = [a for i, a in enumerate(args) if i > 0 and i not in far]
    held += [o for i, o in enumerate(outs) if i not in far_outs]
    limit = SPARE + sum(a.size * a.dtype.itemsize for a in held)
    for item in scratch:
        if len(item.shape) > 1:
            limit += math.prod(item.shape) * jnp.dtype(item.dtype).itemsize

    def spec(space):
        return pl.BlockSpec(memory_space=space)

    ins = [
        spec(pltpu.SMEM if i == 0 else pltpu.HBM if i in far else pltpu.VMEM) for i in range(len(args))
    ]
    return pl.pallas_call(
        kernel,
        out_shape=outs,
        in_specs=ins,
        out_specs=[spec(pl.ANY if i in far_outs else pltpu.VMEM) for i in range(len(outs))],
        scratch_shapes=list(scratch),
        compiler_params=pltpu.CompilerParams(vmem_limit_bytes=limit),
        cost_estimate=pl.CostEstimate(flops=int(micros * 1.15e9), bytes_accessed=size, transcendentals=0),
        name=name,
    )(*args)


def sds(shape, dtype):
    return jax.ShapeDtypeStruct(shape, dtype)


def aligned(value, size):
    return pl.multiple_of(value * size, size)


def load_weights(place, refs, targets, sems):
    if len(refs[0].shape) == 2:
        copies = [pltpu.make_async_copy(r, t, sems.at[n]) for n, (r, t) in enumerate(zip(refs, targets))]
        for copy in copies:
            copy.start()
        return
    split = refs[0].shape[0] == 5
    depth, span = refs[0].shape[-2:]
    for n, k in enumerate(ORDER):
        row = pl.ds(aligned(place[0] ^ k, depth), depth)
        for m in range(4):
            who = (place[1] + m) % 4 if split else place[1] ^ m
            column = pl.ds(aligned(who, span), span)
            for g in range(1 if split else 2):
                source = refs[n].at[m] if split else refs[n].at[m, g]
                pltpu.make_async_copy(source, targets[g].at[row, column], sems.at[g]).start()
        if split:
            wide = targets[1].shape[1]
            pltpu.make_async_copy(refs[n].at[4, :, :wide], targets[1].at[row, :], sems.at[1]).start()
            pltpu.make_async_copy(refs[n].at[4, :, wide:], targets[2].at[row, :], sems.at[2]).start()


def wait_weights(targets, sems):
    for n, target in enumerate(targets):
        pltpu.make_async_copy(target, target, sems.at[n]).wait()


def store_grads(place, sources, outs, sems):
    if len(outs[0].shape) == 2:
        copies = [pltpu.make_async_copy(s, o, sems.at[n]) for n, (s, o) in enumerate(zip(sources, outs))]
        for copy in copies:
            copy.start()
    else:
        split = outs[0].shape[1] == 5
        depth, span = outs[0].shape[-2:]
        for n, k in enumerate(ORDER):
            out = outs[n // 4].at[n % 4]
            sem = sems.at[n // 4]
            row = pl.ds(aligned(place[0] ^ k, depth), depth)
            for m in range(4):
                column = pl.ds(aligned((place[1] + m) % 4, span), span)
                for g in range(1 if split else 2):
                    target = out.at[m] if split else out.at[m, g]
                    pltpu.make_async_copy(sources[g].at[row, column], target, sem).start()
            if split:
                wide = sources[1].shape[1]
                pltpu.make_async_copy(sources[1].at[row, :], out.at[4, :, :wide], sem).start()
                pltpu.make_async_copy(sources[2].at[row, :], out.at[4, :, wide:], sem).start()
    for n, out in enumerate(outs):
        pltpu.make_async_copy(out, out, sems.at[n]).wait()


def unpack_kernel(place, *refs):
    parts, (state, column, taps, par, wide) = refs[:4], refs[4:]
    depth, span = column.shape[1:]
    per = span // HEAD_DIM
    heads = wide.shape[1] // HEAD_DIM
    lane = lax.broadcasted_iota(jnp.int32, (8, LANES), 1)
    step = jnp.zeros((LANES, LANES), F32)
    rows = [jnp.zeros((8, LANES), F32)] * 3
    for m, part in enumerate(parts):
        who = (place[1] + m) % 4
        lanes = pl.ds(aligned(who, span), span)
        column[m] = part[:depth, :]
        low = part[depth:, :].astype(F32)
        tall = jnp.concatenate([low[:, :LANES], jnp.zeros((LANES - HALO, LANES), F32)], axis=0)
        tall = pltpu.roll(tall, LANES - KW - 3, 0)
        tall = jnp.where(lax.broadcasted_iota(jnp.int32, (LANES, LANES), 0) < per, tall, 0.0)
        step = step + pltpu.roll(tall, who * per, 0)
        taps[:, lanes] = low[:8]
        wide[0:1, lanes] = low[KW + 1 : KW + 2]
        row = jnp.broadcast_to(low[KW + 2 : KW + 3, :LANES], (8, LANES))
        for n in range(3):
            own = pltpu.roll(row, LANES - n * per, 1) if n else row
            rows[n] = rows[n] + pltpu.roll(jnp.where(lane < per, own, 0.0), who * per, 1)
    column[4] = jnp.concatenate([state[...], step.T[:depth].astype(BF)], axis=1)
    par[...] = put_rows([rows[0][0:1], jnp.where(lane < heads, -jnp.exp(rows[1]), 0.0)[0:1]], LANES)
    wide[1:2, :] = expand(rows[2], 0, heads)[0:1]


def project_kernel(
    place, *refs
):
    (normed, taps, taps_state, par, cols), refs = refs[:5], refs[5:]
    weights, refs = refs[: -12 - HALVES], refs[-12 - HALVES :]
    pre, conv, spre, sconv, rw, st, keep, c_ref, *pay, win, wst, wsp, sems = refs
    load_weights(place, weights, (win, wst, wsp), sems)
    wait_weights((win, wst, wsp), sems)
    project(normed, win, wst, wsp, taps, taps_state, par, cols, pre, conv, spre, sconv, rw, st, keep, c_ref, pay)


def project(
    normed, win, wst, wsp, taps, taps_state, par, cols, pre, conv, spre, sconv, rw, st, keep, c_ref, pay
):
    tokens = conv.shape[0]
    inner = conv.shape[1]
    blocks = tokens // BLOCK
    x = normed[...]
    low = x[HALO:]
    col = cols[...]
    sp = dot(low, wsp[...]) + par[0:1]
    step = jnp.maximum(sp, 0.0) + jnp.log1p(jnp.exp(-jnp.abs(sp)))
    decay = step * par[1:2]
    i, j = lower_matrix()
    lower = (i >= j).astype(F32)
    st[0] = sp
    st[1] = step
    keeps = []
    outs = []
    for b in range(blocks):
        rows = slice(b * BLOCK, (b + 1) * BLOCK)
        cum = dot_high(lower, decay[rows])
        last = cum[BLOCK - 1 : BLOCK]
        from_prev = col[rows, 3:4]
        out = jnp.exp(last - cum) * col[rows, 4:5]
        st[2, rows] = cum
        st[3, rows] = out
        st[4, rows] = jnp.exp(cum) * from_prev
        keeps.append(jnp.exp(last) * from_prev[BLOCK - 1 : BLOCK])
        outs.append(out * step[rows])
    keep[...] = put_rows(keeps, LANES)
    whole = keeps[0]
    for b in range(1, blocks):
        whole = whole * keeps[b]
    state = dot(x, wst[...])
    spre[...] = state
    sc = conv_forward(state, taps_state, col)
    sconv[...] = sc
    rw[...] = (sc * sigmoid(sc)).astype(BF)
    entry = rw[:, :STATE]
    index = lax.broadcasted_iota(jnp.int32, (HALO, TILE), 0)
    for tile in range(inner // TILE):
        lanes = slice(tile * TILE, (tile + 1) * TILE)
        heads = TILE // HEAD_DIM
        first = tile * heads
        value = dot(x, win[:, lanes])
        pre[:, lanes] = value.astype(BF)
        c = conv_forward(value, taps[:, lanes], col)
        conv[:, lanes] = c
        c = c.astype(F32)
        act = (c * sigmoid(c)).astype(BF).astype(F32)
        total = None
        for b in range(blocks):
            rows = slice(b * BLOCK, (b + 1) * BLOCK)
            scaled = (act[rows] * expand(outs[b], first, heads)).astype(BF)
            part = dot_tn(entry[rows], scaled)
            if b < blocks - 1:
                c_ref[b, :, lanes] = part
            total = part if b == 0 else total * expand(keeps[b], first, heads) + part
        part, local = halved(tile, inner)
        pay[part][:STATE, local] = total.astype(BF)
        wide = expand(whole, first, heads)
        hi = wide.astype(BF).astype(F32)
        pay[part][STATE:, local] = jnp.where(index == 0, hi, jnp.where(index == 1, wide - hi, 0.0)).astype(BF)


def gate_kernel(place, normed, cot, *refs):
    weights, (gate, gout, wg, wo, sems) = refs[:-5], refs[-5:]
    load_weights(place, weights, (wg, wo), sems)
    wait_weights((wg, wo), sems)
    for tile in range(gate.shape[1] // TILE):
        lanes = slice(tile * TILE, (tile + 1) * TILE)
        gate[:, lanes] = dot(normed[HALO:, :], wg[:, lanes])
        gout[:, lanes] = dot(cot[...], wo[:, lanes])


def scan_kernel(b, place, conv, st, rw, seg_col, seg_row, y, smask, cum_t):
    inner = conv.shape[1]
    half = BLOCK // 2
    i, j = lower_matrix()
    lane = lax.broadcasted_iota(jnp.int32, (BLOCK, LANES), 1)
    rows = slice(b * BLOCK, (b + 1) * BLOCK)
    scores = dot_nt(rw[rows, STATE:], rw[rows, :STATE])
    same = (i >= j) & (seg_col[rows, 0:1] == seg_row[0:1, rows])
    smask[...] = jnp.where(same, scores, 0.0)
    cum_t[...] = st[2, rows].T

    def pair(p, carry):
        cum = pltpu.roll(st[2, rows], LANES - 2 * p, 1)
        step = pltpu.roll(st[1, rows], LANES - 2 * p, 1)
        lanes = pl.ds(pl.multiple_of(p * LANES, LANES), LANES)
        c = conv[rows, lanes].astype(F32)
        act = (c * sigmoid(c)).astype(BF).astype(F32)
        xs = (act * jnp.where(lane < HEAD_DIM, step[:, 0:1], step[:, 1:2])).astype(BF)
        top = jnp.zeros((half, LANES), F32)
        bottom = jnp.zeros((half, LANES), F32)
        for a in range(2):
            mine = jnp.where((lane < HEAD_DIM) == (a == 0), xs, jnp.zeros_like(xs))
            row = cum_t[pl.ds(2 * p + a, 1), :]
            e = jnp.exp(jnp.minimum(cum[:half, a : a + 1] - row[:, :half], 0.0))
            top = top + dot((smask[:half, :half] * e).astype(BF), mine[:half])
            e = jnp.exp(jnp.minimum(cum[half:, a : a + 1] - row, 0.0))
            bottom = bottom + dot((smask[half:, :] * e).astype(BF), mine)
        y[:half, lanes] = top
        y[half:, lanes] = bottom
        return carry

    lax.fori_loop(0, inner // LANES, pair, 0, unroll=6)


def output_kernel(
    place, c_ref, keep, gate, gout, conv, rw, st, wide, *refs
):
    refs, (out_low, ggate, gscan, rowside, gread, states, d_ref, pay, sums, so_ref, d_all) = refs[:-11], refs[-11:]
    near, far, y = refs[:HALVES], refs[HALVES : 2 * HALVES], refs[2 * HALVES :]
    tokens, inner = conv.shape
    blocks = tokens // BLOCK
    tiles = inner // TILE
    heads = TILE // HEAD_DIM
    span = inner // HALVES
    for part in range(HALVES):
        lanes = slice(part * span, (part + 1) * span)
        now = entering(near[part], far[part])
        for b in range(blocks):
            if b > 0:
                wide_keep = expand(keep[b - 1 : b], part * span // HEAD_DIM, span // HEAD_DIM)
                now = now * wide_keep + c_ref[b - 1, :, lanes]
            states[b, :, lanes] = now.astype(BF)
    sums[...] = jnp.zeros_like(sums)
    d_all[...] = jnp.zeros_like(d_all)

    def chunk(r, carry):
        rows = pl.ds(pl.multiple_of(r * ROWS, ROWS), ROWS)
        b = r // (BLOCK // ROWS)
        inside = pl.ds(pl.multiple_of(r % (BLOCK // ROWS) * ROWS, ROWS), ROWS)
        read = rw[rows, STATE:]
        scale = st[4, rows, :]
        total = jnp.zeros((ROWS, 1), F32)
        cross = jnp.zeros((ROWS, 1), F32)
        for tile in range(tiles):
            lanes = slice(tile * TILE, (tile + 1) * TILE)
            raw = dot(read, states[b, :, lanes])
            own = y[0][inside, lanes]
            for n in range(1, blocks):
                own = jnp.where(b == n, y[n][inside, lanes], own)
            so = own + raw * expand(scale, tile * heads, heads)
            so_ref[:, lanes] = so
            c = conv[rows, lanes].astype(F32)
            u = so + wide[1:2, lanes] * (c * sigmoid(c))
            g = gate[rows, lanes].astype(F32)
            gated = u * (g * sigmoid(g))
            total = total + jnp.sum(gated * gated, axis=1, keepdims=True)
            go = gout[rows, lanes].astype(F32) * wide[0:1, lanes]
            cross = cross + jnp.sum(go * gated, axis=1, keepdims=True)
        rms = lax.rsqrt(total / inner + EPS)
        cube = rms * rms * rms * (cross / inner)
        side = jnp.zeros((ROWS, LANES), F32)
        read_grad = jnp.zeros((ROWS, STATE), F32)
        for tile in range(tiles):
            lanes = slice(tile * TILE, (tile + 1) * TILE)
            so = so_ref[:, lanes]
            c = conv[rows, lanes].astype(F32)
            act = c * sigmoid(c)
            u = so + wide[1:2, lanes] * act
            g = gate[rows, lanes].astype(F32)
            sg = sigmoid(g)
            silu = g * sg
            gated = u * silu
            gain = wide[0:1, lanes]
            out = gated * rms
            out_low[rows, lanes] = (out * gain).astype(BF)
            go = gout[rows, lanes].astype(F32)
            gg = go * gain * rms - gated * cube
            q = gg * silu
            ggate[rows, lanes] = (gg * u * (sg * (1.0 + g * (1.0 - sg)))).astype(BF)
            low = q.astype(BF)
            gscan[rows, lanes] = low
            low = low.astype(F32)
            sums[0:1, lanes] += jnp.sum(go * out, axis=0, keepdims=True)
            sums[1:2, lanes] += jnp.sum(q * act, axis=0, keepdims=True)
            side = side + head_sum(low * so, head_matrix(tile * heads, TILE))
            scaled = (low * expand(scale, tile * heads, heads)).astype(BF)
            d_all[b, :, lanes] += dot_tn(read, scaled)
            read_grad = read_grad + dot_nt(scaled, states[b, :, lanes])
        rowside[rows, :] = side
        gread[rows, :] = read_grad
        return carry

    lax.fori_loop(0, tokens // ROWS, chunk, 0)
    for b in range(1, blocks):
        d_ref[b - 1] = d_all[b]
    total = d_all[blocks - 1]
    whole = keep[blocks - 1 : blocks]
    for b in range(blocks - 2, -1, -1):
        total = d_all[b] + expand(keep[b : b + 1], 0, inner // HEAD_DIM) * total
        whole = whole * keep[b : b + 1]
    pay[:STATE] = total.astype(BF)
    index = lax.broadcasted_iota(jnp.int32, (HALO, inner), 0)
    wide_keep = expand(whole, 0, inner // HEAD_DIM)
    hi = wide_keep.astype(BF).astype(F32)
    pay[STATE:] = jnp.where(index == 0, hi, jnp.where(index == 1, wide_keep - hi, 0.0)).astype(BF)


def gate_grad_kernel(place, normed, cot, out_low, ggate, tok, *refs):
    (mixed, gn), refs = refs[-9:-7], refs[:-9] + refs[-7:]
    weights, (out_a, out_b, gwg, gwo, wg, wo, sems) = refs[:-7], refs[-7:]
    load_weights(place, weights, (wg, wo), sems)
    inner = out_low.shape[1]
    low = normed[HALO:, :]
    for tile in range(inner // TILE):
        lanes = slice(tile * TILE, (tile + 1) * TILE)
        gwo[:, lanes] = dot_tn(cot[...], out_low[:, lanes]).astype(BF)
        gwg[:, lanes] = dot_tn(low, ggate[:, lanes]).astype(BF)
    wait_weights((wg, wo), sems)
    gn[...] = dot_nt(ggate[...], wg[...])
    mixed[...] = (tok[HALO:, :].astype(F32) + dot_nt(out_low[...], wo[...])).astype(BF)
    store_grads(place, (gwg, gwo), (out_a, out_b), sems)


def scan_grad_kernel(b, place, gscan, conv, st, rw, seg_col, seg_row, z, colside, gentry, gread, smask, acc, cum_t):
    inner = conv.shape[1]
    half = BLOCK // 2
    j, i = lower_matrix()
    lane = lax.broadcasted_iota(jnp.int32, (BLOCK, LANES), 1)
    rows = slice(b * BLOCK, (b + 1) * BLOCK)
    same = (i >= j) & (seg_col[rows, 0:1] == seg_row[0:1, rows])
    scores = dot_nt(rw[rows, :STATE], rw[rows, STATE:])
    smask[...] = jnp.where(same, scores, 0.0)
    cum_t[...] = st[2, rows].T
    acc[...] = jnp.zeros_like(acc)
    colside[...] = jnp.zeros((BLOCK, LANES), F32)

    def pair(p, carry):
        cum = pltpu.roll(st[2, rows], LANES - 2 * p, 1)
        step = pltpu.roll(st[1, rows], LANES - 2 * p, 1)
        lanes = pl.ds(pl.multiple_of(p * LANES, LANES), LANES)
        c = conv[rows, lanes].astype(F32)
        act = (c * sigmoid(c)).astype(BF).astype(F32)
        xs = (act * jnp.where(lane < HEAD_DIM, step[:, 0:1], step[:, 1:2])).astype(BF)
        gs = gscan[rows, lanes]
        gs_t = gs.T
        top = jnp.zeros((half, LANES), F32)
        bottom = jnp.zeros((half, LANES), F32)
        for a in range(2):
            keep = (lane < HEAD_DIM) == (a == 0)
            mine = jnp.where(keep, xs, jnp.zeros_like(xs))
            grad = jnp.where(keep, gs, jnp.zeros_like(gs))
            row = cum_t[pl.ds(2 * p + a, 1), :]
            e = jnp.exp(jnp.minimum(row - cum[:half, a : a + 1], 0.0))
            top = top + dot((smask[:half, :] * e).astype(BF), grad)
            acc[:half, :] += dot(mine[:half], gs_t) * e
            e = jnp.exp(jnp.minimum(row[:, half:] - cum[half:, a : a + 1], 0.0))
            bottom = bottom + dot((smask[half:, half:] * e).astype(BF), grad[half:])
            acc[half:, half:] += dot(mine[half:], gs_t[:, half:]) * e
        both = jnp.concatenate([top, bottom], axis=0)
        z[:, lanes] = both
        channel = lax.broadcasted_iota(jnp.int32, (LANES, LANES), 0)
        head = lax.broadcasted_iota(jnp.int32, (LANES, LANES), 1)
        matrix = (channel // HEAD_DIM + 2 * p == head).astype(BF)
        colside[...] += head_sum(both * xs.astype(F32), matrix)
        return carry

    lax.fori_loop(0, inner // LANES, pair, 0, unroll=6)
    low = jnp.where(same, acc[...], 0.0).astype(BF)
    gentry[...] = dot(low, rw[rows, STATE:])
    gread[...] = dot_tn(low, rw[rows, :STATE])


def input_grad_kernel(
    place, near, far, d_ref, keep, states, conv, pre, gscan, st, rw, sconv, spre, rowside, gread_a, taps,
    taps_state, par, wide, cols, *refs
):
    by_block, (low_inner, low_state, low_step, sums, sums_state, sums_head, gstates) = refs[:-7], refs[-7:]
    z, colside, gentry, gread_b = [
        jnp.concatenate([ref[...] for ref in by_block[n::4]], axis=0) if n else by_block[n::4] for n in range(4)
    ]
    tokens, inner = conv.shape
    blocks = tokens // BLOCK
    tiles = inner // TILE
    heads = TILE // HEAD_DIM
    col = cols[...]
    now = entering(near, far)
    keep_grads = [None] * blocks
    whole_matrix = head_matrix(0, inner)
    for b in range(blocks - 1, -1, -1):
        gstates[b] = now.astype(BF)
        sum_row = jnp.sum(now * states[b].astype(F32), axis=0, keepdims=True)
        keep_grads[b] = head_sum(jnp.broadcast_to(sum_row, (8, inner)), whole_matrix)[0:1]
        if b > 0:
            now = d_ref[b - 1] + expand(keep[b : b + 1], 0, inner // HEAD_DIM) * now
    step_grad = jnp.zeros((tokens, LANES), F32)
    out_side = jnp.zeros((tokens, LANES), F32)
    entry_grad = gentry
    for tile in range(tiles):
        lanes = slice(tile * TILE, (tile + 1) * TILE)
        first = tile * heads
        matrix = head_matrix(first, TILE)
        c = conv[:, lanes].astype(F32)
        sg = sigmoid(c)
        act = (c * sg).astype(BF).astype(F32)
        step = expand(st[1], first, heads)
        out = expand(st[3], first, heads)
        scaled = (act * (step * out)).astype(BF)
        grads = []
        entries = []
        for b in range(blocks):
            rows = slice(b * BLOCK, (b + 1) * BLOCK)
            grads.append(dot(rw[rows, :STATE], gstates[b, :, lanes]))
            entries.append(dot_nt(scaled[rows], gstates[b, :, lanes]))
        grad_scaled = jnp.concatenate(grads, axis=0)
        entry_grad = entry_grad + jnp.concatenate(entries, axis=0)
        w = jnp.concatenate([ref[:, lanes] for ref in z], axis=0) + out * grad_scaled
        step_grad = step_grad + head_sum(act * w, matrix)
        out_side = out_side + head_sum(scaled.astype(F32) * grad_scaled, matrix)
        grad = wide[1:2, lanes] * gscan[:, lanes].astype(F32) + step * w
        grad = grad * (sg * (1.0 + c * (1.0 - sg)))
        back, rows_sum = conv_backward(grad, pre[:, lanes].astype(F32), taps[:, lanes], col)
        low = back.astype(BF)
        low_inner[:, lanes] = low
        sums[:, lanes] = put_rows(rows_sum, TILE)
    sc = sconv[...]
    sg = sigmoid(sc)
    grad = jnp.concatenate([entry_grad, gread_a[...] + gread_b], axis=1)
    grad = grad * (sg * (1.0 + sc * (1.0 - sg)))
    back, rows_sum = conv_backward(grad, spre[...], taps_state, col)
    low = back.astype(BF)
    low_state[...] = low
    sums_state[...] = put_rows(rows_sum, 2 * STATE)
    i, j = lower_matrix()
    upper = (i <= j).astype(F32)
    at_end = lax.broadcasted_iota(jnp.int32, (BLOCK, LANES), 0) == BLOCK - 1
    decays = []
    for b in range(blocks):
        rows = slice(b * BLOCK, (b + 1) * BLOCK)
        side = out_side[rows]
        last = jnp.sum(side, axis=0, keepdims=True) + keep_grads[b] * keep[b : b + 1]
        cum_grad = rowside[rows, :] - colside[rows] - side + jnp.where(at_end, last, 0.0)
        decays.append(dot_high(upper, cum_grad))
    decay_grad = jnp.concatenate(decays, axis=0)
    rate = par[1:2]
    step_grad = (step_grad + decay_grad * rate) * sigmoid(st[0])
    rows_head = [
        jnp.sum(step_grad, axis=0, keepdims=True),
        jnp.sum(decay_grad * st[1] * rate, axis=0, keepdims=True),
    ]
    sums_head[...] = put_rows(rows_head, LANES)
    low = jnp.concatenate([jnp.zeros((HALO, LANES), F32), step_grad], axis=0).astype(BF)
    low_step[...] = low


def weight_grad_kernel(place, normed, low_inner, low_state, low_step, *refs):
    grad_outs, (gwi, gws, gwp, sems) = refs[:-4], refs[-4:]
    x = normed[...]
    for tile in range(low_inner.shape[1] // TILE):
        lanes = slice(tile * TILE, (tile + 1) * TILE)
        gwi[:, lanes] = dot_tn(x, low_inner[:, lanes]).astype(BF)
    gws[...] = dot_tn(x, low_state[...]).astype(BF)
    gwp[...] = dot_tn(x, low_step[...]).astype(BF)
    store_grads(place, (gwi, gws, gwp), grad_outs, sems)


def token_grad_kernel(
    place, low_inner, low_state, low_step, gn_gate, tok, cot, gain, sums_in, sums_out, sums_state, sums_head, *refs
):
    weights, (grad, back, pack, win, wst, wsp, sems) = refs[:-7], refs[-7:]
    load_weights(place, weights, (win, wst, wsp), sems)
    wait_weights((win, wst, wsp), sems)
    width = tok.shape[1]
    gn = dot_nt(low_inner[...], win[...]) + dot_nt(low_state[...], wst[...])
    gn = gn + dot_nt(low_step[...], wsp[...])
    gn = gn + jnp.concatenate([jnp.zeros((HALO, width), F32), gn_gate[...]], axis=0)
    t = tok[...].astype(F32)
    r = lax.rsqrt(jnp.mean(t * t, axis=1, keepdims=True) + EPS)
    scaled = t * r
    inner = pack.shape[1]
    pack[0 : KW + 1, :] = sums_in[: KW + 1]
    pack[KW + 1 : KW + 2, :] = sums_out[0:1]
    pack[KW + 2 :, :] = jnp.zeros((8 - KW - 2, inner), F32)
    pack[KW + 2 : KW + 3, :width] = jnp.sum(gn * scaled, axis=0, keepdims=True)
    pack[KW + 2 : KW + 3, width : width + LANES] = sums_head[0:1]
    pack[KW + 2 : KW + 3, width + LANES : width + 2 * LANES] = sums_head[1:2]
    skips = head_sum(sums_out[...], head_matrix(0, inner))
    pack[KW + 2 : KW + 3, width + 2 * LANES : width + 3 * LANES] = skips[1:2]
    for k in range(KW + 1):
        pack[KW + 3 : KW + 4, 2 * STATE * k : 2 * STATE * (k + 1)] = sums_state[k : k + 1]
    gg = gn * gain[0:1]
    result = gg * r - t * (r * r * r * jnp.mean(gg * t, axis=1, keepdims=True))
    back[...] = result[:HALO]
    grad[...] = result[HALO:] + cot[...].astype(F32)


def finish_kernel(place, a, b, c, d, inner, state, step, conv, conv_state, norm, gain, *heads):
    depth, span = inner.shape
    per = span // HEAD_DIM

    def total(first, count):
        rows = slice(first, first + count)
        return a[rows].astype(F32) + b[rows].astype(F32) + c[rows].astype(F32) + d[rows].astype(F32)

    inner[...] = total(0, depth)
    last = total(depth, depth)
    state[...] = last[:, : 2 * STATE]
    turn_heads = lax.rem(LANES - place[1] * per, LANES)
    step[...] = pltpu.roll(last[:, 2 * STATE :], turn_heads, 1)[:, :per]
    small = total(2 * depth, 2 * 8)
    conv[...] = small[: KW + 1]
    gain[...] = small[KW + 1]
    whole = [
        jnp.concatenate([small[8 + 2 * q + n : 9 + 2 * q + n] for q in range(4)], axis=1) for n in range(2)
    ]
    width = norm.shape[0]
    norm[...] = whole[0][0, :width]
    rows = [whole[1][:, 2 * STATE * k : 2 * STATE * (k + 1)] for k in range(KW + 1)]
    conv_state[...] = put_rows(rows, 2 * STATE)[: KW + 1]
    rows = [whole[0][:, width + LANES * n : width + LANES * (n + 1)] for n in range(3)]
    rows = pltpu.roll(put_rows(rows, LANES), turn_heads, 1)
    for n, head in enumerate(heads):
        head[...] = rows[n, :per]


def line(shift, size):
    return [(i, i + shift) for i in range(size) if 0 <= i + shift < size]


def pass_first(payload, size, sign):
    return lax.ppermute(payload, "tensor", line(sign, size))


def pass_states(payload, came, size, sign, first=()):
    own = payload[:STATE].astype(F32)
    factor = payload[STATE].astype(F32) + payload[STATE + 1].astype(F32)
    near, far, send = came, jnp.zeros_like(came[:STATE]), came
    reach = 2
    while reach < size:
        near_factor = near[STATE].astype(F32) + near[STATE + 1].astype(F32)
        total = near[:STATE].astype(F32)
        if reach > 2:
            total = total + last_factor[None] * far[:STATE].astype(F32)
        send = (own + factor[None] * total).astype(BF)
        if 2 * reach < size:
            both = factor * near_factor
            hi = both.astype(BF)
            lo = (both - hi.astype(F32)).astype(BF)
            send = jnp.concatenate([send, hi[None], lo[None]], axis=0)
        send = after(send, *first)
        far = lax.ppermute(send, "tensor", line(sign * reach, size))
        last_factor = near_factor
        if 2 * reach < size:
            total = near[:STATE].astype(F32) + near_factor[None] * far[:STATE].astype(F32)
            both = near_factor * (far[STATE].astype(F32) + far[STATE + 1].astype(F32))
            hi = both.astype(BF)
            lo = (both - hi.astype(F32)).astype(BF)
            near = jnp.concatenate([total.astype(BF), hi[None], lo[None]], axis=0)
            near = jnp.pad(near, ((0, HALO - 2), (0, 0)))
            far = jnp.zeros_like(far)
        reach = 2 * reach
    return near, far[:STATE], send


def entering(near, far):
    rows = near[STATE:, :].astype(F32)
    return near[:STATE, :].astype(F32) + (rows[0:1] + rows[1:2]) * far[...].astype(F32)


def swap(values, mask):
    return lax.ppermute(values, "dp", [(i, i ^ mask) for i in range(8)])


def turn(values, shift):
    return lax.ppermute(values, "tensor", [(i, (i + shift) % 4) for i in range(4)])


def cross(values, mask):
    return lax.ppermute(values, "tensor", [(i, i ^ mask) for i in range(4)])


def ring(values):
    return [values] + [turn(values, -m) for m in range(1, 4)]


def gather_plane(column):
    return [column] + [swap(column, k) for k in ORDER[1:4]]


def gather_cores(same, first=()):
    return same + [swap(after(v, *first), 1) for v in same]


def sum_pair_kernel(place, mine, came, *outs):
    for n, out in enumerate(outs):
        out[...] = mine[n] + came[n]


def sum_pair_pack_kernel(place, mine, came, pack, came_pack, *outs):
    slots, depth, span = mine.shape[1:]
    total = pack[...] + came_pack[...]
    rows = jnp.concatenate([total[:, q * span : (q + 1) * span] for q in range(4)], axis=0).astype(BF)
    for n, out in enumerate(outs):
        for m in range(slots):
            out[m * depth : (m + 1) * depth, :] = mine[n, m] + came[n, m]
        out[slots * depth :, :] = rows


def sum_column_pack_kernel(place, a, b, c, d, *refs):
    outs, rows = refs[:4], refs[4]
    depth = (a.shape[0] - 32) // 5

    def total(first, count):
        part = slice(first, first + count)
        return a[part].astype(F32) + b[part].astype(F32) + c[part].astype(F32) + d[part].astype(F32)

    rows[...] = total(5 * depth, 32)
    last = total(4 * depth, depth).astype(BF)
    rest = jnp.concatenate([rows[8 * q + KW + 2 : 8 * q + KW + 4] for q in range(4)], axis=0)
    for m, out in enumerate(outs):
        out[:depth, :] = total(m * depth, depth).astype(BF)
        out[depth : 2 * depth, :] = last
        own = rows[pl.ds(aligned((place[1] + m) % 4, 8), 8), :]
        out[2 * depth :, :] = jnp.concatenate([own, rest], axis=0).astype(BF)


def sum_column_kernel(place, a, b, c, d, *outs):
    for m, out in enumerate(outs):
        total = a[m].astype(F32) + b[m].astype(F32) + c[m].astype(F32) + d[m].astype(F32)
        out[...] = total.astype(BF)


def sum_last_kernel(place, a, b, c, d, first, second):
    for n, out in enumerate((first, second)):
        out[...] = a[n].astype(F32) + b[n].astype(F32) + c[n].astype(F32) + d[n].astype(F32)


def reduce_core(where, mine, other):
    came = swap(other, 1)
    return call(sum_pair_kernel, [sds(mine.shape[1:], BF)] * 4, (where, mine, came), name="sum_pair")


def reduce_plane(where, parts):
    came = [swap(parts[n], ORDER[n]) for n in range(1, 4)]
    shape = (2, *parts[0].shape[-2:])
    return call(sum_column_kernel, [sds(shape, BF)] * 4, (where, parts[0], *came), name="sum_column")


def reduce_line(where, parts):
    came = [turn(parts[m], m) for m in range(1, 4)]
    return call(
        sum_last_kernel, [sds(parts[0].shape[1:], F32)] * 2, (where, parts[0], *came), name="sum_last"
    )


def after_all(values, *others):
    return lax.optimization_barrier((*values, *others))[: len(values)]


def after(value, *others):
    return lax.optimization_barrier((value, *others))[0]


def gather(shard):
    return lax.all_gather(
        lax.all_gather(shard, "tensor", axis=1, tiled=True), "dp", axis=0, tiled=True
    )


def scatter(grad):
    part = lax.psum_scatter(grad, "dp", scatter_dimension=0, tiled=True)
    return lax.psum_scatter(part, "tensor", scatter_dimension=1, tiled=True).astype(F32)


def make_shards(mesh):
    size = mesh.shape["tensor"]
    blocked = size == 4 and mesh.shape["dp"] == 8

    def shards(
        tokens, segments, cotangent, norm_gain, w_gate, w_inner, w_step, w_state, conv_inner, conv_state,
        step_bias, decay_log, skip_gain, out_gain, w_out,
    ):
        count, width = tokens.shape
        place = lax.axis_index("tensor")
        blocks = count // BLOCK
        inner = w_inner.shape[1] * size
        heads = w_step.shape[1] * size

        halo = lax.ppermute(tokens[count - HALO :], "tensor", line(1, size))
        tok = jnp.concatenate([halo, tokens], axis=0)
        wide_tok = tok.astype(F32)
        gain = norm_gain.astype(F32)
        rms = lax.rsqrt(jnp.mean(wide_tok * wide_tok, axis=1, keepdims=True) + EPS)
        normed = (wide_tok * rms * gain).astype(BF)

        padded = jnp.concatenate([jnp.full((HALO,), -1, jnp.int32), segments])
        near = lax.dynamic_slice(padded, (place * count,), (HALO + count,))
        seg = near[HALO:]
        masks = [near[HALO - k : HALO - k + count] == seg for k in range(1, KW)]
        grid = seg.reshape(blocks, BLOCK)
        prev = near[HALO - 1 : HALO - 1 + count].reshape(blocks, BLOCK)[:, :1]
        from_prev = (grid == prev).reshape(-1)
        at_last = (grid == grid[:, BLOCK - 1 :]).reshape(-1)
        cols = jnp.stack([*masks, from_prev, at_last], axis=1).astype(F32)
        seg_col = seg.astype(F32)[:, None]
        seg_row = seg.astype(F32)[None]

        def pad_heads(row):
            return jnp.pad(row, ((0, 0), (0, LANES - heads)))

        where = jnp.stack([lax.axis_index("dp"), place]).astype(jnp.int32)
        depth, span = w_inner.shape
        per = heads // size
        if blocked:
            tall = HALO + depth

            def place_at(block, row, lane):
                rows = (row, tall - row - block.shape[0])
                return jnp.pad(block, (rows, (lane, span - lane - block.shape[1])))

            pack = place_at(w_inner, 0, 0) + place_at(w_step.T, depth + KW + 3, 0)
            pack = pack + place_at(conv_inner, depth, 0) + place_at(out_gain[None], depth + KW + 1, 0)
            for n, row in enumerate((step_bias, decay_log, skip_gain)):
                pack = pack + place_at(row[None], depth + KW + 2, n * per)
            came = ring(pack)
            pair_out = jnp.stack([w_gate, w_out])[None]
            pair_out = jnp.concatenate([pair_out, cross(pair_out, 1)])
            came_out = jnp.concatenate([pair_out, cross(pair_out, 2)])

            column, taps, par, wide = call(
                unpack_kernel,
                [
                    sds((5, depth, span), BF),
                    sds((8, inner), F32),
                    sds((8, LANES), F32),
                    sds((8, inner), F32),
                ],
                (where, *came, w_state),
                name="unpack",
            )
            same = gather_plane(column)
            pieces = gather_cores(same, (came_out,))
            same_out = gather_plane(after(came_out, *same[1:]))
        else:
            conv_whole, head_whole, gain_whole = [
                lax.all_gather(v, "tensor", axis=v.ndim - 1, tiled=True).astype(F32)
                for v in (conv_inner, jnp.stack([step_bias, decay_log, skip_gain]), out_gain)
            ]
            pieces = [gather(w_inner), lax.all_gather(w_state, "dp", axis=0, tiled=True), pad_heads(gather(w_step))]
            pieces_out = [gather(w_gate), gather(w_out)]
            taps = jnp.pad(conv_whole, ((0, 8 - KW - 1), (0, 0)))
            bias, rate, skip = head_whole[0], -jnp.exp(head_whole[1]), head_whole[2]
            par = pad_heads(jnp.pad(jnp.stack([bias, rate]), ((0, 6), (0, 0))))
            wide = jnp.pad(jnp.stack([gain_whole, jnp.repeat(skip, HEAD_DIM)]), ((0, 6), (0, 0)))
        taps_state = jnp.pad(conv_state.astype(F32), ((0, 8 - KW - 1), (0, 0)))
        in_scratch = [
            pltpu.VMEM((width, inner), BF),
            pltpu.VMEM((width, 2 * STATE), BF),
            pltpu.VMEM((width, LANES), BF),
            pltpu.SemaphoreType.DMA((3,)),
        ]
        out_scratch = [
            pltpu.VMEM((width, inner), BF),
            pltpu.VMEM((width, inner), BF),
            pltpu.SemaphoreType.DMA((2,)),
        ]

        def last_args(fixed, arrays):
            return {"args": (where, *fixed, *arrays), "far": range(1 + len(fixed), 1 + len(fixed) + len(arrays))}

        pre, conv, spre, sconv, rw, st, keep, c_ref, *pays = call(
            project_kernel,
            [
                sds((HALO + count, inner), BF),
                sds((count, inner), F32),
                sds((HALO + count, 2 * STATE), F32),
                sds((count, 2 * STATE), F32),
                sds((count, 2 * STATE), BF),
                sds((5, count, LANES), F32),
                sds((8, LANES), F32),
                sds((max(1, blocks - 1), STATE, inner), F32),
                *[sds((STATE + HALO, inner // HALVES), BF)] * HALVES,
            ],
            scratch=in_scratch,
            **last_args((normed, taps, taps_state, par, cols), pieces),
            name="project",
            micros=9.5,
        )
        came_pays = [pass_first(pay, size, 1) for pay in pays]
        enter = []
        y = []
        for b in range(blocks):
            y += call(
                functools.partial(scan_kernel, b),
                [sds((BLOCK, inner), F32)],
                (where, conv if b == 0 else after(conv, enter[-1][2], *came_pays), st, rw, seg_col, seg_row),
                [pltpu.VMEM((BLOCK, BLOCK), F32), pltpu.VMEM((LANES, BLOCK), F32)],
                name=f"scan_{b}",
                micros=5,
            )
            if b < HALVES:
                enter.append(pass_states(pays[b], came_pays[b], size, 1, (y[-1],)))
        for part in range(len(enter), HALVES):
            enter.append(pass_states(pays[part], came_pays[part], size, 1))
        near, far, sent = [list(v) for v in zip(*enter)]
        if blocked:
            pieces_out = gather_cores(same_out, (far[0], sent[-1]))
        gate, gout = call(
            gate_kernel,
            [sds((count, inner), F32)] * 2,
            scratch=out_scratch,
            **last_args((after(normed, sent[-1]), cotangent), pieces_out),
            name="gate",
            micros=4,
        )
        out_low, ggate, gscan, rowside, gread_a, states, d_ref, pay, sums = call(
            output_kernel,
            [
                sds((count, inner), BF),
                sds((count, inner), BF),
                sds((count, inner), BF),
                sds((count, LANES), F32),
                sds((count, STATE), F32),
                sds((blocks, STATE, inner), BF),
                sds((max(1, blocks - 1), STATE, inner), F32),
                sds((STATE + HALO, inner), BF),
                sds((8, inner), F32),
            ],
            (where, c_ref, keep, gate, gout, conv, rw, st, wide, *near, *far, *y),
            [pltpu.VMEM((ROWS, inner), F32), pltpu.VMEM((blocks, STATE, inner), F32)],
            name="output",
            micros=9.5,
        )
        if blocked:
            shapes_out = [sds((4, 4, 2, depth, span), BF)] * 2
            shapes_in = [sds((4, 5, depth, span), BF)] * 2
        else:
            shapes_out = [sds((width, inner), BF)] * 2
            shapes_in = [sds((width, inner), BF), sds((width, 2 * STATE), BF), sds((width, LANES), BF)]
        mixed, gn_gate, *grads_out = call(
            gate_grad_kernel,
            [sds((count, width), BF), sds((count, width), F32), *shapes_out],
            far_outs=(2, 3),
            scratch=[
                pltpu.VMEM((width, inner), BF),
                pltpu.VMEM((width, inner), BF),
                *out_scratch,
            ],
            **last_args((normed, cotangent, out_low, ggate, tok), pieces_out),
            name="gate_grad",
            micros=8.3,
        )
        came_pay = pass_first(pay, size, -1)
        if blocked:
            mine_out, other_out = grads_out
            parts_out = reduce_core(where, mine_out, after(other_out, came_pay))
        else:
            parts_out = ()
        *leave, sent = pass_states(pay, came_pay, size, -1)
        by_block = [
            call(
                functools.partial(scan_grad_kernel, b),
                [sds((BLOCK, inner), F32), sds((BLOCK, LANES), F32), *[sds((BLOCK, STATE), F32)] * 2],
                (where, after(gscan, sent, *parts_out), conv, st, rw, seg_col, seg_row),
                [
                    pltpu.VMEM((BLOCK, BLOCK), F32),
                    pltpu.VMEM((BLOCK, BLOCK), F32),
                    pltpu.VMEM((LANES, BLOCK), F32),
                ],
                name=f"scan_grad_{b}",
                micros=9,
            )
            for b in range(blocks)
        ]
        low_inner, low_state, low_step, sums_in, sums_state, sums_head = call(
            input_grad_kernel,
            [
                sds((HALO + count, inner), BF),
                sds((HALO + count, 2 * STATE), BF),
                sds((HALO + count, LANES), BF),
                sds((8, inner), F32),
                sds((8, 2 * STATE), F32),
                sds((8, LANES), F32),
            ],
            (
                where, *leave, d_ref, keep, states, conv, pre, gscan, st, rw, sconv, spre, rowside, gread_a, taps,
                taps_state, par, wide, cols, *[v for part in by_block for v in part],
            ),
            [pltpu.VMEM((blocks, STATE, inner), BF)],
            name="input_grad",
            micros=9,
        )
        low_next = low_inner
        if blocked:
            lines_out = reduce_plane(where, parts_out)
            low_next = after(low_inner, *lines_out)
        grads_in = call(
            weight_grad_kernel,
            shapes_in,
            (where, normed, low_next, low_state, low_step),
            scratch=in_scratch,
            far_outs=range(len(shapes_in)),
            name="weight_grad",
            micros=5,
        )
        if blocked:
            mine_in, other_in = grads_in
            came_in = swap(other_in, 1)
            low_inner = after(low_inner, other_in)
        grad, back, pack = call(
            token_grad_kernel,
            [sds((count, width), F32), sds((HALO, width), F32), sds((8, inner), F32)],
            scratch=in_scratch,
            **last_args((low_inner, low_state, low_step, gn_gate, tok, cotangent, gain[None], sums_in, sums, sums_state, sums_head), pieces),
            name="token_grad",
            micros=5,
        )
        if blocked:
            tall = 5 * depth + 32
            parts_in = call(
                sum_pair_pack_kernel,
                [sds((tall, span), BF)] * 4,
                (where, mine_in, came_in, pack, swap(pack, 1)),
                name="sum_pair_pack",
            )
            lines_out = after_all(lines_out, *parts_in)
            grad_gate, grad_out = reduce_line(where, lines_out)
        if blocked:
            came_in = [swap(parts_in[n], ORDER[n]) for n in range(1, 4)]
            lines_in = call(
                sum_column_pack_kernel,
                [sds((2 * depth + 2 * 8, span), BF)] * 4,
                (where, parts_in[0], *came_in),
                [pltpu.VMEM((32, span), F32)],
                name="sum_column_pack",
            )
            back = after(back, lines_in[0])
            grad_inner, grad_state, grad_step, grad_conv, grad_conv_state, norm, grad_gain, *head_grads = call(
                finish_kernel,
                [
                    sds((depth, span), F32),
                    sds((depth, 2 * STATE), F32),
                    sds((depth, per), F32),
                    sds((KW + 1, span), F32),
                    sds((KW + 1, 2 * STATE), F32),
                    sds((width,), F32),
                    sds((span,), F32),
                    *[sds((per,), F32)] * 3,
                ],
                (where, lines_in[0], *[turn(lines_in[m], m) for m in range(1, 4)]),
                name="finish",
            )
        else:
            pack = lax.psum(pack, ("dp", "tensor"))
            own = lax.dynamic_slice(pack, (0, place * span), (KW + 2, span))
            norm = pack[KW + 2, :width]
            grad_conv, grad_gain = own[: KW + 1], own[KW + 1]
            grad_conv_state = pack[KW + 3, : (KW + 1) * 2 * STATE].reshape(KW + 1, 2 * STATE)
            head_grads = [
                lax.dynamic_slice(pack[KW + 2], (width + LANES * n + place * per,), (per,)) for n in range(3)
            ]
            grad_gate, grad_out, grad_inner, grad_step = [
                scatter(v) for v in (*grads_out, grads_in[0], grads_in[2][:, :heads])
            ]
            grad_state = lax.psum_scatter(grads_in[1], "dp", scatter_dimension=0, tiled=True)
            grad_state = lax.psum(grad_state, "tensor").astype(F32)
        back = lax.ppermute(back, "tensor", line(-1, size))
        grad = grad.at[count - HALO :].add(back)
        return (
            mixed,
            grad,
            norm,
            grad_gate,
            grad_inner,
            grad_step,
            grad_state,
            grad_conv,
            grad_conv_state,
            *head_grads,
            grad_gain,
            grad_out,
        )

    return shards


def solution(mesh):
    in_specs = (
        P(("dp", "tensor"), None),
        P("dp"),
        P(("dp", "tensor"), None),
        P(),
        P("dp", "tensor"),
        P("dp", "tensor"),
        P("dp", "tensor"),
        P("dp", None),
        P(None, "tensor"),
        P(),
        P("tensor"),
        P("tensor"),
        P("tensor"),
        P("tensor"),
        P("dp", "tensor"),
    )
    out_specs = (
        P(("dp", "tensor"), None),
        P(("dp", "tensor"), None),
        P(),
        P("dp", "tensor"),
        P("dp", "tensor"),
        P("dp", "tensor"),
        P("dp", None),
        P(None, "tensor"),
        P(),
        P("tensor"),
        P("tensor"),
        P("tensor"),
        P("tensor"),
        P("dp", "tensor"),
    )
    return jax.shard_map(
        make_shards(mesh), mesh=mesh, in_specs=in_specs, out_specs=out_specs, check_vma=False
    )
```

```python
import functools
import math

import jax
import jax.numpy as jnp
from jax import lax
from jax.experimental import pallas as pl
from jax.experimental.pallas import tpu as pltpu
from jax.sharding import PartitionSpec as P

HEAD_DIM = 64
STATE = 128
KW = 4
BLOCK = 256
HALO = 16
LANES = 128
TILE = 256
SPAN = 384
ROWS = 128
HALVES = 2
EPS = 1e-05
F32 = jnp.float32
BF = jnp.bfloat16
HIGH = lax.Precision.HIGHEST
SPARE = 3 * 2**20
ORDER = (0, 2, 4, 6, 1, 3, 5, 7)


def dot(a, b):
    return lax.dot_general(a, b, (((1,), (0,)), ((), ())), preferred_element_type=F32)


def dot_nt(a, b):
    return lax.dot_general(a, b, (((1,), (1,)), ((), ())), preferred_element_type=F32)


def dot_tn(a, b):
    return lax.dot_general(a, b, (((0,), (0,)), ((), ())), preferred_element_type=F32)


def dot_high(a, b):
    return lax.dot_general(
        a, b, (((1,), (0,)), ((), ())), precision=HIGH, preferred_element_type=F32
    )


def sigmoid(x):
    return 0.5 * jnp.tanh(0.5 * x) + 0.5


def expand(x, first, count):
    lane = lax.broadcasted_iota(jnp.int32, (x.shape[0], LANES), 1)
    return jnp.concatenate(
        [
            jnp.where(lane < HEAD_DIM, x[:, h : h + 1], x[:, h + 1 : h + 2])
            for h in range(first, first + count, 2)
        ],
        axis=1,
    )


def halved(tile, inner, width):
    first = tile * width % (inner // HALVES)
    return tile * width // (inner // HALVES), slice(first, first + width)


def head_matrix(first, channels):
    channel = lax.broadcasted_iota(jnp.int32, (channels, LANES), 0)
    head = lax.broadcasted_iota(jnp.int32, (channels, LANES), 1)
    return (channel // HEAD_DIM + first == head).astype(BF)


def head_sum(x, matrix):
    hi = x.astype(BF)
    lo = (x - hi.astype(F32)).astype(BF)
    return dot(hi, matrix) + dot(lo, matrix)


def lower_matrix():
    i = lax.broadcasted_iota(jnp.int32, (BLOCK, BLOCK), 0)
    j = lax.broadcasted_iota(jnp.int32, (BLOCK, BLOCK), 1)
    return i, j


def conv_forward(values, taps, cols):
    result = taps[KW : KW + 1] + taps[0:1] * values[HALO:]
    for k in range(1, KW):
        result = result + taps[k : k + 1] * pltpu.roll(values, k, 0)[HALO:] * cols[:, k - 1 : k]
    return result


def conv_backward(grad, values, taps, cols):
    width = grad.shape[1]
    whole = HALO + grad.shape[0]
    zero = jnp.zeros((HALO, width), F32)
    base = jnp.concatenate([zero, grad], axis=0)
    result = taps[0:1] * base
    sums = [jnp.sum(grad * values[HALO:], axis=0, keepdims=True)]
    for k in range(1, KW):
        masked = jnp.concatenate([zero, grad * cols[:, k - 1 : k]], axis=0)
        back = pltpu.roll(masked, whole - k, 0)
        result = result + taps[k : k + 1] * back
        sums.append(jnp.sum(back * values, axis=0, keepdims=True))
    sums.append(jnp.sum(grad, axis=0, keepdims=True))
    return result, sums


def put_rows(rows, width):
    index = lax.broadcasted_iota(jnp.int32, (8, width), 0)
    result = jnp.zeros((8, width), F32)
    for i, row in enumerate(rows):
        result = jnp.where(index == i, row, result)
    return result


def call(kernel, outs, args, scratch=(), name=None, micros=1.0, far=(), far_outs=()):
    size = 1 << 20

    held = [a for i, a in enumerate(args) if i > 0 and i not in far]
    held += [o for i, o in enumerate(outs) if i not in far_outs]
    limit = SPARE + sum(a.size * a.dtype.itemsize for a in held)
    for item in scratch:
        if len(item.shape) > 1:
            limit += math.prod(item.shape) * jnp.dtype(item.dtype).itemsize

    def spec(space):
        return pl.BlockSpec(memory_space=space)

    ins = [
        spec(pltpu.SMEM if i == 0 else pltpu.HBM if i in far else pltpu.VMEM) for i in range(len(args))
    ]
    return pl.pallas_call(
        kernel,
        out_shape=outs,
        in_specs=ins,
        out_specs=[spec(pl.ANY if i in far_outs else pltpu.VMEM) for i in range(len(outs))],
        scratch_shapes=list(scratch),
        compiler_params=pltpu.CompilerParams(vmem_limit_bytes=limit),
        cost_estimate=pl.CostEstimate(flops=int(micros * 1.15e9), bytes_accessed=size, transcendentals=0),
        name=name,
    )(*args)


def sds(shape, dtype):
    return jax.ShapeDtypeStruct(shape, dtype)


def aligned(value, size):
    return pl.multiple_of(value * size, size)


def load_weights(place, refs, targets, sems):
    if len(refs[0].shape) == 2:
        copies = [pltpu.make_async_copy(r, t, sems.at[n]) for n, (r, t) in enumerate(zip(refs, targets))]
        for copy in copies:
            copy.start()
        return
    split = refs[0].shape[0] == 5
    depth, span = refs[0].shape[-2:]
    for n, k in enumerate(ORDER):
        row = pl.ds(aligned(place[0] ^ k, depth), depth)
        for m in range(4):
            who = (place[1] + m) % 4 if split else place[1] ^ m
            column = pl.ds(aligned(who, span), span)
            for g in range(1 if split else 2):
                source = refs[n].at[m] if split else refs[n].at[m, g]
                pltpu.make_async_copy(source, targets[g].at[row, column], sems.at[g]).start()
        if split:
            wide = targets[1].shape[1]
            pltpu.make_async_copy(refs[n].at[4, :, :wide], targets[1].at[row, :], sems.at[1]).start()
            pltpu.make_async_copy(refs[n].at[4, :, wide:], targets[2].at[row, :], sems.at[2]).start()


def wait_weights(targets, sems):
    for n, target in enumerate(targets):
        pltpu.make_async_copy(target, target, sems.at[n]).wait()


def store_grads(place, sources, outs, sems):
    if len(outs[0].shape) == 2:
        copies = [pltpu.make_async_copy(s, o, sems.at[n]) for n, (s, o) in enumerate(zip(sources, outs))]
        for copy in copies:
            copy.start()
    else:
        split = outs[0].shape[1] == 5
        depth, span = outs[0].shape[-2:]
        for n, k in enumerate(ORDER):
            out = outs[n // 4].at[n % 4]
            sem = sems.at[n // 4]
            row = pl.ds(aligned(place[0] ^ k, depth), depth)
            for m in range(4):
                column = pl.ds(aligned((place[1] + m) % 4, span), span)
                for g in range(1 if split else 2):
                    target = out.at[m] if split else out.at[m, g]
                    pltpu.make_async_copy(sources[g].at[row, column], target, sem).start()
            if split:
                wide = sources[1].shape[1]
                pltpu.make_async_copy(sources[1].at[row, :], out.at[4, :, :wide], sem).start()
                pltpu.make_async_copy(sources[2].at[row, :], out.at[4, :, wide:], sem).start()
    for n, out in enumerate(outs):
        pltpu.make_async_copy(out, out, sems.at[n]).wait()


def unpack_kernel(place, *refs):
    parts, (state, column, taps, par, wide) = refs[:4], refs[4:]
    depth, span = column.shape[1:]
    per = span // HEAD_DIM
    heads = wide.shape[1] // HEAD_DIM
    lane = lax.broadcasted_iota(jnp.int32, (8, LANES), 1)
    step = jnp.zeros((LANES, LANES), F32)
    rows = [jnp.zeros((8, LANES), F32)] * 3
    for m, part in enumerate(parts):
        who = (place[1] + m) % 4
        lanes = pl.ds(aligned(who, span), span)
        column[m] = part[:depth, :]
        low = part[depth:, :].astype(F32)
        tall = jnp.concatenate([low[:, :LANES], jnp.zeros((LANES - HALO, LANES), F32)], axis=0)
        tall = pltpu.roll(tall, LANES - KW - 3, 0)
        tall = jnp.where(lax.broadcasted_iota(jnp.int32, (LANES, LANES), 0) < per, tall, 0.0)
        step = step + pltpu.roll(tall, who * per, 0)
        taps[:, lanes] = low[:8]
        wide[0:1, lanes] = low[KW + 1 : KW + 2]
        row = jnp.broadcast_to(low[KW + 2 : KW + 3, :LANES], (8, LANES))
        for n in range(3):
            own = pltpu.roll(row, LANES - n * per, 1) if n else row
            rows[n] = rows[n] + pltpu.roll(jnp.where(lane < per, own, 0.0), who * per, 1)
    column[4] = jnp.concatenate([state[...], step.T[:depth].astype(BF)], axis=1)
    par[...] = put_rows([rows[0][0:1], jnp.where(lane < heads, -jnp.exp(rows[1]), 0.0)[0:1]], LANES)
    wide[1:2, :] = expand(rows[2], 0, heads)[0:1]


def project_kernel(
    place, *refs
):
    (normed, taps, taps_state, par, cols), refs = refs[:5], refs[5:]
    weights, refs = refs[: -12 - HALVES], refs[-12 - HALVES :]
    pre, conv, spre, sconv, rw, st, keep, c_ref, *pay, win, wst, wsp, sems = refs
    load_weights(place, weights, (win, wst, wsp), sems)
    wait_weights((win, wst, wsp), sems)
    project(normed, win, wst, wsp, taps, taps_state, par, cols, pre, conv, spre, sconv, rw, st, keep, c_ref, pay)


def project(
    normed, win, wst, wsp, taps, taps_state, par, cols, pre, conv, spre, sconv, rw, st, keep, c_ref, pay
):
    tokens = conv.shape[0]
    inner = conv.shape[1]
    blocks = tokens // BLOCK
    x = normed[...]
    low = x[HALO:]
    col = cols[...]
    sp = dot(low, wsp[...]) + par[0:1]
    step = jnp.maximum(sp, 0.0) + jnp.log1p(jnp.exp(-jnp.abs(sp)))
    decay = step * par[1:2]
    i, j = lower_matrix()
    lower = (i >= j).astype(F32)
    st[0] = sp
    st[1] = step
    keeps = []
    outs = []
    for b in range(blocks):
        rows = slice(b * BLOCK, (b + 1) * BLOCK)
        cum = dot_high(lower, decay[rows])
        last = cum[BLOCK - 1 : BLOCK]
        from_prev = col[rows, 3:4]
        out = jnp.exp(last - cum) * col[rows, 4:5]
        st[2, rows] = cum
        st[3, rows] = out
        st[4, rows] = jnp.exp(cum) * from_prev
        keeps.append(jnp.exp(last) * from_prev[BLOCK - 1 : BLOCK])
        outs.append(out * step[rows])
    keep[...] = put_rows(keeps, LANES)
    whole = keeps[0]
    for b in range(1, blocks):
        whole = whole * keeps[b]
    state = dot(x, wst[...])
    spre[...] = state
    sc = conv_forward(state, taps_state, col)
    sconv[...] = sc
    rw[...] = (sc * sigmoid(sc)).astype(BF)
    entry = rw[:, :STATE]
    index = lax.broadcasted_iota(jnp.int32, (HALO, SPAN), 0)
    for tile in range(inner // SPAN):
        lanes = slice(tile * SPAN, (tile + 1) * SPAN)
        heads = SPAN // HEAD_DIM
        first = tile * heads
        value = dot(x, win[:, lanes])
        pre[:, lanes] = value.astype(BF)
        c = conv_forward(value, taps[:, lanes], col)
        conv[:, lanes] = c
        c = c.astype(F32)
        act = (c * sigmoid(c)).astype(BF).astype(F32)
        total = None
        for b in range(blocks):
            rows = slice(b * BLOCK, (b + 1) * BLOCK)
            scaled = (act[rows] * expand(outs[b], first, heads)).astype(BF)
            part = dot_tn(entry[rows], scaled)
            if b < blocks - 1:
                c_ref[b, :, lanes] = part
            total = part if b == 0 else total * expand(keeps[b], first, heads) + part
        part, local = halved(tile, inner, SPAN)
        pay[part][:STATE, local] = total.astype(BF)
        wide = expand(whole, first, heads)
        hi = wide.astype(BF).astype(F32)
        pay[part][STATE:, local] = jnp.where(index == 0, hi, jnp.where(index == 1, wide - hi, 0.0)).astype(BF)


def gate_kernel(place, normed, cot, *refs):
    weights, (gate, gout, wg, wo, sems) = refs[:-5], refs[-5:]
    load_weights(place, weights, (wg, wo), sems)
    wait_weights((wg, wo), sems)
    for tile in range(gate.shape[1] // TILE):
        lanes = slice(tile * TILE, (tile + 1) * TILE)
        gate[:, lanes] = dot(normed[HALO:, :], wg[:, lanes])
        gout[:, lanes] = dot(cot[...], wo[:, lanes])


def scan_kernel(b, place, conv, st, rw, seg_col, seg_row, y, smask, cum_t):
    inner = conv.shape[1]
    half = BLOCK // 2
    i, j = lower_matrix()
    lane = lax.broadcasted_iota(jnp.int32, (BLOCK, LANES), 1)
    rows = slice(b * BLOCK, (b + 1) * BLOCK)
    scores = dot_nt(rw[rows, STATE:], rw[rows, :STATE])
    same = (i >= j) & (seg_col[rows, 0:1] == seg_row[0:1, rows])
    smask[...] = jnp.where(same, scores, 0.0)
    cum_t[...] = st[2, rows].T

    def pair(p, carry):
        cum = pltpu.roll(st[2, rows], lax.rem(LANES - 2 * p, LANES), 1)
        step = pltpu.roll(st[1, rows], lax.rem(LANES - 2 * p, LANES), 1)
        lanes = pl.ds(pl.multiple_of(p * LANES, LANES), LANES)
        c = conv[rows, lanes].astype(F32)
        act = (c * sigmoid(c)).astype(BF).astype(F32)
        xs = (act * jnp.where(lane < HEAD_DIM, step[:, 0:1], step[:, 1:2])).astype(BF)
        top = jnp.zeros((half, LANES), F32)
        bottom = jnp.zeros((half, LANES), F32)
        for a in range(2):
            mine = jnp.where((lane < HEAD_DIM) == (a == 0), xs, jnp.zeros_like(xs))
            row = cum_t[pl.ds(2 * p + a, 1), :]
            e = jnp.exp(jnp.minimum(cum[:half, a : a + 1] - row[:, :half], 0.0))
            top = top + dot((smask[:half, :half] * e).astype(BF), mine[:half])
            e = jnp.exp(jnp.minimum(cum[half:, a : a + 1] - row, 0.0))
            bottom = bottom + dot((smask[half:, :] * e).astype(BF), mine)
        y[:half, lanes] = top
        y[half:, lanes] = bottom
        return carry

    lax.fori_loop(0, inner // LANES, pair, 0, unroll=12)


def output_kernel(
    place, c_ref, keep, gate, gout, conv, rw, st, wide, *refs
):
    refs, (out_low, ggate, gscan, rowside, gread, states, d_ref, pay, sums, so_ref, d_all) = refs[:-11], refs[-11:]
    near, far, y = refs[:HALVES], refs[HALVES : 2 * HALVES], refs[2 * HALVES :]
    tokens, inner = conv.shape
    blocks = tokens // BLOCK
    tiles = inner // TILE
    heads = TILE // HEAD_DIM
    span = inner // HALVES
    for part in range(HALVES):
        lanes = slice(part * span, (part + 1) * span)
        now = entering(near[part], far[part])
        for b in range(blocks):
            if b > 0:
                wide_keep = expand(keep[b - 1 : b], part * span // HEAD_DIM, span // HEAD_DIM)
                now = now * wide_keep + c_ref[b - 1, :, lanes]
            states[b, :, lanes] = now.astype(BF)
    sums[...] = jnp.zeros_like(sums)
    d_all[...] = jnp.zeros_like(d_all)

    def chunk(r, carry):
        rows = pl.ds(pl.multiple_of(r * ROWS, ROWS), ROWS)
        b = r // (BLOCK // ROWS)
        inside = pl.ds(pl.multiple_of(r % (BLOCK // ROWS) * ROWS, ROWS), ROWS)
        read = rw[rows, STATE:]
        scale = st[4, rows, :]
        total = jnp.zeros((ROWS, 1), F32)
        cross = jnp.zeros((ROWS, 1), F32)
        for tile in range(tiles):
            lanes = slice(tile * TILE, (tile + 1) * TILE)
            raw = dot(read, states[b, :, lanes])
            own = y[0][inside, lanes]
            for n in range(1, blocks):
                own = jnp.where(b == n, y[n][inside, lanes], own)
            so = own + raw * expand(scale, tile * heads, heads)
            so_ref[:, lanes] = so
            c = conv[rows, lanes].astype(F32)
            u = so + wide[1:2, lanes] * (c * sigmoid(c))
            g = gate[rows, lanes].astype(F32)
            gated = u * (g * sigmoid(g))
            total = total + jnp.sum(gated * gated, axis=1, keepdims=True)
            go = gout[rows, lanes].astype(F32) * wide[0:1, lanes]
            cross = cross + jnp.sum(go * gated, axis=1, keepdims=True)
        rms = lax.rsqrt(total / inner + EPS)
        cube = rms * rms * rms * (cross / inner)
        side = jnp.zeros((ROWS, LANES), F32)
        read_grad = jnp.zeros((ROWS, STATE), F32)
        for tile in range(tiles):
            lanes = slice(tile * TILE, (tile + 1) * TILE)
            so = so_ref[:, lanes]
            c = conv[rows, lanes].astype(F32)
            act = c * sigmoid(c)
            u = so + wide[1:2, lanes] * act
            g = gate[rows, lanes].astype(F32)
            sg = sigmoid(g)
            silu = g * sg
            gated = u * silu
            gain = wide[0:1, lanes]
            out = gated * rms
            out_low[rows, lanes] = (out * gain).astype(BF)
            go = gout[rows, lanes].astype(F32)
            gg = go * gain * rms - gated * cube
            q = gg * silu
            ggate[rows, lanes] = (gg * u * (sg * (1.0 + g * (1.0 - sg)))).astype(BF)
            low = q.astype(BF)
            gscan[rows, lanes] = low
            low = low.astype(F32)
            sums[0:1, lanes] += jnp.sum(go * out, axis=0, keepdims=True)
            sums[1:2, lanes] += jnp.sum(q * act, axis=0, keepdims=True)
            side = side + head_sum(low * so, head_matrix(tile * heads, TILE))
            scaled = (low * expand(scale, tile * heads, heads)).astype(BF)
            d_all[b, :, lanes] += dot_tn(read, scaled)
            read_grad = read_grad + dot_nt(scaled, states[b, :, lanes])
        rowside[rows, :] = side
        gread[rows, :] = read_grad
        return carry

    lax.fori_loop(0, tokens // ROWS, chunk, 0)
    for b in range(1, blocks):
        d_ref[b - 1] = d_all[b]
    total = d_all[blocks - 1]
    whole = keep[blocks - 1 : blocks]
    for b in range(blocks - 2, -1, -1):
        total = d_all[b] + expand(keep[b : b + 1], 0, inner // HEAD_DIM) * total
        whole = whole * keep[b : b + 1]
    pay[:STATE] = total.astype(BF)
    index = lax.broadcasted_iota(jnp.int32, (HALO, inner), 0)
    wide_keep = expand(whole, 0, inner // HEAD_DIM)
    hi = wide_keep.astype(BF).astype(F32)
    pay[STATE:] = jnp.where(index == 0, hi, jnp.where(index == 1, wide_keep - hi, 0.0)).astype(BF)


def gate_grad_kernel(place, normed, cot, out_low, ggate, tok, *refs):
    (mixed, gn), refs = refs[-9:-7], refs[:-9] + refs[-7:]
    weights, (out_a, out_b, gwg, gwo, wg, wo, sems) = refs[:-7], refs[-7:]
    load_weights(place, weights, (wg, wo), sems)
    inner = out_low.shape[1]
    low = normed[HALO:, :]
    for tile in range(inner // TILE):
        lanes = slice(tile * TILE, (tile + 1) * TILE)
        gwo[:, lanes] = dot_tn(cot[...], out_low[:, lanes]).astype(BF)
        gwg[:, lanes] = dot_tn(low, ggate[:, lanes]).astype(BF)
    wait_weights((wg, wo), sems)
    gn[...] = dot_nt(ggate[...], wg[...])
    mixed[...] = (tok[HALO:, :].astype(F32) + dot_nt(out_low[...], wo[...])).astype(BF)
    store_grads(place, (gwg, gwo), (out_a, out_b), sems)


def scan_grad_kernel(b, place, gscan, conv, st, rw, seg_col, seg_row, z, colside, gentry, gread, smask, acc, cum_t):
    inner = conv.shape[1]
    half = BLOCK // 2
    j, i = lower_matrix()
    lane = lax.broadcasted_iota(jnp.int32, (BLOCK, LANES), 1)
    rows = slice(b * BLOCK, (b + 1) * BLOCK)
    same = (i >= j) & (seg_col[rows, 0:1] == seg_row[0:1, rows])
    scores = dot_nt(rw[rows, :STATE], rw[rows, STATE:])
    smask[...] = jnp.where(same, scores, 0.0)
    cum_t[...] = st[2, rows].T
    acc[...] = jnp.zeros_like(acc)
    colside[...] = jnp.zeros((BLOCK, LANES), F32)

    def pair(p, carry):
        cum = pltpu.roll(st[2, rows], lax.rem(LANES - 2 * p, LANES), 1)
        step = pltpu.roll(st[1, rows], lax.rem(LANES - 2 * p, LANES), 1)
        lanes = pl.ds(pl.multiple_of(p * LANES, LANES), LANES)
        c = conv[rows, lanes].astype(F32)
        act = (c * sigmoid(c)).astype(BF).astype(F32)
        xs = (act * jnp.where(lane < HEAD_DIM, step[:, 0:1], step[:, 1:2])).astype(BF)
        gs = gscan[rows, lanes]
        gs_t = gs.T
        top = jnp.zeros((half, LANES), F32)
        bottom = jnp.zeros((half, LANES), F32)
        for a in range(2):
            keep = (lane < HEAD_DIM) == (a == 0)
            mine = jnp.where(keep, xs, jnp.zeros_like(xs))
            grad = jnp.where(keep, gs, jnp.zeros_like(gs))
            row = cum_t[pl.ds(2 * p + a, 1), :]
            e = jnp.exp(jnp.minimum(row - cum[:half, a : a + 1], 0.0))
            top = top + dot((smask[:half, :] * e).astype(BF), grad)
            acc[:half, :] += dot(mine[:half], gs_t) * e
            e = jnp.exp(jnp.minimum(row[:, half:] - cum[half:, a : a + 1], 0.0))
            bottom = bottom + dot((smask[half:, half:] * e).astype(BF), grad[half:])
            acc[half:, half:] += dot(mine[half:], gs_t[:, half:]) * e
        both = jnp.concatenate([top, bottom], axis=0)
        z[:, lanes] = both
        channel = lax.broadcasted_iota(jnp.int32, (LANES, LANES), 0)
        head = lax.broadcasted_iota(jnp.int32, (LANES, LANES), 1)
        matrix = (channel // HEAD_DIM + 2 * p == head).astype(BF)
        colside[...] += head_sum(both * xs.astype(F32), matrix)
        return carry

    lax.fori_loop(0, inner // LANES, pair, 0, unroll=12)
    low = jnp.where(same, acc[...], 0.0).astype(BF)
    gentry[...] = dot(low, rw[rows, STATE:])
    gread[...] = dot_tn(low, rw[rows, :STATE])


def input_grad_kernel(
    place, near, far, d_ref, keep, states, conv, pre, gscan, st, rw, sconv, spre, rowside, gread_a, taps,
    taps_state, par, wide, cols, *refs
):
    by_block, (low_inner, low_state, low_step, sums, sums_state, sums_head, gstates) = refs[:-7], refs[-7:]
    z, colside, gentry, gread_b = [
        jnp.concatenate([ref[...] for ref in by_block[n::4]], axis=0) if n else by_block[n::4] for n in range(4)
    ]
    tokens, inner = conv.shape
    blocks = tokens // BLOCK
    tiles = inner // TILE
    heads = TILE // HEAD_DIM
    col = cols[...]
    now = entering(near, far)
    keep_grads = [None] * blocks
    whole_matrix = head_matrix(0, inner)
    for b in range(blocks - 1, -1, -1):
        gstates[b] = now.astype(BF)
        sum_row = jnp.sum(now * states[b].astype(F32), axis=0, keepdims=True)
        keep_grads[b] = head_sum(jnp.broadcast_to(sum_row, (8, inner)), whole_matrix)[0:1]
        if b > 0:
            now = d_ref[b - 1] + expand(keep[b : b + 1], 0, inner // HEAD_DIM) * now
    step_grad = jnp.zeros((tokens, LANES), F32)
    out_side = jnp.zeros((tokens, LANES), F32)
    entry_grad = gentry
    for tile in range(tiles):
        lanes = slice(tile * TILE, (tile + 1) * TILE)
        first = tile * heads
        matrix = head_matrix(first, TILE)
        c = conv[:, lanes].astype(F32)
        sg = sigmoid(c)
        act = (c * sg).astype(BF).astype(F32)
        step = expand(st[1], first, heads)
        out = expand(st[3], first, heads)
        scaled = (act * (step * out)).astype(BF)
        grads = []
        entries = []
        for b in range(blocks):
            rows = slice(b * BLOCK, (b + 1) * BLOCK)
            grads.append(dot(rw[rows, :STATE], gstates[b, :, lanes]))
            entries.append(dot_nt(scaled[rows], gstates[b, :, lanes]))
        grad_scaled = jnp.concatenate(grads, axis=0)
        entry_grad = entry_grad + jnp.concatenate(entries, axis=0)
        w = jnp.concatenate([ref[:, lanes] for ref in z], axis=0) + out * grad_scaled
        step_grad = step_grad + head_sum(act * w, matrix)
        out_side = out_side + head_sum(scaled.astype(F32) * grad_scaled, matrix)
        grad = wide[1:2, lanes] * gscan[:, lanes].astype(F32) + step * w
        grad = grad * (sg * (1.0 + c * (1.0 - sg)))
        back, rows_sum = conv_backward(grad, pre[:, lanes].astype(F32), taps[:, lanes], col)
        low = back.astype(BF)
        low_inner[:, lanes] = low
        sums[:, lanes] = put_rows(rows_sum, TILE)
    sc = sconv[...]
    sg = sigmoid(sc)
    grad = jnp.concatenate([entry_grad, gread_a[...] + gread_b], axis=1)
    grad = grad * (sg * (1.0 + sc * (1.0 - sg)))
    back, rows_sum = conv_backward(grad, spre[...], taps_state, col)
    low = back.astype(BF)
    low_state[...] = low
    sums_state[...] = put_rows(rows_sum, 2 * STATE)
    i, j = lower_matrix()
    upper = (i <= j).astype(F32)
    at_end = lax.broadcasted_iota(jnp.int32, (BLOCK, LANES), 0) == BLOCK - 1
    decays = []
    for b in range(blocks):
        rows = slice(b * BLOCK, (b + 1) * BLOCK)
        side = out_side[rows]
        last = jnp.sum(side, axis=0, keepdims=True) + keep_grads[b] * keep[b : b + 1]
        cum_grad = rowside[rows, :] - colside[rows] - side + jnp.where(at_end, last, 0.0)
        decays.append(dot_high(upper, cum_grad))
    decay_grad = jnp.concatenate(decays, axis=0)
    rate = par[1:2]
    step_grad = (step_grad + decay_grad * rate) * sigmoid(st[0])
    rows_head = [
        jnp.sum(step_grad, axis=0, keepdims=True),
        jnp.sum(decay_grad * st[1] * rate, axis=0, keepdims=True),
    ]
    sums_head[...] = put_rows(rows_head, LANES)
    low = jnp.concatenate([jnp.zeros((HALO, LANES), F32), step_grad], axis=0).astype(BF)
    low_step[...] = low


def weight_first_kernel(place, normed, low_inner, first):
    x = normed[...]
    for tile in range(first.shape[1] // SPAN):
        lanes = slice(tile * SPAN, (tile + 1) * SPAN)
        first[:, lanes] = dot_tn(x, low_inner[:, lanes]).astype(BF)


def weight_grad_kernel(place, normed, first, low_inner, low_state, low_step, *refs):
    grad_outs, (gwi, gws, gwp, sems) = refs[:-4], refs[-4:]
    x = normed[...]
    done = first.shape[1]
    gwi[:, :done] = first[...]
    gwi[:, done:] = dot_tn(x, low_inner[:, done:]).astype(BF)
    gws[...] = dot_tn(x, low_state[...]).astype(BF)
    gwp[...] = dot_tn(x, low_step[...]).astype(BF)
    store_grads(place, (gwi, gws, gwp), grad_outs, sems)


def token_grad_kernel(
    place, low_inner, low_state, low_step, gn_gate, tok, cot, gain, sums_in, sums_out, sums_state, sums_head, *refs
):
    weights, (grad, back, pack, win, wst, wsp, sems) = refs[:-7], refs[-7:]
    load_weights(place, weights, (win, wst, wsp), sems)
    wait_weights((win, wst, wsp), sems)
    width = tok.shape[1]
    gn = dot_nt(low_inner[...], win[...]) + dot_nt(low_state[...], wst[...])
    gn = gn + dot_nt(low_step[...], wsp[...])
    gn = gn + jnp.concatenate([jnp.zeros((HALO, width), F32), gn_gate[...]], axis=0)
    t = tok[...].astype(F32)
    r = lax.rsqrt(jnp.mean(t * t, axis=1, keepdims=True) + EPS)
    scaled = t * r
    inner = pack.shape[1]
    pack[0 : KW + 1, :] = sums_in[: KW + 1]
    pack[KW + 1 : KW + 2, :] = sums_out[0:1]
    pack[KW + 2 :, :] = jnp.zeros((8 - KW - 2, inner), F32)
    pack[KW + 2 : KW + 3, :width] = jnp.sum(gn * scaled, axis=0, keepdims=True)
    pack[KW + 2 : KW + 3, width : width + LANES] = sums_head[0:1]
    pack[KW + 2 : KW + 3, width + LANES : width + 2 * LANES] = sums_head[1:2]
    skips = head_sum(sums_out[...], head_matrix(0, inner))
    pack[KW + 2 : KW + 3, width + 2 * LANES : width + 3 * LANES] = skips[1:2]
    for k in range(KW + 1):
        pack[KW + 3 : KW + 4, 2 * STATE * k : 2 * STATE * (k + 1)] = sums_state[k : k + 1]
    gg = gn * gain[0:1]
    result = gg * r - t * (r * r * r * jnp.mean(gg * t, axis=1, keepdims=True))
    back[...] = result[:HALO]
    grad[...] = result[HALO:] + cot[...].astype(F32)


def finish_kernel(place, a, b, c, d, inner, state, step, conv, conv_state, norm, gain, *heads):
    depth, span = inner.shape
    per = span // HEAD_DIM

    def total(first, count):
        rows = slice(first, first + count)
        return a[rows].astype(F32) + b[rows].astype(F32) + c[rows].astype(F32) + d[rows].astype(F32)

    inner[...] = total(0, depth)
    last = total(depth, depth)
    state[...] = last[:, : 2 * STATE]
    turn_heads = lax.rem(LANES - place[1] * per, LANES)
    step[...] = pltpu.roll(last[:, 2 * STATE :], turn_heads, 1)[:, :per]
    small = total(2 * depth, 2 * 8)
    conv[...] = small[: KW + 1]
    gain[...] = small[KW + 1]
    whole = [
        jnp.concatenate([small[8 + 2 * q + n : 9 + 2 * q + n] for q in range(4)], axis=1) for n in range(2)
    ]
    width = norm.shape[0]
    norm[...] = whole[0][0, :width]
    rows = [whole[1][:, 2 * STATE * k : 2 * STATE * (k + 1)] for k in range(KW + 1)]
    conv_state[...] = put_rows(rows, 2 * STATE)[: KW + 1]
    rows = [whole[0][:, width + LANES * n : width + LANES * (n + 1)] for n in range(3)]
    rows = pltpu.roll(put_rows(rows, LANES), turn_heads, 1)
    for n, head in enumerate(heads):
        head[...] = rows[n, :per]


def line(shift, size):
    return [(i, i + shift) for i in range(size) if 0 <= i + shift < size]


def pass_first(payload, size, sign):
    return lax.ppermute(payload, "tensor", line(sign, size))


def pass_states(payload, came, size, sign, first=()):
    own = payload[:STATE].astype(F32)
    factor = payload[STATE].astype(F32) + payload[STATE + 1].astype(F32)
    near, far, send = came, jnp.zeros_like(came[:STATE]), came
    reach = 2
    while reach < size:
        near_factor = near[STATE].astype(F32) + near[STATE + 1].astype(F32)
        total = near[:STATE].astype(F32)
        if reach > 2:
            total = total + last_factor[None] * far[:STATE].astype(F32)
        send = (own + factor[None] * total).astype(BF)
        if 2 * reach < size:
            both = factor * near_factor
            hi = both.astype(BF)
            lo = (both - hi.astype(F32)).astype(BF)
            send = jnp.concatenate([send, hi[None], lo[None]], axis=0)
        send = after(send, *first)
        far = lax.ppermute(send, "tensor", line(sign * reach, size))
        last_factor = near_factor
        if 2 * reach < size:
            total = near[:STATE].astype(F32) + near_factor[None] * far[:STATE].astype(F32)
            both = near_factor * (far[STATE].astype(F32) + far[STATE + 1].astype(F32))
            hi = both.astype(BF)
            lo = (both - hi.astype(F32)).astype(BF)
            near = jnp.concatenate([total.astype(BF), hi[None], lo[None]], axis=0)
            near = jnp.pad(near, ((0, HALO - 2), (0, 0)))
            far = jnp.zeros_like(far)
        reach = 2 * reach
    return near, far[:STATE], send


def entering(near, far):
    rows = near[STATE:, :].astype(F32)
    return near[:STATE, :].astype(F32) + (rows[0:1] + rows[1:2]) * far[...].astype(F32)


def swap(values, mask):
    return lax.ppermute(values, "dp", [(i, i ^ mask) for i in range(8)])


def turn(values, shift):
    return lax.ppermute(values, "tensor", [(i, (i + shift) % 4) for i in range(4)])


def cross(values, mask):
    return lax.ppermute(values, "tensor", [(i, i ^ mask) for i in range(4)])


def ring(values):
    return [values] + [turn(values, -m) for m in range(1, 4)]


def gather_plane(column):
    return [column] + [swap(column, k) for k in ORDER[1:4]]


def gather_cores(same, first=()):
    return same + [swap(after(v, *first), 1) for v in same]


def sum_pair_kernel(place, mine, came, *outs):
    for n, out in enumerate(outs):
        out[...] = mine[n] + came[n]


def sum_pair_pack_kernel(place, mine, came, pack, came_pack, *outs):
    slots, depth, span = mine.shape[1:]
    total = pack[...] + came_pack[...]
    rows = jnp.concatenate([total[:, q * span : (q + 1) * span] for q in range(4)], axis=0).astype(BF)
    for n, out in enumerate(outs):
        for m in range(slots):
            out[m * depth : (m + 1) * depth, :] = mine[n, m] + came[n, m]
        out[slots * depth :, :] = rows


def sum_column_pack_kernel(place, a, b, c, d, *refs):
    outs, rows = refs[:4], refs[4]
    depth = (a.shape[0] - 32) // 5

    def total(first, count):
        part = slice(first, first + count)
        return a[part].astype(F32) + b[part].astype(F32) + c[part].astype(F32) + d[part].astype(F32)

    rows[...] = total(5 * depth, 32)
    last = total(4 * depth, depth).astype(BF)
    rest = jnp.concatenate([rows[8 * q + KW + 2 : 8 * q + KW + 4] for q in range(4)], axis=0)
    for m, out in enumerate(outs):
        out[:depth, :] = total(m * depth, depth).astype(BF)
        out[depth : 2 * depth, :] = last
        own = rows[pl.ds(aligned((place[1] + m) % 4, 8), 8), :]
        out[2 * depth :, :] = jnp.concatenate([own, rest], axis=0).astype(BF)


def sum_column_kernel(place, a, b, c, d, *outs):
    for m, out in enumerate(outs):
        total = a[m].astype(F32) + b[m].astype(F32) + c[m].astype(F32) + d[m].astype(F32)
        out[...] = total.astype(BF)


def sum_last_kernel(place, a, b, c, d, first, second):
    for n, out in enumerate((first, second)):
        out[...] = a[n].astype(F32) + b[n].astype(F32) + c[n].astype(F32) + d[n].astype(F32)


def reduce_core(where, mine, other):
    came = swap(other, 1)
    return call(sum_pair_kernel, [sds(mine.shape[1:], BF)] * 4, (where, mine, came), name="sum_pair")


def reduce_plane(where, parts):
    came = [swap(parts[n], ORDER[n]) for n in range(1, 4)]
    shape = (2, *parts[0].shape[-2:])
    return call(sum_column_kernel, [sds(shape, BF)] * 4, (where, parts[0], *came), name="sum_column")


def reduce_line(where, parts):
    came = [turn(parts[m], m) for m in range(1, 4)]
    return call(
        sum_last_kernel, [sds(parts[0].shape[1:], F32)] * 2, (where, parts[0], *came), name="sum_last"
    )


def after_all(values, *others):
    return lax.optimization_barrier((*values, *others))[: len(values)]


def after(value, *others):
    return lax.optimization_barrier((value, *others))[0]


def gather(shard):
    return lax.all_gather(
        lax.all_gather(shard, "tensor", axis=1, tiled=True), "dp", axis=0, tiled=True
    )


def scatter(grad):
    part = lax.psum_scatter(grad, "dp", scatter_dimension=0, tiled=True)
    return lax.psum_scatter(part, "tensor", scatter_dimension=1, tiled=True).astype(F32)


def make_shards(mesh):
    size = mesh.shape["tensor"]
    blocked = size == 4 and mesh.shape["dp"] == 8

    def shards(
        tokens, segments, cotangent, norm_gain, w_gate, w_inner, w_step, w_state, conv_inner, conv_state,
        step_bias, decay_log, skip_gain, out_gain, w_out,
    ):
        count, width = tokens.shape
        place = lax.axis_index("tensor")
        blocks = count // BLOCK
        inner = w_inner.shape[1] * size
        heads = w_step.shape[1] * size

        halo = lax.ppermute(tokens[count - HALO :], "tensor", line(1, size))
        tok = jnp.concatenate([halo, tokens], axis=0)
        wide_tok = tok.astype(F32)
        gain = norm_gain.astype(F32)
        rms = lax.rsqrt(jnp.mean(wide_tok * wide_tok, axis=1, keepdims=True) + EPS)
        normed = (wide_tok * rms * gain).astype(BF)

        padded = jnp.concatenate([jnp.full((HALO,), -1, jnp.int32), segments])
        near = lax.dynamic_slice(padded, (place * count,), (HALO + count,))
        seg = near[HALO:]
        masks = [near[HALO - k : HALO - k + count] == seg for k in range(1, KW)]
        grid = seg.reshape(blocks, BLOCK)
        prev = near[HALO - 1 : HALO - 1 + count].reshape(blocks, BLOCK)[:, :1]
        from_prev = (grid == prev).reshape(-1)
        at_last = (grid == grid[:, BLOCK - 1 :]).reshape(-1)
        cols = jnp.stack([*masks, from_prev, at_last], axis=1).astype(F32)
        seg_col = seg.astype(F32)[:, None]
        seg_row = seg.astype(F32)[None]

        def pad_heads(row):
            return jnp.pad(row, ((0, 0), (0, LANES - heads)))

        where = jnp.stack([lax.axis_index("dp"), place]).astype(jnp.int32)
        depth, span = w_inner.shape
        per = heads // size
        if blocked:
            tall = HALO + depth

            def place_at(block, row, lane):
                rows = (row, tall - row - block.shape[0])
                return jnp.pad(block, (rows, (lane, span - lane - block.shape[1])))

            pack = place_at(w_inner, 0, 0) + place_at(w_step.T, depth + KW + 3, 0)
            pack = pack + place_at(conv_inner, depth, 0) + place_at(out_gain[None], depth + KW + 1, 0)
            for n, row in enumerate((step_bias, decay_log, skip_gain)):
                pack = pack + place_at(row[None], depth + KW + 2, n * per)
            came = ring(pack)
            pair_out = jnp.stack([w_gate, w_out])[None]
            pair_out = jnp.concatenate([pair_out, cross(pair_out, 1)])
            came_out = jnp.concatenate([pair_out, cross(pair_out, 2)])

            column, taps, par, wide = call(
                unpack_kernel,
                [
                    sds((5, depth, span), BF),
                    sds((8, inner), F32),
                    sds((8, LANES), F32),
                    sds((8, inner), F32),
                ],
                (where, *came, w_state),
                name="unpack",
            )
            same = gather_plane(column)
            pieces = gather_cores(same, (came_out,))
            same_out = gather_plane(after(came_out, *same[1:]))
        else:
            conv_whole, head_whole, gain_whole = [
                lax.all_gather(v, "tensor", axis=v.ndim - 1, tiled=True).astype(F32)
                for v in (conv_inner, jnp.stack([step_bias, decay_log, skip_gain]), out_gain)
            ]
            pieces = [gather(w_inner), lax.all_gather(w_state, "dp", axis=0, tiled=True), pad_heads(gather(w_step))]
            pieces_out = [gather(w_gate), gather(w_out)]
            taps = jnp.pad(conv_whole, ((0, 8 - KW - 1), (0, 0)))
            bias, rate, skip = head_whole[0], -jnp.exp(head_whole[1]), head_whole[2]
            par = pad_heads(jnp.pad(jnp.stack([bias, rate]), ((0, 6), (0, 0))))
            wide = jnp.pad(jnp.stack([gain_whole, jnp.repeat(skip, HEAD_DIM)]), ((0, 6), (0, 0)))
        taps_state = jnp.pad(conv_state.astype(F32), ((0, 8 - KW - 1), (0, 0)))
        in_scratch = [
            pltpu.VMEM((width, inner), BF),
            pltpu.VMEM((width, 2 * STATE), BF),
            pltpu.VMEM((width, LANES), BF),
            pltpu.SemaphoreType.DMA((3,)),
        ]
        out_scratch = [
            pltpu.VMEM((width, inner), BF),
            pltpu.VMEM((width, inner), BF),
            pltpu.SemaphoreType.DMA((2,)),
        ]

        def last_args(fixed, arrays):
            return {"args": (where, *fixed, *arrays), "far": range(1 + len(fixed), 1 + len(fixed) + len(arrays))}

        pre, conv, spre, sconv, rw, st, keep, c_ref, *pays = call(
            project_kernel,
            [
                sds((HALO + count, inner), BF),
                sds((count, inner), F32),
                sds((HALO + count, 2 * STATE), F32),
                sds((count, 2 * STATE), F32),
                sds((count, 2 * STATE), BF),
                sds((5, count, LANES), F32),
                sds((8, LANES), F32),
                sds((max(1, blocks - 1), STATE, inner), F32),
                *[sds((STATE + HALO, inner // HALVES), BF)] * HALVES,
            ],
            scratch=in_scratch,
            **last_args((normed, taps, taps_state, par, cols), pieces),
            name="project",
            micros=9.5,
        )
        came_pays = [pass_first(pay, size, 1) for pay in pays]
        enter = []
        y = []
        for b in range(blocks):
            y += call(
                functools.partial(scan_kernel, b),
                [sds((BLOCK, inner), F32)],
                (where, conv if b == 0 else after(conv, enter[-1][2], *came_pays), st, rw, seg_col, seg_row),
                [pltpu.VMEM((BLOCK, BLOCK), F32), pltpu.VMEM((LANES, BLOCK), F32)],
                name=f"scan_{b}",
                micros=5,
            )
            if b < HALVES:
                enter.append(pass_states(pays[b], came_pays[b], size, 1, (y[-1],)))
        for part in range(len(enter), HALVES):
            enter.append(pass_states(pays[part], came_pays[part], size, 1))
        near, far, sent = [list(v) for v in zip(*enter)]
        if blocked:
            pieces_out = gather_cores(same_out, (far[0], sent[-1]))
        gate, gout = call(
            gate_kernel,
            [sds((count, inner), F32)] * 2,
            scratch=out_scratch,
            **last_args((after(normed, sent[-1]), cotangent), pieces_out),
            name="gate",
            micros=4,
        )
        out_low, ggate, gscan, rowside, gread_a, states, d_ref, pay, sums = call(
            output_kernel,
            [
                sds((count, inner), BF),
                sds((count, inner), BF),
                sds((count, inner), BF),
                sds((count, LANES), F32),
                sds((count, STATE), F32),
                sds((blocks, STATE, inner), BF),
                sds((max(1, blocks - 1), STATE, inner), F32),
                sds((STATE + HALO, inner), BF),
                sds((8, inner), F32),
            ],
            (where, c_ref, keep, gate, gout, conv, rw, st, wide, *near, *far, *y),
            [pltpu.VMEM((ROWS, inner), F32), pltpu.VMEM((blocks, STATE, inner), F32)],
            name="output",
            micros=9.5,
        )
        if blocked:
            shapes_out = [sds((4, 4, 2, depth, span), BF)] * 2
            shapes_in = [sds((4, 5, depth, span), BF)] * 2
        else:
            shapes_out = [sds((width, inner), BF)] * 2
            shapes_in = [sds((width, inner), BF), sds((width, 2 * STATE), BF), sds((width, LANES), BF)]
        mixed, gn_gate, *grads_out = call(
            gate_grad_kernel,
            [sds((count, width), BF), sds((count, width), F32), *shapes_out],
            far_outs=(2, 3),
            scratch=[
                pltpu.VMEM((width, inner), BF),
                pltpu.VMEM((width, inner), BF),
                *out_scratch,
            ],
            **last_args((normed, cotangent, out_low, ggate, tok), pieces_out),
            name="gate_grad",
            micros=8.3,
        )
        came_pay = pass_first(pay, size, -1)
        if blocked:
            mine_out, other_out = grads_out
            parts_out = reduce_core(where, mine_out, after(other_out, came_pay))
        else:
            parts_out = ()
        *leave, sent = pass_states(pay, came_pay, size, -1)
        by_block = [
            call(
                functools.partial(scan_grad_kernel, b),
                [sds((BLOCK, inner), F32), sds((BLOCK, LANES), F32), *[sds((BLOCK, STATE), F32)] * 2],
                (where, after(gscan, sent, *parts_out), conv, st, rw, seg_col, seg_row),
                [
                    pltpu.VMEM((BLOCK, BLOCK), F32),
                    pltpu.VMEM((BLOCK, BLOCK), F32),
                    pltpu.VMEM((LANES, BLOCK), F32),
                ],
                name=f"scan_grad_{b}",
                micros=9,
            )
            for b in range(blocks)
        ]
        low_inner, low_state, low_step, sums_in, sums_state, sums_head = call(
            input_grad_kernel,
            [
                sds((HALO + count, inner), BF),
                sds((HALO + count, 2 * STATE), BF),
                sds((HALO + count, LANES), BF),
                sds((8, inner), F32),
                sds((8, 2 * STATE), F32),
                sds((8, LANES), F32),
            ],
            (
                where, *leave, d_ref, keep, states, conv, pre, gscan, st, rw, sconv, spre, rowside, gread_a, taps,
                taps_state, par, wide, cols, *[v for part in by_block for v in part],
            ),
            [pltpu.VMEM((blocks, STATE, inner), BF)],
            name="input_grad",
            micros=9,
        )
        first = call(
            weight_first_kernel,
            [sds((width, inner - SPAN), BF)],
            (where, normed, low_inner),
            name="weight_first",
            micros=3,
        )[0]
        low_next = low_inner
        if blocked:
            lines_out = reduce_plane(where, parts_out)
            low_next = after(low_inner, *lines_out)
        grads_in = call(
            weight_grad_kernel,
            shapes_in,
            (where, normed, first, low_next, low_state, low_step),
            scratch=in_scratch,
            far_outs=range(len(shapes_in)),
            name="weight_grad",
            micros=5,
        )
        if blocked:
            mine_in, other_in = grads_in
            came_in = swap(other_in, 1)
            low_inner = after(low_inner, other_in)
        grad, back, pack = call(
            token_grad_kernel,
            [sds((count, width), F32), sds((HALO, width), F32), sds((8, inner), F32)],
            scratch=in_scratch,
            **last_args((low_inner, low_state, low_step, gn_gate, tok, cotangent, gain[None], sums_in, sums, sums_state, sums_head), pieces),
            name="token_grad",
            micros=5,
        )
        if blocked:
            tall = 5 * depth + 32
            parts_in = call(
                sum_pair_pack_kernel,
                [sds((tall, span), BF)] * 4,
                (where, mine_in, came_in, pack, swap(pack, 1)),
                name="sum_pair_pack",
            )
            back = lax.ppermute(after(back, *parts_in), "tensor", line(-1, size))
            lines_out = after_all(lines_out, *parts_in)
            grad_gate, grad_out = reduce_line(where, lines_out)
        if blocked:
            came_in = [swap(parts_in[n], ORDER[n]) for n in range(1, 4)]
            lines_in = call(
                sum_column_pack_kernel,
                [sds((2 * depth + 2 * 8, span), BF)] * 4,
                (where, after(parts_in[0], back), *came_in),
                [pltpu.VMEM((32, span), F32)],
                name="sum_column_pack",
            )
            grad_inner, grad_state, grad_step, grad_conv, grad_conv_state, norm, grad_gain, *head_grads = call(
                finish_kernel,
                [
                    sds((depth, span), F32),
                    sds((depth, 2 * STATE), F32),
                    sds((depth, per), F32),
                    sds((KW + 1, span), F32),
                    sds((KW + 1, 2 * STATE), F32),
                    sds((width,), F32),
                    sds((span,), F32),
                    *[sds((per,), F32)] * 3,
                ],
                (where, lines_in[0], *[turn(lines_in[m], m) for m in range(1, 4)]),
                name="finish",
            )
        else:
            pack = lax.psum(pack, ("dp", "tensor"))
            own = lax.dynamic_slice(pack, (0, place * span), (KW + 2, span))
            norm = pack[KW + 2, :width]
            grad_conv, grad_gain = own[: KW + 1], own[KW + 1]
            grad_conv_state = pack[KW + 3, : (KW + 1) * 2 * STATE].reshape(KW + 1, 2 * STATE)
            head_grads = [
                lax.dynamic_slice(pack[KW + 2], (width + LANES * n + place * per,), (per,)) for n in range(3)
            ]
            grad_gate, grad_out, grad_inner, grad_step = [
                scatter(v) for v in (*grads_out, grads_in[0], grads_in[2][:, :heads])
            ]
            grad_state = lax.psum_scatter(grads_in[1], "dp", scatter_dimension=0, tiled=True)
            grad_state = lax.psum(grad_state, "tensor").astype(F32)
        if not blocked:
            back = lax.ppermute(back, "tensor", line(-1, size))
        grad = grad.at[count - HALO :].add(back)
        return (
            mixed,
            grad,
            norm,
            grad_gate,
            grad_inner,
            grad_step,
            grad_state,
            grad_conv,
            grad_conv_state,
            *head_grads,
            grad_gain,
            grad_out,
        )

    return shards


def solution(mesh):
    in_specs = (
        P(("dp", "tensor"), None),
        P("dp"),
        P(("dp", "tensor"), None),
        P(),
        P("dp", "tensor"),
        P("dp", "tensor"),
        P("dp", "tensor"),
        P("dp", None),
        P(None, "tensor"),
        P(),
        P("tensor"),
        P("tensor"),
        P("tensor"),
        P("tensor"),
        P("dp", "tensor"),
    )
    out_specs = (
        P(("dp", "tensor"), None),
        P(("dp", "tensor"), None),
        P(),
        P("dp", "tensor"),
        P("dp", "tensor"),
        P("dp", "tensor"),
        P("dp", None),
        P(None, "tensor"),
        P(),
        P("tensor"),
        P("tensor"),
        P("tensor"),
        P("tensor"),
        P("dp", "tensor"),
    )
    return jax.shard_map(
        make_shards(mesh), mesh=mesh, in_specs=in_specs, out_specs=out_specs, check_vma=False
    )
```

```python
import functools
import math

import jax
import jax.numpy as jnp
from jax import lax
from jax.experimental import pallas as pl
from jax.experimental.pallas import tpu as pltpu
from jax.sharding import PartitionSpec as P

HEAD_DIM = 64
STATE = 128
KW = 4
BLOCK = 256
HALO = 16
LANES = 128
TILE = 256
SPAN = 384
ROWS = 128
HALVES = 2
EPS = 1e-05
F32 = jnp.float32
BF = jnp.bfloat16
HIGH = lax.Precision.HIGHEST
SPARE = 3 * 2**20
ORDER = (0, 2, 4, 6, 1, 3, 5, 7)


def dot(a, b):
    return lax.dot_general(a, b, (((1,), (0,)), ((), ())), preferred_element_type=F32)


def dot_nt(a, b):
    return lax.dot_general(a, b, (((1,), (1,)), ((), ())), preferred_element_type=F32)


def dot_tn(a, b):
    return lax.dot_general(a, b, (((0,), (0,)), ((), ())), preferred_element_type=F32)


def dot_high(a, b):
    return lax.dot_general(
        a, b, (((1,), (0,)), ((), ())), precision=HIGH, preferred_element_type=F32
    )


def sigmoid(x):
    return 0.5 * jnp.tanh(0.5 * x) + 0.5


def expand(x, first, count):
    lane = lax.broadcasted_iota(jnp.int32, (x.shape[0], LANES), 1)
    return jnp.concatenate(
        [
            jnp.where(lane < HEAD_DIM, x[:, h : h + 1], x[:, h + 1 : h + 2])
            for h in range(first, first + count, 2)
        ],
        axis=1,
    )


def halved(tile, inner, width):
    first = tile * width % (inner // HALVES)
    return tile * width // (inner // HALVES), slice(first, first + width)


def head_matrix(first, channels):
    channel = lax.broadcasted_iota(jnp.int32, (channels, LANES), 0)
    head = lax.broadcasted_iota(jnp.int32, (channels, LANES), 1)
    return (channel // HEAD_DIM + first == head).astype(BF)


def head_sum(x, matrix):
    hi = x.astype(BF)
    lo = (x - hi.astype(F32)).astype(BF)
    return dot(hi, matrix) + dot(lo, matrix)


def lower_matrix():
    i = lax.broadcasted_iota(jnp.int32, (BLOCK, BLOCK), 0)
    j = lax.broadcasted_iota(jnp.int32, (BLOCK, BLOCK), 1)
    return i, j


def conv_forward(values, taps, cols):
    result = taps[KW : KW + 1] + taps[0:1] * values[HALO:]
    for k in range(1, KW):
        result = result + taps[k : k + 1] * pltpu.roll(values, k, 0)[HALO:] * cols[:, k - 1 : k]
    return result


def conv_backward(grad, values, taps, cols):
    width = grad.shape[1]
    whole = HALO + grad.shape[0]
    zero = jnp.zeros((HALO, width), F32)
    base = jnp.concatenate([zero, grad], axis=0)
    result = taps[0:1] * base
    sums = [jnp.sum(grad * values[HALO:], axis=0, keepdims=True)]
    for k in range(1, KW):
        masked = jnp.concatenate([zero, grad * cols[:, k - 1 : k]], axis=0)
        back = pltpu.roll(masked, whole - k, 0)
        result = result + taps[k : k + 1] * back
        sums.append(jnp.sum(back * values, axis=0, keepdims=True))
    sums.append(jnp.sum(grad, axis=0, keepdims=True))
    return result, sums


def put_rows(rows, width):
    index = lax.broadcasted_iota(jnp.int32, (8, width), 0)
    result = jnp.zeros((8, width), F32)
    for i, row in enumerate(rows):
        result = jnp.where(index == i, row, result)
    return result


def call(kernel, outs, args, scratch=(), name=None, micros=1.0, far=(), far_outs=()):
    size = 1 << 20

    held = [a for i, a in enumerate(args) if i > 0 and i not in far]
    held += [o for i, o in enumerate(outs) if i not in far_outs]
    limit = SPARE + sum(a.size * a.dtype.itemsize for a in held)
    for item in scratch:
        if len(item.shape) > 1:
            limit += math.prod(item.shape) * jnp.dtype(item.dtype).itemsize

    def spec(space):
        return pl.BlockSpec(memory_space=space)

    ins = [
        spec(pltpu.SMEM if i == 0 else pltpu.HBM if i in far else pltpu.VMEM) for i in range(len(args))
    ]
    return pl.pallas_call(
        kernel,
        out_shape=outs,
        in_specs=ins,
        out_specs=[spec(pl.ANY if i in far_outs else pltpu.VMEM) for i in range(len(outs))],
        scratch_shapes=list(scratch),
        compiler_params=pltpu.CompilerParams(vmem_limit_bytes=limit),
        cost_estimate=pl.CostEstimate(flops=int(micros * 1.15e9), bytes_accessed=size, transcendentals=0),
        name=name,
    )(*args)


def sds(shape, dtype):
    return jax.ShapeDtypeStruct(shape, dtype)


def aligned(value, size):
    return pl.multiple_of(value * size, size)


def load_weights(place, refs, targets, sems):
    if len(refs[0].shape) == 2:
        copies = [pltpu.make_async_copy(r, t, sems.at[n]) for n, (r, t) in enumerate(zip(refs, targets))]
        for copy in copies:
            copy.start()
        return
    split = refs[0].shape[0] == 5
    depth, span = refs[0].shape[-2:]
    for n, k in enumerate(ORDER):
        row = pl.ds(aligned(place[0] ^ k, depth), depth)
        for m in range(4):
            who = (place[1] + m) % 4 if split else place[1] ^ m
            column = pl.ds(aligned(who, span), span)
            for g in range(1 if split else 2):
                source = refs[n].at[m] if split else refs[n].at[m, g]
                pltpu.make_async_copy(source, targets[g].at[row, column], sems.at[g]).start()
        if split:
            wide = targets[1].shape[1]
            pltpu.make_async_copy(refs[n].at[4, :, :wide], targets[1].at[row, :], sems.at[1]).start()
            pltpu.make_async_copy(refs[n].at[4, :, wide:], targets[2].at[row, :], sems.at[2]).start()


def wait_weights(targets, sems):
    for n, target in enumerate(targets):
        pltpu.make_async_copy(target, target, sems.at[n]).wait()


def store_grads(place, sources, outs, sems):
    if len(outs[0].shape) == 2:
        copies = [pltpu.make_async_copy(s, o, sems.at[n]) for n, (s, o) in enumerate(zip(sources, outs))]
        for copy in copies:
            copy.start()
    else:
        split = outs[0].shape[1] == 5
        depth, span = outs[0].shape[-2:]
        for n, k in enumerate(ORDER):
            out = outs[n // 4].at[n % 4]
            sem = sems.at[n // 4]
            row = pl.ds(aligned(place[0] ^ k, depth), depth)
            for m in range(4):
                column = pl.ds(aligned((place[1] + m) % 4, span), span)
                for g in range(1 if split else 2):
                    target = out.at[m] if split else out.at[m, g]
                    pltpu.make_async_copy(sources[g].at[row, column], target, sem).start()
            if split:
                wide = sources[1].shape[1]
                pltpu.make_async_copy(sources[1].at[row, :], out.at[4, :, :wide], sem).start()
                pltpu.make_async_copy(sources[2].at[row, :], out.at[4, :, wide:], sem).start()
    for n, out in enumerate(outs):
        pltpu.make_async_copy(out, out, sems.at[n]).wait()


def unpack_kernel(place, *refs):
    parts, (state, column, taps, par, wide) = refs[:4], refs[4:]
    depth, span = column.shape[1:]
    per = span // HEAD_DIM
    heads = wide.shape[1] // HEAD_DIM
    lane = lax.broadcasted_iota(jnp.int32, (8, LANES), 1)
    step = jnp.zeros((LANES, LANES), F32)
    rows = [jnp.zeros((8, LANES), F32)] * 3
    for m, part in enumerate(parts):
        who = (place[1] + m) % 4
        lanes = pl.ds(aligned(who, span), span)
        column[m] = part[:depth, :]
        low = part[depth:, :].astype(F32)
        tall = jnp.concatenate([low[:, :LANES], jnp.zeros((LANES - HALO, LANES), F32)], axis=0)
        tall = pltpu.roll(tall, LANES - KW - 3, 0)
        tall = jnp.where(lax.broadcasted_iota(jnp.int32, (LANES, LANES), 0) < per, tall, 0.0)
        step = step + pltpu.roll(tall, who * per, 0)
        taps[:, lanes] = low[:8]
        wide[0:1, lanes] = low[KW + 1 : KW + 2]
        row = jnp.broadcast_to(low[KW + 2 : KW + 3, :LANES], (8, LANES))
        for n in range(3):
            own = pltpu.roll(row, LANES - n * per, 1) if n else row
            rows[n] = rows[n] + pltpu.roll(jnp.where(lane < per, own, 0.0), who * per, 1)
    column[4] = jnp.concatenate([state[...], step.T[:depth].astype(BF)], axis=1)
    par[...] = put_rows([rows[0][0:1], jnp.where(lane < heads, -jnp.exp(rows[1]), 0.0)[0:1]], LANES)
    wide[1:2, :] = expand(rows[2], 0, heads)[0:1]


def project_kernel(
    place, *refs
):
    (normed, taps, taps_state, par, cols), refs = refs[:5], refs[5:]
    weights, refs = refs[: -12 - HALVES], refs[-12 - HALVES :]
    pre, conv, spre, sconv, rw, st, keep, c_ref, *pay, win, wst, wsp, sems = refs
    load_weights(place, weights, (win, wst, wsp), sems)
    wait_weights((win, wst, wsp), sems)
    project(normed, win, wst, wsp, taps, taps_state, par, cols, pre, conv, spre, sconv, rw, st, keep, c_ref, pay)


def project(
    normed, win, wst, wsp, taps, taps_state, par, cols, pre, conv, spre, sconv, rw, st, keep, c_ref, pay
):
    tokens = conv.shape[0]
    inner = conv.shape[1]
    blocks = tokens // BLOCK
    x = normed[...]
    low = x[HALO:]
    col = cols[...]
    sp = dot(low, wsp[...]) + par[0:1]
    step = jnp.maximum(sp, 0.0) + jnp.log1p(jnp.exp(-jnp.abs(sp)))
    decay = step * par[1:2]
    i, j = lower_matrix()
    lower = (i >= j).astype(F32)
    st[0] = sp
    st[1] = step
    keeps = []
    outs = []
    for b in range(blocks):
        rows = slice(b * BLOCK, (b + 1) * BLOCK)
        cum = dot_high(lower, decay[rows])
        last = cum[BLOCK - 1 : BLOCK]
        from_prev = col[rows, 3:4]
        out = jnp.exp(last - cum) * col[rows, 4:5]
        st[2, rows] = cum
        st[3, rows] = out
        st[4, rows] = jnp.exp(cum) * from_prev
        keeps.append(jnp.exp(last) * from_prev[BLOCK - 1 : BLOCK])
        outs.append(out * step[rows])
    keep[...] = put_rows(keeps, LANES)
    whole = keeps[0]
    for b in range(1, blocks):
        whole = whole * keeps[b]
    state = dot(x, wst[...])
    spre[...] = state
    sc = conv_forward(state, taps_state, col)
    sconv[...] = sc
    rw[...] = (sc * sigmoid(sc)).astype(BF)
    entry = rw[:, :STATE]
    index = lax.broadcasted_iota(jnp.int32, (HALO, SPAN), 0)
    for tile in range(inner // SPAN):
        lanes = slice(tile * SPAN, (tile + 1) * SPAN)
        heads = SPAN // HEAD_DIM
        first = tile * heads
        value = dot(x, win[:, lanes])
        pre[:, lanes] = value.astype(BF)
        c = conv_forward(value, taps[:, lanes], col)
        conv[:, lanes] = c
        c = c.astype(F32)
        act = (c * sigmoid(c)).astype(BF).astype(F32)
        total = None
        for b in range(blocks):
            rows = slice(b * BLOCK, (b + 1) * BLOCK)
            scaled = (act[rows] * expand(outs[b], first, heads)).astype(BF)
            part = dot_tn(entry[rows], scaled)
            if b < blocks - 1:
                c_ref[b, :, lanes] = part
            total = part if b == 0 else total * expand(keeps[b], first, heads) + part
        part, local = halved(tile, inner, SPAN)
        pay[part][:STATE, local] = total.astype(BF)
        wide = expand(whole, first, heads)
        hi = wide.astype(BF).astype(F32)
        pay[part][STATE:, local] = jnp.where(index == 0, hi, jnp.where(index == 1, wide - hi, 0.0)).astype(BF)


def gate_kernel(place, normed, cot, *refs):
    weights, (gate, gout, wg, wo, sems) = refs[:-5], refs[-5:]
    load_weights(place, weights, (wg, wo), sems)
    wait_weights((wg, wo), sems)
    for tile in range(gate.shape[1] // TILE):
        lanes = slice(tile * TILE, (tile + 1) * TILE)
        gate[:, lanes] = dot(normed[HALO:, :], wg[:, lanes])
        gout[:, lanes] = dot(cot[...], wo[:, lanes])


def scan_kernel(b, place, conv, st, rw, seg_col, seg_row, y, smask, cum_t):
    inner = conv.shape[1]
    half = BLOCK // 2
    i, j = lower_matrix()
    lane = lax.broadcasted_iota(jnp.int32, (BLOCK, LANES), 1)
    rows = slice(b * BLOCK, (b + 1) * BLOCK)
    scores = dot_nt(rw[rows, STATE:], rw[rows, :STATE])
    same = (i >= j) & (seg_col[rows, 0:1] == seg_row[0:1, rows])
    smask[...] = jnp.where(same, scores, 0.0)
    cum_t[...] = st[2, rows].T

    def pair(p, carry):
        cum = pltpu.roll(st[2, rows], lax.rem(LANES - 2 * p, LANES), 1)
        step = pltpu.roll(st[1, rows], lax.rem(LANES - 2 * p, LANES), 1)
        lanes = pl.ds(pl.multiple_of(p * LANES, LANES), LANES)
        c = conv[rows, lanes].astype(F32)
        act = (c * sigmoid(c)).astype(BF).astype(F32)
        xs = (act * jnp.where(lane < HEAD_DIM, step[:, 0:1], step[:, 1:2])).astype(BF)
        top = jnp.zeros((half, LANES), F32)
        bottom = jnp.zeros((half, LANES), F32)
        for a in range(2):
            mine = jnp.where((lane < HEAD_DIM) == (a == 0), xs, jnp.zeros_like(xs))
            row = cum_t[pl.ds(2 * p + a, 1), :]
            e = jnp.exp(jnp.minimum(cum[:half, a : a + 1] - row[:, :half], 0.0))
            top = top + dot((smask[:half, :half] * e).astype(BF), mine[:half])
            e = jnp.exp(jnp.minimum(cum[half:, a : a + 1] - row, 0.0))
            bottom = bottom + dot((smask[half:, :] * e).astype(BF), mine)
        y[:half, lanes] = top
        y[half:, lanes] = bottom
        return carry

    lax.fori_loop(0, inner // LANES, pair, 0, unroll=12)


def output_kernel(
    place, c_ref, keep, gate, gout, conv, rw, st, wide, *refs
):
    refs, (out_low, ggate, gscan, rowside, gread, states, d_ref, pay, sums, so_ref, d_all) = refs[:-11], refs[-11:]
    near, far, y = refs[:HALVES], refs[HALVES : 2 * HALVES], refs[2 * HALVES :]
    tokens, inner = conv.shape
    blocks = tokens // BLOCK
    tiles = inner // TILE
    heads = TILE // HEAD_DIM
    span = inner // HALVES
    for part in range(HALVES):
        lanes = slice(part * span, (part + 1) * span)
        now = entering(near[part], far[part])
        for b in range(blocks):
            if b > 0:
                wide_keep = expand(keep[b - 1 : b], part * span // HEAD_DIM, span // HEAD_DIM)
                now = now * wide_keep + c_ref[b - 1, :, lanes]
            states[b, :, lanes] = now.astype(BF)
    sums[...] = jnp.zeros_like(sums)
    d_all[...] = jnp.zeros_like(d_all)

    def chunk(r, carry):
        rows = pl.ds(pl.multiple_of(r * ROWS, ROWS), ROWS)
        b = r // (BLOCK // ROWS)
        inside = pl.ds(pl.multiple_of(r % (BLOCK // ROWS) * ROWS, ROWS), ROWS)
        read = rw[rows, STATE:]
        scale = st[4, rows, :]
        total = jnp.zeros((ROWS, 1), F32)
        cross = jnp.zeros((ROWS, 1), F32)
        for tile in range(tiles):
            lanes = slice(tile * TILE, (tile + 1) * TILE)
            raw = dot(read, states[b, :, lanes])
            own = y[0][inside, lanes]
            for n in range(1, blocks):
                own = jnp.where(b == n, y[n][inside, lanes], own)
            so = own + raw * expand(scale, tile * heads, heads)
            so_ref[:, lanes] = so
            c = conv[rows, lanes].astype(F32)
            u = so + wide[1:2, lanes] * (c * sigmoid(c))
            g = gate[rows, lanes].astype(F32)
            gated = u * (g * sigmoid(g))
            total = total + jnp.sum(gated * gated, axis=1, keepdims=True)
            go = gout[rows, lanes].astype(F32) * wide[0:1, lanes]
            cross = cross + jnp.sum(go * gated, axis=1, keepdims=True)
        rms = lax.rsqrt(total / inner + EPS)
        cube = rms * rms * rms * (cross / inner)
        side = jnp.zeros((ROWS, LANES), F32)
        read_grad = jnp.zeros((ROWS, STATE), F32)
        for tile in range(tiles):
            lanes = slice(tile * TILE, (tile + 1) * TILE)
            so = so_ref[:, lanes]
            c = conv[rows, lanes].astype(F32)
            act = c * sigmoid(c)
            u = so + wide[1:2, lanes] * act
            g = gate[rows, lanes].astype(F32)
            sg = sigmoid(g)
            silu = g * sg
            gated = u * silu
            gain = wide[0:1, lanes]
            out = gated * rms
            out_low[rows, lanes] = (out * gain).astype(BF)
            go = gout[rows, lanes].astype(F32)
            gg = go * gain * rms - gated * cube
            q = gg * silu
            ggate[rows, lanes] = (gg * u * (sg * (1.0 + g * (1.0 - sg)))).astype(BF)
            low = q.astype(BF)
            gscan[rows, lanes] = low
            low = low.astype(F32)
            sums[0:1, lanes] += jnp.sum(go * out, axis=0, keepdims=True)
            sums[1:2, lanes] += jnp.sum(q * act, axis=0, keepdims=True)
            side = side + head_sum(low * so, head_matrix(tile * heads, TILE))
            scaled = (low * expand(scale, tile * heads, heads)).astype(BF)
            d_all[b, :, lanes] += dot_tn(read, scaled)
            read_grad = read_grad + dot_nt(scaled, states[b, :, lanes])
        rowside[rows, :] = side
        gread[rows, :] = read_grad
        return carry

    lax.fori_loop(0, tokens // ROWS, chunk, 0)
    for b in range(1, blocks):
        d_ref[b - 1] = d_all[b]
    total = d_all[blocks - 1]
    whole = keep[blocks - 1 : blocks]
    for b in range(blocks - 2, -1, -1):
        total = d_all[b] + expand(keep[b : b + 1], 0, inner // HEAD_DIM) * total
        whole = whole * keep[b : b + 1]
    pay[:STATE] = total.astype(BF)
    index = lax.broadcasted_iota(jnp.int32, (HALO, inner), 0)
    wide_keep = expand(whole, 0, inner // HEAD_DIM)
    hi = wide_keep.astype(BF).astype(F32)
    pay[STATE:] = jnp.where(index == 0, hi, jnp.where(index == 1, wide_keep - hi, 0.0)).astype(BF)


def gate_grad_kernel(place, normed, cot, out_low, ggate, tok, *refs):
    (mixed, gn), refs = refs[-9:-7], refs[:-9] + refs[-7:]
    weights, (out_a, out_b, gwg, gwo, wg, wo, sems) = refs[:-7], refs[-7:]
    load_weights(place, weights, (wg, wo), sems)
    inner = out_low.shape[1]
    low = normed[HALO:, :]
    for tile in range(inner // TILE):
        lanes = slice(tile * TILE, (tile + 1) * TILE)
        gwo[:, lanes] = dot_tn(cot[...], out_low[:, lanes]).astype(BF)
        gwg[:, lanes] = dot_tn(low, ggate[:, lanes]).astype(BF)
    wait_weights((wg, wo), sems)
    gn[...] = dot_nt(ggate[...], wg[...])
    mixed[...] = (tok[HALO:, :].astype(F32) + dot_nt(out_low[...], wo[...])).astype(BF)
    store_grads(place, (gwg, gwo), (out_a, out_b), sems)


def scan_grad_kernel(b, place, gscan, conv, st, rw, seg_col, seg_row, z, colside, gentry, gread, smask, acc, cum_t):
    inner = conv.shape[1]
    half = BLOCK // 2
    j, i = lower_matrix()
    lane = lax.broadcasted_iota(jnp.int32, (BLOCK, LANES), 1)
    rows = slice(b * BLOCK, (b + 1) * BLOCK)
    same = (i >= j) & (seg_col[rows, 0:1] == seg_row[0:1, rows])
    scores = dot_nt(rw[rows, :STATE], rw[rows, STATE:])
    smask[...] = jnp.where(same, scores, 0.0)
    cum_t[...] = st[2, rows].T
    acc[...] = jnp.zeros_like(acc)
    colside[...] = jnp.zeros((BLOCK, LANES), F32)

    def pair(p, carry):
        cum = pltpu.roll(st[2, rows], lax.rem(LANES - 2 * p, LANES), 1)
        step = pltpu.roll(st[1, rows], lax.rem(LANES - 2 * p, LANES), 1)
        lanes = pl.ds(pl.multiple_of(p * LANES, LANES), LANES)
        c = conv[rows, lanes].astype(F32)
        act = (c * sigmoid(c)).astype(BF).astype(F32)
        xs = (act * jnp.where(lane < HEAD_DIM, step[:, 0:1], step[:, 1:2])).astype(BF)
        gs = gscan[rows, lanes]
        gs_t = gs.T
        top = jnp.zeros((half, LANES), F32)
        bottom = jnp.zeros((half, LANES), F32)
        for a in range(2):
            keep = (lane < HEAD_DIM) == (a == 0)
            mine = jnp.where(keep, xs, jnp.zeros_like(xs))
            grad = jnp.where(keep, gs, jnp.zeros_like(gs))
            row = cum_t[pl.ds(2 * p + a, 1), :]
            e = jnp.exp(jnp.minimum(row - cum[:half, a : a + 1], 0.0))
            top = top + dot((smask[:half, :] * e).astype(BF), grad)
            acc[:half, :] += dot(mine[:half], gs_t) * e
            e = jnp.exp(jnp.minimum(row[:, half:] - cum[half:, a : a + 1], 0.0))
            bottom = bottom + dot((smask[half:, half:] * e).astype(BF), grad[half:])
            acc[half:, half:] += dot(mine[half:], gs_t[:, half:]) * e
        both = jnp.concatenate([top, bottom], axis=0)
        z[:, lanes] = both
        channel = lax.broadcasted_iota(jnp.int32, (LANES, LANES), 0)
        head = lax.broadcasted_iota(jnp.int32, (LANES, LANES), 1)
        matrix = (channel // HEAD_DIM + 2 * p == head).astype(BF)
        colside[...] += head_sum(both * xs.astype(F32), matrix)
        return carry

    lax.fori_loop(0, inner // LANES, pair, 0, unroll=12)
    low = jnp.where(same, acc[...], 0.0).astype(BF)
    gentry[...] = dot(low, rw[rows, STATE:])
    gread[...] = dot_tn(low, rw[rows, :STATE])


def input_grad_kernel(
    place, near, far, d_ref, keep, states, conv, pre, gscan, st, rw, sconv, spre, rowside, gread_a, taps,
    taps_state, par, wide, cols, *refs
):
    by_block, (low_inner, low_state, low_step, sums, sums_state, sums_head, gstates) = refs[:-7], refs[-7:]
    z, colside, gentry, gread_b = [
        jnp.concatenate([ref[...] for ref in by_block[n::4]], axis=0) if n else by_block[n::4] for n in range(4)
    ]
    tokens, inner = conv.shape
    blocks = tokens // BLOCK
    tiles = inner // TILE
    heads = TILE // HEAD_DIM
    col = cols[...]
    now = entering(near, far)
    keep_grads = [None] * blocks
    whole_matrix = head_matrix(0, inner)
    for b in range(blocks - 1, -1, -1):
        gstates[b] = now.astype(BF)
        sum_row = jnp.sum(now * states[b].astype(F32), axis=0, keepdims=True)
        keep_grads[b] = head_sum(jnp.broadcast_to(sum_row, (8, inner)), whole_matrix)[0:1]
        if b > 0:
            now = d_ref[b - 1] + expand(keep[b : b + 1], 0, inner // HEAD_DIM) * now
    step_grad = jnp.zeros((tokens, LANES), F32)
    out_side = jnp.zeros((tokens, LANES), F32)
    entry_grad = gentry
    for tile in range(tiles):
        lanes = slice(tile * TILE, (tile + 1) * TILE)
        first = tile * heads
        matrix = head_matrix(first, TILE)
        c = conv[:, lanes].astype(F32)
        sg = sigmoid(c)
        act = (c * sg).astype(BF).astype(F32)
        step = expand(st[1], first, heads)
        out = expand(st[3], first, heads)
        scaled = (act * (step * out)).astype(BF)
        grads = []
        entries = []
        for b in range(blocks):
            rows = slice(b * BLOCK, (b + 1) * BLOCK)
            grads.append(dot(rw[rows, :STATE], gstates[b, :, lanes]))
            entries.append(dot_nt(scaled[rows], gstates[b, :, lanes]))
        grad_scaled = jnp.concatenate(grads, axis=0)
        entry_grad = entry_grad + jnp.concatenate(entries, axis=0)
        w = jnp.concatenate([ref[:, lanes] for ref in z], axis=0) + out * grad_scaled
        step_grad = step_grad + head_sum(act * w, matrix)
        out_side = out_side + head_sum(scaled.astype(F32) * grad_scaled, matrix)
        grad = wide[1:2, lanes] * gscan[:, lanes].astype(F32) + step * w
        grad = grad * (sg * (1.0 + c * (1.0 - sg)))
        back, rows_sum = conv_backward(grad, pre[:, lanes].astype(F32), taps[:, lanes], col)
        low = back.astype(BF)
        low_inner[:, lanes] = low
        sums[:, lanes] = put_rows(rows_sum, TILE)
    sc = sconv[...]
    sg = sigmoid(sc)
    grad = jnp.concatenate([entry_grad, gread_a[...] + gread_b], axis=1)
    grad = grad * (sg * (1.0 + sc * (1.0 - sg)))
    back, rows_sum = conv_backward(grad, spre[...], taps_state, col)
    low = back.astype(BF)
    low_state[...] = low
    sums_state[...] = put_rows(rows_sum, 2 * STATE)
    i, j = lower_matrix()
    upper = (i <= j).astype(F32)
    at_end = lax.broadcasted_iota(jnp.int32, (BLOCK, LANES), 0) == BLOCK - 1
    decays = []
    for b in range(blocks):
        rows = slice(b * BLOCK, (b + 1) * BLOCK)
        side = out_side[rows]
        last = jnp.sum(side, axis=0, keepdims=True) + keep_grads[b] * keep[b : b + 1]
        cum_grad = rowside[rows, :] - colside[rows] - side + jnp.where(at_end, last, 0.0)
        decays.append(dot_high(upper, cum_grad))
    decay_grad = jnp.concatenate(decays, axis=0)
    rate = par[1:2]
    step_grad = (step_grad + decay_grad * rate) * sigmoid(st[0])
    rows_head = [
        jnp.sum(step_grad, axis=0, keepdims=True),
        jnp.sum(decay_grad * st[1] * rate, axis=0, keepdims=True),
    ]
    sums_head[...] = put_rows(rows_head, LANES)
    low = jnp.concatenate([jnp.zeros((HALO, LANES), F32), step_grad], axis=0).astype(BF)
    low_step[...] = low


def weight_grad_kernel(place, normed, low_inner, low_state, low_step, gwi, gws, gwp):
    x = normed[...]
    for tile in range(low_inner.shape[1] // SPAN):
        lanes = slice(tile * SPAN, (tile + 1) * SPAN)
        gwi[:, lanes] = dot_tn(x, low_inner[:, lanes]).astype(BF)
    gws[...] = dot_tn(x, low_state[...]).astype(BF)
    gwp[...] = dot_tn(x, low_step[...]).astype(BF)


def weight_store_kernel(place, gwi, gws, gwp, *refs):
    store_grads(place, (gwi, gws, gwp), refs[:-1], refs[-1])


def token_grad_kernel(
    place, low_inner, low_state, low_step, gn_gate, tok, cot, gain, sums_in, sums_out, sums_state, sums_head, *refs
):
    weights, (grad, back, pack, win, wst, wsp, sems) = refs[:-7], refs[-7:]
    load_weights(place, weights, (win, wst, wsp), sems)
    wait_weights((win, wst, wsp), sems)
    width = tok.shape[1]
    gn = dot_nt(low_inner[...], win[...]) + dot_nt(low_state[...], wst[...])
    gn = gn + dot_nt(low_step[...], wsp[...])
    gn = gn + jnp.concatenate([jnp.zeros((HALO, width), F32), gn_gate[...]], axis=0)
    t = tok[...].astype(F32)
    r = lax.rsqrt(jnp.mean(t * t, axis=1, keepdims=True) + EPS)
    scaled = t * r
    inner = pack.shape[1]
    pack[0 : KW + 1, :] = sums_in[: KW + 1]
    pack[KW + 1 : KW + 2, :] = sums_out[0:1]
    pack[KW + 2 :, :] = jnp.zeros((8 - KW - 2, inner), F32)
    pack[KW + 2 : KW + 3, :width] = jnp.sum(gn * scaled, axis=0, keepdims=True)
    pack[KW + 2 : KW + 3, width : width + LANES] = sums_head[0:1]
    pack[KW + 2 : KW + 3, width + LANES : width + 2 * LANES] = sums_head[1:2]
    skips = head_sum(sums_out[...], head_matrix(0, inner))
    pack[KW + 2 : KW + 3, width + 2 * LANES : width + 3 * LANES] = skips[1:2]
    for k in range(KW + 1):
        pack[KW + 3 : KW + 4, 2 * STATE * k : 2 * STATE * (k + 1)] = sums_state[k : k + 1]
    gg = gn * gain[0:1]
    result = gg * r - t * (r * r * r * jnp.mean(gg * t, axis=1, keepdims=True))
    back[...] = result[:HALO]
    grad[...] = result[HALO:] + cot[...].astype(F32)


def finish_kernel(place, a, b, c, d, inner, state, step, conv, conv_state, norm, gain, *heads):
    depth, span = inner.shape
    per = span // HEAD_DIM

    def total(first, count):
        rows = slice(first, first + count)
        return a[rows].astype(F32) + b[rows].astype(F32) + c[rows].astype(F32) + d[rows].astype(F32)

    inner[...] = total(0, depth)
    last = total(depth, depth)
    state[...] = last[:, : 2 * STATE]
    turn_heads = lax.rem(LANES - place[1] * per, LANES)
    step[...] = pltpu.roll(last[:, 2 * STATE :], turn_heads, 1)[:, :per]
    small = total(2 * depth, 2 * 8)
    conv[...] = small[: KW + 1]
    gain[...] = small[KW + 1]
    whole = [
        jnp.concatenate([small[8 + 2 * q + n : 9 + 2 * q + n] for q in range(4)], axis=1) for n in range(2)
    ]
    width = norm.shape[0]
    norm[...] = whole[0][0, :width]
    rows = [whole[1][:, 2 * STATE * k : 2 * STATE * (k + 1)] for k in range(KW + 1)]
    conv_state[...] = put_rows(rows, 2 * STATE)[: KW + 1]
    rows = [whole[0][:, width + LANES * n : width + LANES * (n + 1)] for n in range(3)]
    rows = pltpu.roll(put_rows(rows, LANES), turn_heads, 1)
    for n, head in enumerate(heads):
        head[...] = rows[n, :per]


def line(shift, size):
    return [(i, i + shift) for i in range(size) if 0 <= i + shift < size]


def pass_first(payload, size, sign):
    return lax.ppermute(payload, "tensor", line(sign, size))


def pass_states(payload, came, size, sign, first=()):
    own = payload[:STATE].astype(F32)
    factor = payload[STATE].astype(F32) + payload[STATE + 1].astype(F32)
    near, far, send = came, jnp.zeros_like(came[:STATE]), came
    reach = 2
    while reach < size:
        near_factor = near[STATE].astype(F32) + near[STATE + 1].astype(F32)
        total = near[:STATE].astype(F32)
        if reach > 2:
            total = total + last_factor[None] * far[:STATE].astype(F32)
        send = (own + factor[None] * total).astype(BF)
        if 2 * reach < size:
            both = factor * near_factor
            hi = both.astype(BF)
            lo = (both - hi.astype(F32)).astype(BF)
            send = jnp.concatenate([send, hi[None], lo[None]], axis=0)
        send = after(send, *first)
        far = lax.ppermute(send, "tensor", line(sign * reach, size))
        last_factor = near_factor
        if 2 * reach < size:
            total = near[:STATE].astype(F32) + near_factor[None] * far[:STATE].astype(F32)
            both = near_factor * (far[STATE].astype(F32) + far[STATE + 1].astype(F32))
            hi = both.astype(BF)
            lo = (both - hi.astype(F32)).astype(BF)
            near = jnp.concatenate([total.astype(BF), hi[None], lo[None]], axis=0)
            near = jnp.pad(near, ((0, HALO - 2), (0, 0)))
            far = jnp.zeros_like(far)
        reach = 2 * reach
    return near, far[:STATE], send


def entering(near, far):
    rows = near[STATE:, :].astype(F32)
    return near[:STATE, :].astype(F32) + (rows[0:1] + rows[1:2]) * far[...].astype(F32)


def swap(values, mask):
    return lax.ppermute(values, "dp", [(i, i ^ mask) for i in range(8)])


def turn(values, shift):
    return lax.ppermute(values, "tensor", [(i, (i + shift) % 4) for i in range(4)])


def cross(values, mask):
    return lax.ppermute(values, "tensor", [(i, i ^ mask) for i in range(4)])


def ring(values):
    return [values] + [turn(values, -m) for m in range(1, 4)]


def gather_plane(column):
    return [column] + [swap(column, k) for k in ORDER[1:4]]


def gather_cores(same, first=()):
    return same + [swap(after(v, *first), 1) for v in same]


def sum_pair_kernel(place, mine, came, *outs):
    for n, out in enumerate(outs):
        out[...] = mine[n] + came[n]


def sum_pair_pack_kernel(place, mine, came, pack, came_pack, *outs):
    slots, depth, span = mine.shape[1:]
    total = pack[...] + came_pack[...]
    rows = jnp.concatenate([total[:, q * span : (q + 1) * span] for q in range(4)], axis=0).astype(BF)
    for n, out in enumerate(outs):
        for m in range(slots):
            out[m * depth : (m + 1) * depth, :] = mine[n, m] + came[n, m]
        out[slots * depth :, :] = rows


def sum_column_pack_kernel(place, a, b, c, d, *refs):
    outs, rows = refs[:4], refs[4]
    depth = (a.shape[0] - 32) // 5

    def total(first, count):
        part = slice(first, first + count)
        return a[part].astype(F32) + b[part].astype(F32) + c[part].astype(F32) + d[part].astype(F32)

    rows[...] = total(5 * depth, 32)
    last = total(4 * depth, depth).astype(BF)
    rest = jnp.concatenate([rows[8 * q + KW + 2 : 8 * q + KW + 4] for q in range(4)], axis=0)
    for m, out in enumerate(outs):
        out[:depth, :] = total(m * depth, depth).astype(BF)
        out[depth : 2 * depth, :] = last
        own = rows[pl.ds(aligned((place[1] + m) % 4, 8), 8), :]
        out[2 * depth :, :] = jnp.concatenate([own, rest], axis=0).astype(BF)


def sum_column_kernel(place, a, b, c, d, *outs):
    for m, out in enumerate(outs):
        total = a[m].astype(F32) + b[m].astype(F32) + c[m].astype(F32) + d[m].astype(F32)
        out[...] = total.astype(BF)


def sum_last_kernel(place, a, b, c, d, first, second):
    for n, out in enumerate((first, second)):
        out[...] = a[n].astype(F32) + b[n].astype(F32) + c[n].astype(F32) + d[n].astype(F32)


def reduce_core(where, mine, other):
    came = swap(other, 1)
    return call(sum_pair_kernel, [sds(mine.shape[1:], BF)] * 4, (where, mine, came), name="sum_pair")


def reduce_plane(where, parts):
    came = [swap(parts[n], ORDER[n]) for n in range(1, 4)]
    shape = (2, *parts[0].shape[-2:])
    return call(sum_column_kernel, [sds(shape, BF)] * 4, (where, parts[0], *came), name="sum_column")


def reduce_line(where, parts):
    came = [turn(parts[m], m) for m in range(1, 4)]
    return call(
        sum_last_kernel, [sds(parts[0].shape[1:], F32)] * 2, (where, parts[0], *came), name="sum_last"
    )


def after_all(values, *others):
    return lax.optimization_barrier((*values, *others))[: len(values)]


def after(value, *others):
    return lax.optimization_barrier((value, *others))[0]


def gather(shard):
    return lax.all_gather(
        lax.all_gather(shard, "tensor", axis=1, tiled=True), "dp", axis=0, tiled=True
    )


def scatter(grad):
    part = lax.psum_scatter(grad, "dp", scatter_dimension=0, tiled=True)
    return lax.psum_scatter(part, "tensor", scatter_dimension=1, tiled=True).astype(F32)


def make_shards(mesh):
    size = mesh.shape["tensor"]
    blocked = size == 4 and mesh.shape["dp"] == 8

    def shards(
        tokens, segments, cotangent, norm_gain, w_gate, w_inner, w_step, w_state, conv_inner, conv_state,
        step_bias, decay_log, skip_gain, out_gain, w_out,
    ):
        count, width = tokens.shape
        place = lax.axis_index("tensor")
        blocks = count // BLOCK
        inner = w_inner.shape[1] * size
        heads = w_step.shape[1] * size

        halo = lax.ppermute(tokens[count - HALO :], "tensor", line(1, size))
        tok = jnp.concatenate([halo, tokens], axis=0)
        wide_tok = tok.astype(F32)
        gain = norm_gain.astype(F32)
        rms = lax.rsqrt(jnp.mean(wide_tok * wide_tok, axis=1, keepdims=True) + EPS)
        normed = (wide_tok * rms * gain).astype(BF)

        padded = jnp.concatenate([jnp.full((HALO,), -1, jnp.int32), segments])
        near = lax.dynamic_slice(padded, (place * count,), (HALO + count,))
        seg = near[HALO:]
        masks = [near[HALO - k : HALO - k + count] == seg for k in range(1, KW)]
        grid = seg.reshape(blocks, BLOCK)
        prev = near[HALO - 1 : HALO - 1 + count].reshape(blocks, BLOCK)[:, :1]
        from_prev = (grid == prev).reshape(-1)
        at_last = (grid == grid[:, BLOCK - 1 :]).reshape(-1)
        cols = jnp.stack([*masks, from_prev, at_last], axis=1).astype(F32)
        seg_col = seg.astype(F32)[:, None]
        seg_row = seg.astype(F32)[None]

        def pad_heads(row):
            return jnp.pad(row, ((0, 0), (0, LANES - heads)))

        where = jnp.stack([lax.axis_index("dp"), place]).astype(jnp.int32)
        depth, span = w_inner.shape
        per = heads // size
        if blocked:
            tall = HALO + depth

            def place_at(block, row, lane):
                rows = (row, tall - row - block.shape[0])
                return jnp.pad(block, (rows, (lane, span - lane - block.shape[1])))

            pack = place_at(w_inner, 0, 0) + place_at(w_step.T, depth + KW + 3, 0)
            pack = pack + place_at(conv_inner, depth, 0) + place_at(out_gain[None], depth + KW + 1, 0)
            for n, row in enumerate((step_bias, decay_log, skip_gain)):
                pack = pack + place_at(row[None], depth + KW + 2, n * per)
            came = ring(pack)
            pair_out = jnp.stack([w_gate, w_out])[None]
            pair_out = jnp.concatenate([pair_out, cross(pair_out, 1)])
            came_out = jnp.concatenate([pair_out, cross(pair_out, 2)])

            column, taps, par, wide = call(
                unpack_kernel,
                [
                    sds((5, depth, span), BF),
                    sds((8, inner), F32),
                    sds((8, LANES), F32),
                    sds((8, inner), F32),
                ],
                (where, *came, w_state),
                name="unpack",
            )
            same = gather_plane(column)
            pieces = gather_cores(same, (came_out,))
            same_out = gather_plane(after(came_out, *same[1:]))
        else:
            conv_whole, head_whole, gain_whole = [
                lax.all_gather(v, "tensor", axis=v.ndim - 1, tiled=True).astype(F32)
                for v in (conv_inner, jnp.stack([step_bias, decay_log, skip_gain]), out_gain)
            ]
            pieces = [gather(w_inner), lax.all_gather(w_state, "dp", axis=0, tiled=True), pad_heads(gather(w_step))]
            pieces_out = [gather(w_gate), gather(w_out)]
            taps = jnp.pad(conv_whole, ((0, 8 - KW - 1), (0, 0)))
            bias, rate, skip = head_whole[0], -jnp.exp(head_whole[1]), head_whole[2]
            par = pad_heads(jnp.pad(jnp.stack([bias, rate]), ((0, 6), (0, 0))))
            wide = jnp.pad(jnp.stack([gain_whole, jnp.repeat(skip, HEAD_DIM)]), ((0, 6), (0, 0)))
        taps_state = jnp.pad(conv_state.astype(F32), ((0, 8 - KW - 1), (0, 0)))
        in_scratch = [
            pltpu.VMEM((width, inner), BF),
            pltpu.VMEM((width, 2 * STATE), BF),
            pltpu.VMEM((width, LANES), BF),
            pltpu.SemaphoreType.DMA((3,)),
        ]
        out_scratch = [
            pltpu.VMEM((width, inner), BF),
            pltpu.VMEM((width, inner), BF),
            pltpu.SemaphoreType.DMA((2,)),
        ]

        def last_args(fixed, arrays):
            return {"args": (where, *fixed, *arrays), "far": range(1 + len(fixed), 1 + len(fixed) + len(arrays))}

        pre, conv, spre, sconv, rw, st, keep, c_ref, *pays = call(
            project_kernel,
            [
                sds((HALO + count, inner), BF),
                sds((count, inner), F32),
                sds((HALO + count, 2 * STATE), F32),
                sds((count, 2 * STATE), F32),
                sds((count, 2 * STATE), BF),
                sds((5, count, LANES), F32),
                sds((8, LANES), F32),
                sds((max(1, blocks - 1), STATE, inner), F32),
                *[sds((STATE + HALO, inner // HALVES), BF)] * HALVES,
            ],
            scratch=in_scratch,
            **last_args((normed, taps, taps_state, par, cols), pieces),
            name="project",
            micros=9.5,
        )
        came_pays = [pass_first(pay, size, 1) for pay in pays]
        enter = []
        y = []
        for b in range(blocks):
            y += call(
                functools.partial(scan_kernel, b),
                [sds((BLOCK, inner), F32)],
                (where, conv if b == 0 else after(conv, enter[-1][2], *came_pays), st, rw, seg_col, seg_row),
                [pltpu.VMEM((BLOCK, BLOCK), F32), pltpu.VMEM((LANES, BLOCK), F32)],
                name=f"scan_{b}",
                micros=5,
            )
            if b < HALVES:
                enter.append(pass_states(pays[b], came_pays[b], size, 1, (y[-1],)))
        for part in range(len(enter), HALVES):
            enter.append(pass_states(pays[part], came_pays[part], size, 1))
        near, far, sent = [list(v) for v in zip(*enter)]
        if blocked:
            pieces_out = gather_cores(same_out, (far[0], sent[-1]))
        gate, gout = call(
            gate_kernel,
            [sds((count, inner), F32)] * 2,
            scratch=out_scratch,
            **last_args((after(normed, sent[-1]), cotangent), pieces_out),
            name="gate",
            micros=4,
        )
        out_low, ggate, gscan, rowside, gread_a, states, d_ref, pay, sums = call(
            output_kernel,
            [
                sds((count, inner), BF),
                sds((count, inner), BF),
                sds((count, inner), BF),
                sds((count, LANES), F32),
                sds((count, STATE), F32),
                sds((blocks, STATE, inner), BF),
                sds((max(1, blocks - 1), STATE, inner), F32),
                sds((STATE + HALO, inner), BF),
                sds((8, inner), F32),
            ],
            (where, c_ref, keep, gate, gout, conv, rw, st, wide, *near, *far, *y),
            [pltpu.VMEM((ROWS, inner), F32), pltpu.VMEM((blocks, STATE, inner), F32)],
            name="output",
            micros=9.5,
        )
        if blocked:
            shapes_out = [sds((4, 4, 2, depth, span), BF)] * 2
            shapes_in = [sds((4, 5, depth, span), BF)] * 2
        else:
            shapes_out = [sds((width, inner), BF)] * 2
            shapes_in = [sds((width, inner), BF), sds((width, 2 * STATE), BF), sds((width, LANES), BF)]
        mixed, gn_gate, *grads_out = call(
            gate_grad_kernel,
            [sds((count, width), BF), sds((count, width), F32), *shapes_out],
            far_outs=(2, 3),
            scratch=[
                pltpu.VMEM((width, inner), BF),
                pltpu.VMEM((width, inner), BF),
                *out_scratch,
            ],
            **last_args((normed, cotangent, out_low, ggate, tok), pieces_out),
            name="gate_grad",
            micros=8.3,
        )
        came_pay = pass_first(pay, size, -1)
        if blocked:
            mine_out, other_out = grads_out
            parts_out = reduce_core(where, mine_out, after(other_out, came_pay))
        else:
            parts_out = ()
        *leave, sent = pass_states(pay, came_pay, size, -1)
        by_block = [
            call(
                functools.partial(scan_grad_kernel, b),
                [sds((BLOCK, inner), F32), sds((BLOCK, LANES), F32), *[sds((BLOCK, STATE), F32)] * 2],
                (where, after(gscan, sent, *parts_out), conv, st, rw, seg_col, seg_row),
                [
                    pltpu.VMEM((BLOCK, BLOCK), F32),
                    pltpu.VMEM((BLOCK, BLOCK), F32),
                    pltpu.VMEM((LANES, BLOCK), F32),
                ],
                name=f"scan_grad_{b}",
                micros=9,
            )
            for b in range(blocks)
        ]
        low_inner, low_state, low_step, sums_in, sums_state, sums_head = call(
            input_grad_kernel,
            [
                sds((HALO + count, inner), BF),
                sds((HALO + count, 2 * STATE), BF),
                sds((HALO + count, LANES), BF),
                sds((8, inner), F32),
                sds((8, 2 * STATE), F32),
                sds((8, LANES), F32),
            ],
            (
                where, *leave, d_ref, keep, states, conv, pre, gscan, st, rw, sconv, spre, rowside, gread_a, taps,
                taps_state, par, wide, cols, *[v for part in by_block for v in part],
            ),
            [pltpu.VMEM((blocks, STATE, inner), BF)],
            name="input_grad",
            micros=9,
        )
        weight_grads = call(
            weight_grad_kernel,
            [sds((width, inner), BF), sds((width, 2 * STATE), BF), sds((width, LANES), BF)],
            (where, normed, low_inner, low_state, low_step),
            name="weight_grad",
            micros=4,
        )
        if blocked:
            lines_out = reduce_plane(where, parts_out)
            weight_grads = after_all(weight_grads, *lines_out)
        grads_in = call(
            weight_store_kernel,
            shapes_in,
            (where, *weight_grads),
            scratch=in_scratch[-1:],
            far_outs=range(len(shapes_in)),
            name="weight_store",
            micros=1,
        )
        if blocked:
            mine_in, other_in = grads_in
            came_in = swap(other_in, 1)
            low_inner = after(low_inner, other_in)
        grad, back, pack = call(
            token_grad_kernel,
            [sds((count, width), F32), sds((HALO, width), F32), sds((8, inner), F32)],
            scratch=in_scratch,
            **last_args((low_inner, low_state, low_step, gn_gate, tok, cotangent, gain[None], sums_in, sums, sums_state, sums_head), pieces),
            name="token_grad",
            micros=5,
        )
        if blocked:
            tall = 5 * depth + 32
            parts_in = call(
                sum_pair_pack_kernel,
                [sds((tall, span), BF)] * 4,
                (where, mine_in, came_in, pack, swap(pack, 1)),
                name="sum_pair_pack",
            )
            back = lax.ppermute(after(back, *parts_in), "tensor", line(-1, size))
            lines_out = after_all(lines_out, *parts_in)
            grad_gate, grad_out = reduce_line(where, lines_out)
        if blocked:
            came_in = [swap(parts_in[n], ORDER[n]) for n in range(1, 4)]
            lines_in = call(
                sum_column_pack_kernel,
                [sds((2 * depth + 2 * 8, span), BF)] * 4,
                (where, after(parts_in[0], back), *came_in),
                [pltpu.VMEM((32, span), F32)],
                name="sum_column_pack",
            )
            grad_inner, grad_state, grad_step, grad_conv, grad_conv_state, norm, grad_gain, *head_grads = call(
                finish_kernel,
                [
                    sds((depth, span), F32),
                    sds((depth, 2 * STATE), F32),
                    sds((depth, per), F32),
                    sds((KW + 1, span), F32),
                    sds((KW + 1, 2 * STATE), F32),
                    sds((width,), F32),
                    sds((span,), F32),
                    *[sds((per,), F32)] * 3,
                ],
                (where, lines_in[0], *[turn(lines_in[m], m) for m in range(1, 4)]),
                name="finish",
            )
        else:
            pack = lax.psum(pack, ("dp", "tensor"))
            own = lax.dynamic_slice(pack, (0, place * span), (KW + 2, span))
            norm = pack[KW + 2, :width]
            grad_conv, grad_gain = own[: KW + 1], own[KW + 1]
            grad_conv_state = pack[KW + 3, : (KW + 1) * 2 * STATE].reshape(KW + 1, 2 * STATE)
            head_grads = [
                lax.dynamic_slice(pack[KW + 2], (width + LANES * n + place * per,), (per,)) for n in range(3)
            ]
            grad_gate, grad_out, grad_inner, grad_step = [
                scatter(v) for v in (*grads_out, grads_in[0], grads_in[2][:, :heads])
            ]
            grad_state = lax.psum_scatter(grads_in[1], "dp", scatter_dimension=0, tiled=True)
            grad_state = lax.psum(grad_state, "tensor").astype(F32)
        if not blocked:
            back = lax.ppermute(back, "tensor", line(-1, size))
        grad = grad.at[count - HALO :].add(back)
        return (
            mixed,
            grad,
            norm,
            grad_gate,
            grad_inner,
            grad_step,
            grad_state,
            grad_conv,
            grad_conv_state,
            *head_grads,
            grad_gain,
            grad_out,
        )

    return shards


def solution(mesh):
    in_specs = (
        P(("dp", "tensor"), None),
        P("dp"),
        P(("dp", "tensor"), None),
        P(),
        P("dp", "tensor"),
        P("dp", "tensor"),
        P("dp", "tensor"),
        P("dp", None),
        P(None, "tensor"),
        P(),
        P("tensor"),
        P("tensor"),
        P("tensor"),
        P("tensor"),
        P("dp", "tensor"),
    )
    out_specs = (
        P(("dp", "tensor"), None),
        P(("dp", "tensor"), None),
        P(),
        P("dp", "tensor"),
        P("dp", "tensor"),
        P("dp", "tensor"),
        P("dp", None),
        P(None, "tensor"),
        P(),
        P("tensor"),
        P("tensor"),
        P("tensor"),
        P("tensor"),
        P("dp", "tensor"),
    )
    return jax.shard_map(
        make_shards(mesh), mesh=mesh, in_specs=in_specs, out_specs=out_specs, check_vma=False
    )
```
